256 devices in a mesh: row: 16 (over x, y), col: 16 (over z, core).
Axes of the slice: x: 4, y: 4, z: 8, core: 2. Of those that a mesh axis runs over, the one named last changes fastest.
Arguments:
- features: bfloat16 [32768, 512], P('col', 'row'), may hold values from -6 to 6
- weight: bfloat16 [512, 512], replicated, may hold values from -0.25 to 0.25
- block_cols: int32 [256, 16, 8], P('row', 'col'), may hold values from 0 to 15
- block_count: int32 [256, 16], P('row', 'col'), may hold values from 1 to 8
- edge_src: int32 [256, 16, 8, 512], P('row', 'col'), may hold values from 0 to 127
- edge_dst: int32 [256, 16, 8, 512], P('row', 'col'), may hold values from 0 to 127
- edge_weight: bfloat16 [256, 16, 8, 512], P('row', 'col'), may hold values from 0.099609375 to 0.5
- cotangent: bfloat16 [32768, 512], P('row', 'col'), may hold values from -6 to 6
Outputs:
- activated: bfloat16 [32768, 512], P('row', 'col')
- feature_grad: bfloat16 [32768, 512], P('col', 'row')
- weight_grad: float32 [512, 512], replicated
The draws below stay inside these ranges and needn't reach their ends.
Inputs may be any that keep to these rules, and one draw needn't show every extreme that they name: `block_cols`: column blocks are numbered within their column group; the same block may appear in several slots.
All inputs are finite; a program needn't handle non-finite values.
Results may differ from the reference program's by a relative error of at most 0.0069.
Values may be sent and summed in bfloat16 or wider, within the bound.
A program may use at most 192 MiB of HBM per device.

```python
import jax
import jax.numpy as jnp
from jax import lax

F = 512
KMAX = 8
EDGES = 512
BLK = 1
NB = 256
NODES = 32768
N_ROW = 16
N_COL = 16


def draw_block_count(key, part):
    key = jax.random.fold_in(key, 7)
    level_key, count_key, spot_key = jax.random.split(key, 3)
    levels = jax.random.randint(level_key, (N_ROW, N_COL), 1, KMAX + 1)
    levels = jnp.repeat(levels, NB // N_ROW, axis=0)
    raw = jax.random.randint(count_key, (NB, N_COL), 0, 1 << 20)
    counts = 1 + raw % levels
    spot = jax.random.randint(spot_key, (), 0, NB * N_COL)
    flat = jnp.arange(NB * N_COL, dtype=jnp.int32).reshape(NB, N_COL)
    return jnp.where(flat == spot, KMAX, counts).astype(jnp.int32)


def touch_ends(values, key, low, largest):
    longest = values.shape.index(max(values.shape))
    spots = []
    for shift in (0, 1):
        where = [jax.random.randint(jax.random.fold_in(key, axis), (), 0, length) for axis, length in enumerate(values.shape)]
        where[longest] = (where[longest] + shift) % values.shape[longest]
        spots.append(tuple(where))
    return values.at[spots[0]].set(low).at[spots[1]].set(largest)


def steps_of(key, extent, cuts, low, top_value):
    loudness = 1.0
    for position, blocks in cuts:
        steps = jax.random.uniform(jax.random.fold_in(jax.random.fold_in(key, 6), position), (blocks,), jnp.float32, low / len(cuts), top_value / len(cuts))
        loudness = loudness * jnp.repeat(jnp.exp(steps), extent[position] // blocks).reshape((-1,) + (1,) * (len(extent) - 1 - position))
    return loudness


def scatter_about(own_key, extent, scale, most, pieces=(), kind=jnp.bfloat16):
    factor_of = steps_of(own_key, extent, pieces, -0.22, 0.18) if pieces else 1.0
    drawn = jax.random.normal(own_key, extent, jnp.float32) * scale * factor_of
    return jnp.minimum(jnp.maximum(drawn, -most), most).astype(kind)


def setup_inputs(seed: int = 0) -> dict:
    key_of = jax.random.split(jax.random.key(seed), 9)
    return {
        "features": scatter_about(key_of[0], (NODES, F), 1.0, 6.0, ((0, 16), (1, 16))),
        "weight": scatter_about(key_of[1], (F, F), F ** -0.5, 0.25),
        "block_cols": touch_ends(jax.random.randint(key_of[2], (NB, N_COL, KMAX), 0, BLK * N_ROW), jax.random.fold_in(key_of[2], 1), 0, (BLK * N_ROW) - 1).astype(jnp.int32),
        "block_count": draw_block_count(jax.random.fold_in(key_of[8], 71), 0),
        "edge_src": touch_ends(jax.random.randint(key_of[4], (NB, N_COL, KMAX, EDGES), 0, 128), jax.random.fold_in(key_of[4], 1), 0, 127).astype(jnp.int32),
        "edge_dst": touch_ends(jax.random.randint(key_of[5], (NB, N_COL, KMAX, EDGES), 0, 128), jax.random.fold_in(key_of[5], 1), 0, 127).astype(jnp.int32),
        "edge_weight": jnp.clip(0.099609375 + 0.40039062 * jax.random.uniform(key_of[6], (NB, N_COL, KMAX, EDGES), jnp.float32) ** steps_of(key_of[6], (NB, N_COL, KMAX, EDGES), ((0, 16), (1, 16)), -0.2, 0.2), 0.099609375, 0.5).astype(jnp.bfloat16),
        "cotangent": scatter_about(key_of[7], (NODES, F), 1.0, 6.0, ((0, 16), (1, 16))),
    }


def build_tile(src, dst, wts):
    tile = jnp.zeros((128, 128), jnp.float32).at[dst, src].add(wts)
    return tile.astype(jnp.bfloat16)


def reference(features, weight, block_cols, block_count, edge_src, edge_dst, edge_weight, cotangent):
    nblocks = block_cols.shape[0]
    ncol = block_cols.shape[1]
    kmax = block_cols.shape[2]
    width = weight.shape[1]
    cbl = nblocks // ncol
    projected = jnp.dot(features, weight, preferred_element_type=jnp.float32).astype(jnp.bfloat16)
    proj_blocks = projected.reshape(nblocks, 128, width)
    slots = jnp.arange(kmax, dtype=jnp.int32)
    group_base = (jnp.arange(ncol, dtype=jnp.int32) * cbl)[:, None]

    def tiles_of(g):
        live = (slots[None, :] < block_count[g][:, None]).astype(jnp.float32)
        wts = edge_weight[g].astype(jnp.float32) * live[:, :, None]
        tiles = jax.vmap(jax.vmap(build_tile))(edge_src[g], edge_dst[g], wts)
        index = (group_base + block_cols[g]).astype(jnp.int32)
        return tiles, index

    def forward_block(g):
        tiles, index = tiles_of(g)
        picked = proj_blocks[index]
        return jnp.einsum('ckab,ckbf->af', tiles.astype(jnp.float32), picked.astype(jnp.float32))

    hidden = lax.map(forward_block, jnp.arange(nblocks, dtype=jnp.int32)).reshape(nblocks * 128, width)
    sig = jax.nn.sigmoid(hidden)
    activated = (hidden * sig).astype(jnp.bfloat16)
    slope = (cotangent.astype(jnp.float32) * sig * (1.0 + hidden * (1.0 - sig))).astype(jnp.bfloat16)
    slope_blocks = slope.reshape(nblocks, 128, width)

    def backward_block(total, g):
        tiles, index = tiles_of(g)
        parts = jnp.einsum('ckab,af->ckbf', tiles.astype(jnp.float32), slope_blocks[g].astype(jnp.float32))
        return total.at[index.reshape(-1)].add(parts.reshape(-1, 128, width)), None

    total, _ = lax.scan(backward_block, jnp.zeros((nblocks, 128, width), jnp.float32), jnp.arange(nblocks, dtype=jnp.int32))
    back = total.reshape(nblocks * 128, width).astype(jnp.bfloat16)
    weight_grad = lax.dot_general(features, back, (((0,), (0,)), ((), ())), preferred_element_type=jnp.float32)
    feature_grad = lax.dot_general(back, weight, (((1,), (1,)), ((), ())), preferred_element_type=jnp.float32).astype(jnp.bfloat16)
    return activated, feature_grad, weight_grad
```

```python
import jax
import jax.numpy as jnp
from jax import lax
from jax.experimental import pallas as pl
from jax.experimental.pallas import tpu as pltpu
from jax.sharding import PartitionSpec as P

MESH = pl.DeviceIdType.MESH
BF = jnp.bfloat16
F32 = jnp.float32
NT = (((1,), (1,)), ((), ()))
TN = (((0,), (0,)), ((), ()))
NS = 2
SUB = 512 // NS


def build_kernel(cols_ref, counts_ref, src_ref, dst_ref, w_ref, out_ref):
    g = pl.program_id(0)
    out_ref[...] = jnp.zeros_like(out_ref)
    spots = lax.broadcasted_iota(jnp.int32, (128, 512), 0).astype(F32).astype(BF)
    src = src_ref[0].astype(F32)
    dst = dst_ref[0].astype(F32)
    wts = w_ref[0].astype(F32)
    one = jnp.ones((128, 512), BF)
    zero = jnp.zeros((128, 512), BF)

    def spread(row):
        piece = jnp.broadcast_to(row, (16, 512)).astype(BF)
        return jnp.concatenate([piece] * 8, axis=0)

    for k in range(8):

        @pl.when(k < counts_ref[g])
        def _():
            left = jnp.where(spots == spread(dst[k : k + 1]), spread(wts[k : k + 1]), zero)
            right = jnp.where(spots == spread(src[k : k + 1]), one, zero)
            tile = lax.dot_general(left, right, NT, preferred_element_type=F32).astype(BF)
            where = pl.ds(pl.multiple_of(cols_ref[g, k] * 128, 128), 128)
            out_ref[:, where] = out_ref[:, where] + tile


def build(cols, counts, src, dst, wts):
    return pl.pallas_call(
        build_kernel,
        out_shape=jax.ShapeDtypeStruct((2048, 2048), BF),
        grid_spec=pltpu.PrefetchScalarGridSpec(
            num_scalar_prefetch=2,
            grid=(16,),
            in_specs=[pl.BlockSpec((1, 8, 512), lambda g, *_: (g, 0, 0))] * 3,
            out_specs=pl.BlockSpec((128, 2048), lambda g, *_: (g, 0)),
        ),
        name="build",
    )(cols, counts, src, dst, wts)


def layer_kernel(
    xt_ref, cot_ref, w_ref, a_hbm,
    act_ref, fg_ref, wg_ref,
    a, xg, cotb, pown, psend, precv, zr, zs, axb, actb, slb, tg, acc,
    xs1, xr1h, xr1f, s1, xs2, xr2h, xr2f,
    wp, wr, wz,
    a_sem, loc_sem,
    cot_ss, cot_rs, ag_ss, ag_rs, core_ss, core_rs, rz_ss, rz_rs,
    act_ss, act_rs, gz_ss, gz_rs, gc_ss, gc_rs, rx_ss, rx_rs,
    w1_ss, w1_rs, w2_ss, w2_rs, w3_ss, w3_rs,
):
    r = lax.axis_index("row")
    c = lax.axis_index("col")
    x, y = r // 4, r % 4
    z, k = c // 2, c % 2

    def at_x(o):
        return ((x + o) % 4 * 4 + y, c)

    def at_y(o):
        return (x * 4 + (y + o) % 4, c)

    def at_z(o):
        return (r, (z + o) % 8 * 2 + k)

    twin = (r, z * 2 + 1 - k)

    def rc(src, dst, ss, rs, dev):
        return pltpu.make_async_remote_copy(
            src_ref=src, dst_ref=dst, send_sem=ss, recv_sem=rs, device_id=dev, device_id_type=MESH
        )

    sent = []

    def send(src, dst, ss, rs, dev):
        copy = rc(src, dst, ss, rs, dev)
        copy.start()
        sent.append(copy)

    def got(ref, ss, rs, dev):
        rc(ref, ref, ss, rs, dev).wait_recv()

    barrier = pltpu.get_barrier_semaphore()

    def greet(i, _):
        pl.semaphore_signal(barrier, inc=1, device_id=((r + i) % 16, c), device_id_type=MESH)
        pl.semaphore_signal(barrier, inc=1, device_id=(r, (c + i) % 16), device_id_type=MESH)
        return 0

    lax.fori_loop(1, 16, greet, 0)
    a_copy = pltpu.make_async_copy(a_hbm, a, a_sem)
    a_copy.start()
    for h in (0, 1):
        xg[h, x, y] = xt_ref[:, h * 1024 : (h + 1) * 1024]
    pl.semaphore_wait(barrier, 30)

    def xg_at(h, o1, o2):
        if h == 0:
            return xg.at[0, (x + o2) % 4, (y + o1) % 4]
        return xg.at[1, (x + o1) % 4, (y + o2) % 4]

    def axis(h, ring):
        return (at_y, at_x)[(h + ring) % 2]

    def ag_send(h, ring, lane, j, piece):
        dev = axis(h, ring)(1 if j % 2 == 0 else -1)
        if j == 2:
            piece = piece.at[0:16]
        if j == 3:
            piece = piece.at[16:32]
        send(piece, piece, ag_ss.at[h, lane, j], ag_rs.at[h, lane, j], dev)

    def ag_got(h, ring, lane, j, piece):
        dev = axis(h, ring)(-1 if j % 2 == 0 else 1)
        if j == 2:
            piece = piece.at[0:16]
        if j == 3:
            piece = piece.at[16:32]
        got(piece, ag_ss.at[h, lane, j], ag_rs.at[h, lane, j], dev)

    def ag_ring2_own(h, o1):
        for j in (0, 1):
            ag_send(h, 1, 1 + o1, j, xg_at(h, o1, 0))

    def ag_ring2_pass(h, o1):
        for j, o in ((0, 3), (1, 1)):
            ag_got(h, 1, 1 + o1, j, xg_at(h, o1, o))
            ag_send(h, 1, 1 + o1, 2 + j, xg_at(h, o1, o))

    for h in (0, 1):
        for j in (0, 1):
            ag_send(h, 0, 0, j, xg_at(h, 0, 0))
    for h in (0, 1):
        ag_ring2_own(h, 0)

    def cot_copy(i, peer, mine):
        return rc(
            cot_ref.at[:, pl.ds(pl.multiple_of(peer * 128, 128), 128)],
            cotb.at[pl.ds(pl.multiple_of(mine * 32, 32), 32), :],
            cot_ss.at[i], cot_rs.at[i], (r, peer),
        )

    def cot_send(i, _):
        cot_copy(i, (c + i) % 16, c).start()
        return 0

    lax.fori_loop(1, 16, cot_send, 0)
    cotb[pl.ds(pl.multiple_of(c * 32, 32), 32), :] = cot_ref[:, pl.ds(pl.multiple_of(c * 128, 128), 128)]

    for j, o in ((0, 3), (1, 1)):
        for h in (0, 1):
            ag_got(h, 0, 0, j, xg_at(h, o, 0))
            ag_send(h, 0, 0, 2 + j, xg_at(h, o, 0))
            ag_ring2_own(h, o)
    for h in (0, 1):
        ag_ring2_pass(h, 0)
    for h in (0, 1):
        for j in (2, 3):
            ag_got(h, 0, 0, j, xg_at(h, 2, 0))
        ag_ring2_own(h, 2)
    for o1 in (3, 1, 2):
        for h in (0, 1):
            ag_ring2_pass(h, o1)
    for o1 in (0, 3, 1, 2):
        for h in (0, 1):
            for j in (2, 3):
                ag_got(h, 1, 1 + o1, j, xg_at(h, o1, 2))
    a_copy.wait()

    def product(d):
        rows = pl.ds(pl.multiple_of((z + d) % 8 * 256, 256), 256)
        total = lax.dot_general(
            xg[0].reshape(512, 1024), a[rows, 0:1024], NT, preferred_element_type=F32
        ) + lax.dot_general(
            xg[1].reshape(512, 1024), a[rows, 1024:2048], NT, preferred_element_type=F32
        )
        low, high = total[:, 0:128], total[:, 128:256]
        first = k == 0
        pown[d] = jnp.where(first, low, high)
        psend[d] = jnp.where(first, high, low).astype(BF)
        send(psend.at[d], precv.at[d], core_ss.at[d], core_rs.at[d], twin)

    def twin_got(d):
        got(precv.at[d], core_ss.at[d], core_rs.at[d], twin)

    def z_rows(side, dist, j):
        return dist < 4 or (j < NS // 2) == (side == 0)

    def z_step(dist):
        offsets = (4,) if dist == 4 else (dist, 8 - dist)
        for d in offsets:
            twin_got(d)
        for j in range(NS):
            rows = pl.ds(j * SUB, SUB)
            for side in (0, 1):
                if not z_rows(side, dist, j):
                    continue
                d = dist if side == 0 else (8 - dist) % 8
                value = pown[d, rows] + precv[d, rows].astype(F32)
                if dist < 4 and z_rows(side, dist + 1, j):
                    got(zr.at[side, dist, rows], rz_ss.at[side, dist + 1, j], rz_rs.at[side, dist + 1, j], at_z(-1 if side == 0 else 1))
                    value = value + zr[side, dist, rows].astype(F32)
                zs[side, dist, rows] = value.astype(BF)
                send(
                    zs.at[side, dist, rows], zr.at[side, dist - 1, rows],
                    rz_ss.at[side, dist, j], rz_rs.at[side, dist, j], at_z(1 if side == 0 else -1),
                )

    product(4)
    product(3)
    product(5)
    z_step(4)
    product(2)
    product(6)
    z_step(3)
    product(1)
    product(7)
    z_step(2)
    product(0)
    z_step(1)
    twin_got(0)
    for j in range(NS):
        rows = pl.ds(j * SUB, SUB)
        value = pown[0, rows] + precv[0, rows].astype(F32)
        for side in (0, 1):
            got(zr.at[side, 0, rows], rz_ss.at[side, 1, j], rz_rs.at[side, 1, j], at_z(-1 if side == 0 else 1))
            value = value + zr[side, 0, rows].astype(F32)
        axb[rows] = value.astype(BF)

    def cot_wait(i, _):
        cot_copy(i, c, (c + 16 - i) % 16).wait_recv()
        return 0

    lax.fori_loop(1, 16, cot_wait, 0)
    hidden = lax.dot_general(w_ref[...], axb[...], TN, preferred_element_type=F32)
    sig = jax.nn.sigmoid(hidden)
    actb[...] = (hidden * sig).astype(BF)
    slb[...] = (cotb[...].astype(F32) * sig * (1.0 + hidden * (1.0 - sig))).astype(BF)
    tg[z, k] = jnp.dot(w_ref[...], slb[...], preferred_element_type=F32).astype(BF)

    def gz_send(side, dist, j):
        owner = (z - dist + 8) % 8 if side == 0 else (z + dist) % 8
        piece = tg.at[owner, k, pl.ds(j * SUB, SUB)]
        send(piece, piece, gz_ss.at[side, dist, j], gz_rs.at[side, dist, j], at_z(1 if side == 0 else -1))

    def gz_got(side, dist, j):
        owner = (z - dist + 8) % 8 if side == 0 else (z + dist) % 8
        piece = tg.at[owner, k, pl.ds(j * SUB, SUB)]
        got(piece, gz_ss.at[side, dist - 1, j], gz_rs.at[side, dist - 1, j], at_z(-1 if side == 0 else 1))

    def gc_send(d):
        piece = tg.at[(z + d) % 8, k]
        send(piece, piece, gc_ss.at[d], gc_rs.at[d], twin)

    def gc_got(d):
        piece = tg.at[(z + d) % 8, 1 - k]
        got(piece, gc_ss.at[d], gc_rs.at[d], twin)

    for j in range(NS):
        for side in (0, 1):
            gz_send(side, 0, j)
    gc_send(0)

    def act_copy(i, peer, mine):
        return rc(
            actb.at[pl.ds(pl.multiple_of(peer * 32, 32), 32), :],
            act_ref.at[:, pl.ds(pl.multiple_of(mine * 128, 128), 128)],
            act_ss.at[i], act_rs.at[i], (r, peer),
        )

    def act_send(i, _):
        act_copy(i, (c + i) % 16, c).start()
        return 0

    lax.fori_loop(1, 16, act_send, 0)
    act_ref[:, pl.ds(pl.multiple_of(c * 128, 128), 128)] = actb[pl.ds(pl.multiple_of(c * 32, 32), 32), :]

    wp[...] = lax.dot_general(axb[...], slb[...], NT, preferred_element_type=F32).astype(BF)

    def w_rows(i):
        return pl.ds(pl.multiple_of(i * 32, 32), 32)

    def w1_copy(i, peer, mine):
        return rc(wp.at[w_rows(peer)], wr.at[mine], w1_ss.at[i], w1_rs.at[i], (peer, c))

    def w1_send(i, _):
        w1_copy(i, (r + i) % 16, r).start()
        return 0

    lax.fori_loop(1, 16, w1_send, 0)
    wr[r] = wp[w_rows(r)]

    def gather_step(dist):
        for j in range(NS):
            for side in (0, 1):
                if not z_rows(side, dist, j):
                    continue
                gz_got(side, dist, j)
                if dist < 4 and z_rows(side, dist + 1, j):
                    gz_send(side, dist, j)
        for d in (4,) if dist == 4 else (dist, 8 - dist):
            gc_send(d)

    def back_part(d):
        block = (z + d) % 8
        left = jnp.concatenate([tg[block, 0], tg[block, 1]], axis=1)
        rows = pl.ds(pl.multiple_of(block * 256, 256), 256)
        return jnp.dot(left, a[rows, :], preferred_element_type=F32)

    gc_got(0)
    acc[...] = back_part(0)
    for dist in (1, 2, 3, 4):
        gather_step(dist)
        for d in (4,) if dist == 4 else (dist, 8 - dist):
            gc_got(d)
            acc[...] += back_part(d)

    def q_rows(h, o1, o2):
        if h == 0:
            block = (x + o1) % 4 * 4 + (y + o2) % 4
        else:
            block = (x + o2) % 4 * 4 + (y + o1) % 4
        return block * 32

    def q(h, o1, o2, half):
        start = q_rows(h, o1, o2)
        if half is None:
            return acc[pl.ds(pl.multiple_of(start, 32), 32), h * 1024 : (h + 1) * 1024]
        return acc[pl.ds(pl.multiple_of(start + 16 * half, 16), 16), h * 1024 : (h + 1) * 1024]

    def rx_axis(h, ring):
        return (at_x, at_y)[(h + ring) % 2]

    def rx(src, dst, h, ring, lane, j, start):
        dev = rx_axis(h, ring)(1 if j % 2 == 0 else -1)
        if start:
            send(src, dst, rx_ss.at[h, lane, j], rx_rs.at[h, lane, j], dev)
        else:
            got(dst, rx_ss.at[h, lane, j], rx_rs.at[h, lane, j], dev)

    ORDER = (2, 1, 3, 0)
    for o2 in ORDER:
        for h in (0, 1):
            for j in (0, 1):
                xs1[h, o2, 0, 16 * j : 16 * j + 16] = q(h, 2, o2, j).astype(BF)
                rx(xs1.at[h, o2, 0, 16 * j : 16 * j + 16], xr1h.at[h, o2, j], h, 0, o2, j, True)

    def w1_wait(i, _):
        w1_copy(i, r, (r + 16 - i) % 16).wait_recv()
        return 0

    lax.fori_loop(1, 16, w1_wait, 0)
    total = wr[0].astype(F32)
    for i in range(1, 16):
        total = total + wr[i].astype(F32)
    wz[c] = total.astype(BF)

    def w2_copy(i, peer, mine):
        return rc(wz.at[mine], wz.at[mine], w2_ss.at[i], w2_rs.at[i], (r, peer))

    def w2_send(i, _):
        w2_copy(i, (c + i) % 16, c).start()
        return 0

    lax.fori_loop(1, 16, w2_send, 0)

    for o2 in ORDER:
        for h in (0, 1):
            for j, o in ((0, 1), (1, 3)):
                rx(None, xr1h.at[h, o2, j], h, 0, o2, j, False)
                xs1[h, o2, 1 + j, 16 * j : 16 * j + 16] = (q(h, o, o2, j) + xr1h[h, o2, j].astype(F32)).astype(BF)
                xs1[h, o2, 1 + j, 16 - 16 * j : 32 - 16 * j] = q(h, o, o2, 1 - j).astype(BF)
                rx(xs1.at[h, o2, 1 + j], xr1f.at[h, o2, j], h, 0, o2, 2 + j, True)

    for o2 in ORDER:
        for h in (0, 1):
            for j in (0, 1):
                rx(None, xr1f.at[h, o2, j], h, 0, o2, 2 + j, False)
            s1[h, o2] = q(h, 0, o2, None) + xr1f[h, o2, 0].astype(F32) + xr1f[h, o2, 1].astype(F32)
            if o2 == 2:
                for j in (0, 1):
                    xs2[h, 0, 16 * j : 16 * j + 16] = s1[h, 2, 16 * j : 16 * j + 16].astype(BF)
                    rx(xs2.at[h, 0, 16 * j : 16 * j + 16], xr2h.at[h, j], h, 1, 4, j, True)

    def w2_wait(i, _):
        w2_copy(i, c, (c + 16 - i) % 16).wait_recv()
        return 0

    lax.fori_loop(1, 16, w2_wait, 0)
    total = wz[0].astype(F32)
    for i in range(1, 16):
        total = total + wz[i].astype(F32)
    wg_ref[w_rows(r)] = total.astype(BF)

    def w3_copy(i, peer, mine):
        return rc(wg_ref.at[w_rows(mine)], wg_ref.at[w_rows(mine)], w3_ss.at[i], w3_rs.at[i], (peer, c))

    def w3_send(i, _):
        w3_copy(i, (r + i) % 16, r).start()
        return 0

    lax.fori_loop(1, 16, w3_send, 0)

    for h in (0, 1):
        for j, o in ((0, 1), (1, 3)):
            rx(None, xr2h.at[h, j], h, 1, 4, j, False)
            xs2[h, 1 + j, 16 * j : 16 * j + 16] = (s1[h, o, 16 * j : 16 * j + 16] + xr2h[h, j].astype(F32)).astype(BF)
            xs2[h, 1 + j, 16 - 16 * j : 32 - 16 * j] = s1[h, o, 16 - 16 * j : 32 - 16 * j].astype(BF)
            rx(xs2.at[h, 1 + j], xr2f.at[h, j], h, 1, 4, 2 + j, True)
    for h in (0, 1):
        for j in (0, 1):
            rx(None, xr2f.at[h, j], h, 1, 4, 2 + j, False)
        value = s1[h, 0] + xr2f[h, 0].astype(F32) + xr2f[h, 1].astype(F32)
        fg_ref[:, h * 1024 : (h + 1) * 1024] = value.astype(BF)

    def last(i, _):
        act_copy(i, c, (c + 16 - i) % 16).wait_recv()
        w3_copy(i, r, (r + 16 - i) % 16).wait_recv()
        act_copy(i, (c + i) % 16, c).wait_send()
        cot_copy(i, (c + i) % 16, c).wait_send()
        w1_copy(i, (r + i) % 16, r).wait_send()
        w2_copy(i, (c + i) % 16, c).wait_send()
        w3_copy(i, (r + i) % 16, r).wait_send()
        return 0

    lax.fori_loop(1, 16, last, 0)
    for copy in sent:
        copy.wait_send()


def layer(xt, cot, weight, a):
    dma = pltpu.SemaphoreType.DMA
    vm = pltpu.VMEM
    vspec = pl.BlockSpec(memory_space=pltpu.VMEM)
    return pl.pallas_call(
        layer_kernel,
        out_shape=(
            jax.ShapeDtypeStruct((32, 2048), BF),
            jax.ShapeDtypeStruct((32, 2048), BF),
            jax.ShapeDtypeStruct((512, 512), BF),
        ),
        in_specs=[vspec] * 3 + [pl.BlockSpec(memory_space=pl.ANY)],
        out_specs=(vspec,) * 3,
        scratch_shapes=[
            vm((2048, 2048), BF),
            vm((2, 4, 4, 32, 1024), BF),
            vm((512, 128), BF),
            vm((8, 512, 128), F32),
            vm((8, 512, 128), BF),
            vm((8, 512, 128), BF),
            vm((2, 4, 512, 128), BF),
            vm((2, 5, 512, 128), BF),
            vm((512, 128), BF),
            vm((512, 128), BF),
            vm((512, 128), BF),
            vm((8, 2, 512, 128), BF),
            vm((512, 2048), F32),
            vm((2, 4, 3, 32, 1024), BF),
            vm((2, 4, 2, 16, 1024), BF),
            vm((2, 4, 2, 32, 1024), BF),
            vm((2, 4, 32, 1024), F32),
            vm((2, 3, 32, 1024), BF),
            vm((2, 2, 16, 1024), BF),
            vm((2, 2, 32, 1024), BF),
            vm((512, 512), BF),
            vm((16, 32, 512), BF),
            vm((16, 32, 512), BF),
            dma,
            dma,
        ]
        + [dma((16,))] * 2
        + [dma((2, 5, 4))] * 2
        + [dma((8,))] * 2
        + [dma((2, 5, NS))] * 2
        + [dma((16,))] * 2
        + [dma((2, 4, NS))] * 2
        + [dma((8,))] * 2
        + [dma((2, 5, 4))] * 2
        + [dma((16,))] * 6,
        compiler_params=pltpu.CompilerParams(
            collective_id=0, has_side_effects=True, vmem_limit_bytes=56 << 20
        ),
        name="layer",
    )(xt, cot, weight, a)


def shards(features, weight, block_cols, block_count, edge_src, edge_dst, edge_weight, cotangent):
    a = build(block_cols[:, 0, :], block_count[:, 0], edge_src[:, 0], edge_dst[:, 0], edge_weight[:, 0])
    act, fg, wg = layer(features.T, cotangent.T, weight, a)
    return act.T, fg.T, wg.astype(F32)


def solution(mesh):
    return jax.shard_map(
        shards,
        mesh=mesh,
        in_specs=(
            P("col", "row"),
            P(),
            P("row", "col", None),
            P("row", "col"),
            P("row", "col", None, None),
            P("row", "col", None, None),
            P("row", "col", None, None),
            P("row", "col"),
        ),
        out_specs=(P("row", "col"), P("col", "row"), P()),
        check_vma=False,
    )
```

```python
import jax
import jax.numpy as jnp
from jax import lax
from jax.experimental import pallas as pl
from jax.experimental.pallas import tpu as pltpu
from jax.sharding import PartitionSpec as P

MESH = pl.DeviceIdType.MESH
BF = jnp.bfloat16
F32 = jnp.float32
NT = (((1,), (1,)), ((), ()))
TN = (((0,), (0,)), ((), ()))
NS = 2
SUB = 512 // NS


def layer_kernel(
    cols_ref, counts_ref, src_ref, dst_ref, ew_ref, xt_ref, cot_ref, w_ref,
    act_ref, fg_ref, wg_ref,
    a, tiles, xg, cotb, pown, psend, precv, zr, zs, axb, axl, actb, slb, tg, acc,
    xs1, xr1h, xr1f, s1, xs2, xr2h, xr2f,
    wp, wr, wz,
    cot_ss, cot_rs, ag_ss, ag_rs, core_ss, core_rs, rz_ss, rz_rs,
    act_ss, act_rs, gz_ss, gz_rs, gc_ss, gc_rs, rx_ss, rx_rs,
    w1_ss, w1_rs, w2_ss, w2_rs, w3_ss, w3_rs,
):
    r = lax.axis_index("row")
    c = lax.axis_index("col")
    x, y = r // 4, r % 4
    z, k = c // 2, c % 2

    def at_x(o):
        return ((x + o) % 4 * 4 + y, c)

    def at_y(o):
        return (x * 4 + (y + o) % 4, c)

    def at_z(o):
        return (r, (z + o) % 8 * 2 + k)

    twin = (r, z * 2 + 1 - k)

    def rc(src, dst, ss, rs, dev):
        return pltpu.make_async_remote_copy(
            src_ref=src, dst_ref=dst, send_sem=ss, recv_sem=rs, device_id=dev, device_id_type=MESH
        )

    sent = []

    def send(src, dst, ss, rs, dev):
        copy = rc(src, dst, ss, rs, dev)
        copy.start()
        sent.append(copy)

    def got(ref, ss, rs, dev):
        rc(ref, ref, ss, rs, dev).wait_recv()

    barrier = pltpu.get_barrier_semaphore()

    def greet(i, _):
        pl.semaphore_signal(barrier, inc=1, device_id=((r + i) % 16, c), device_id_type=MESH)
        pl.semaphore_signal(barrier, inc=1, device_id=(r, (c + i) % 16), device_id_type=MESH)
        return 0

    lax.fori_loop(1, 16, greet, 0)
    for h in (0, 1):
        xg[h, x, y] = xt_ref[:, h * 1024 : (h + 1) * 1024]
    pl.semaphore_wait(barrier, 30)

    spots = lax.broadcasted_iota(jnp.int32, (128, 512), 0).astype(F32).astype(BF)
    slots = lax.broadcasted_iota(jnp.int32, (8, 512), 0)

    def spread(row):
        piece = jnp.broadcast_to(row, (16, row.shape[1])).astype(BF)
        return jnp.concatenate([piece] * 8, axis=0)

    def build_block(g):
        src = src_ref[g].astype(F32)
        dst = dst_ref[g].astype(F32)
        wts = jnp.where(slots < counts_ref[0, g], ew_ref[g].astype(F32), 0.0)
        for s in range(8):
            left = jnp.where(spots == spread(dst[s : s + 1]), spread(wts[s : s + 1]), BF(0))
            right = jnp.where(spots == spread(src[s : s + 1]), BF(1), BF(0))
            tiles[s] = lax.dot_general(left, right, NT, preferred_element_type=F32).astype(BF)
        names = [spread(jnp.full((1, 128), cols_ref[s, g].astype(F32), F32)) for s in range(8)]
        rows = pl.ds(pl.multiple_of(g * 128, 128), 128)

        def place(j, _):
            here = spread(jnp.full((1, 128), j.astype(F32), F32))
            total = jnp.where(names[0] == here, tiles[0], BF(0))
            for s in range(1, 8):
                total = total + jnp.where(names[s] == here, tiles[s], BF(0))
            a[rows, pl.ds(pl.multiple_of(j * 128, 128), 128)] = total
            return 0

        lax.fori_loop(0, 16, place, 0, unroll=4)

    def build(*offsets):
        for d in offsets:

            def one(i, _, d=d):
                build_block((z + d) % 8 * 2 + i)
                return 0

            lax.fori_loop(0, 2, one, 0)

    def xg_at(h, o1, o2):
        if h == 0:
            return xg.at[0, (x + o2) % 4, (y + o1) % 4]
        return xg.at[1, (x + o1) % 4, (y + o2) % 4]

    def axis(h, ring):
        return (at_y, at_x)[(h + ring) % 2]

    def ag_send(h, ring, lane, j, piece):
        dev = axis(h, ring)(1 if j % 2 == 0 else -1)
        if j == 2:
            piece = piece.at[0:16]
        if j == 3:
            piece = piece.at[16:32]
        send(piece, piece, ag_ss.at[h, lane, j], ag_rs.at[h, lane, j], dev)

    def ag_got(h, ring, lane, j, piece):
        dev = axis(h, ring)(-1 if j % 2 == 0 else 1)
        if j == 2:
            piece = piece.at[0:16]
        if j == 3:
            piece = piece.at[16:32]
        got(piece, ag_ss.at[h, lane, j], ag_rs.at[h, lane, j], dev)

    def ag_ring2_own(h, o1):
        for j in (0, 1):
            ag_send(h, 1, 1 + o1, j, xg_at(h, o1, 0))

    def ag_ring2_pass(h, o1):
        for j, o in ((0, 3), (1, 1)):
            ag_got(h, 1, 1 + o1, j, xg_at(h, o1, o))
            ag_send(h, 1, 1 + o1, 2 + j, xg_at(h, o1, o))

    for h in (0, 1):
        for j in (0, 1):
            ag_send(h, 0, 0, j, xg_at(h, 0, 0))
    for h in (0, 1):
        ag_ring2_own(h, 0)

    def cot_copy(i, peer, mine):
        return rc(
            cot_ref.at[:, pl.ds(pl.multiple_of(peer * 128, 128), 128)],
            cotb.at[pl.ds(pl.multiple_of(mine * 32, 32), 32), :],
            cot_ss.at[i], cot_rs.at[i], (r, peer),
        )

    def cot_send(i, _):
        cot_copy(i, (c + i) % 16, c).start()
        return 0

    lax.fori_loop(1, 16, cot_send, 0)
    cotb[pl.ds(pl.multiple_of(c * 32, 32), 32), :] = cot_ref[:, pl.ds(pl.multiple_of(c * 128, 128), 128)]

    build(4)
    for j, o in ((0, 3), (1, 1)):
        for h in (0, 1):
            ag_got(h, 0, 0, j, xg_at(h, o, 0))
            ag_send(h, 0, 0, 2 + j, xg_at(h, o, 0))
            ag_ring2_own(h, o)
    build(3)
    for h in (0, 1):
        ag_ring2_pass(h, 0)
    for h in (0, 1):
        for j in (2, 3):
            ag_got(h, 0, 0, j, xg_at(h, 2, 0))
        ag_ring2_own(h, 2)
    build(5)
    for o1 in (3, 1):
        for h in (0, 1):
            ag_ring2_pass(h, o1)
    build(2)
    for h in (0, 1):
        ag_ring2_pass(h, 2)
    build(6)
    for o1 in (0, 3, 1, 2):
        for h in (0, 1):
            for j in (2, 3):
                ag_got(h, 1, 1 + o1, j, xg_at(h, o1, 2))

    def product(d):
        rows = pl.ds(pl.multiple_of((z + d) % 8 * 256, 256), 256)
        total = lax.dot_general(
            xg[0].reshape(512, 1024), a[rows, 0:1024], NT, preferred_element_type=F32
        ) + lax.dot_general(
            xg[1].reshape(512, 1024), a[rows, 1024:2048], NT, preferred_element_type=F32
        )
        low, high = total[:, 0:128], total[:, 128:256]
        first = k == 0
        pown[d] = jnp.where(first, low, high)
        psend[d] = jnp.where(first, high, low)
        send(psend.at[d], precv.at[d], core_ss.at[d], core_rs.at[d], twin)

    def twin_got(d):
        got(precv.at[d], core_ss.at[d], core_rs.at[d], twin)

    def z_rows(side, dist, j):
        return dist < 4 or (j < NS // 2) == (side == 0)

    def z_step(dist):
        offsets = (4,) if dist == 4 else (dist, 8 - dist)
        for d in offsets:
            twin_got(d)
        for j in range(NS):
            rows = pl.ds(j * SUB, SUB)
            for side in (0, 1):
                if not z_rows(side, dist, j):
                    continue
                d = dist if side == 0 else (8 - dist) % 8
                value = pown[d, rows] + precv[d, rows]
                if dist < 4 and z_rows(side, dist + 1, j):
                    got(zr.at[side, dist, rows], rz_ss.at[side, dist + 1, j], rz_rs.at[side, dist + 1, j], at_z(-1 if side == 0 else 1))
                    value = value + zr[side, dist, rows].astype(F32)
                zs[side, dist, rows] = value.astype(BF)
                send(
                    zs.at[side, dist, rows], zr.at[side, dist - 1, rows],
                    rz_ss.at[side, dist, j], rz_rs.at[side, dist, j], at_z(1 if side == 0 else -1),
                )

    product(4)
    product(3)
    product(5)
    z_step(4)
    product(2)
    product(6)
    z_step(3)
    build(1)
    product(1)
    build(7)
    product(7)
    z_step(2)
    build(0)
    product(0)
    z_step(1)
    twin_got(0)
    for j in range(NS):
        rows = pl.ds(j * SUB, SUB)
        value = pown[0, rows] + precv[0, rows]
        for side in (0, 1):
            got(zr.at[side, 0, rows], rz_ss.at[side, 1, j], rz_rs.at[side, 1, j], at_z(-1 if side == 0 else 1))
            value = value + zr[side, 0, rows].astype(F32)
        axb[rows] = value.astype(BF)
        axl[rows] = (value - axb[rows].astype(F32)).astype(BF)

    def cot_wait(i, _):
        cot_copy(i, c, (c + 16 - i) % 16).wait_recv()
        return 0

    lax.fori_loop(1, 16, cot_wait, 0)
    hidden = lax.dot_general(w_ref[...], axb[...], TN, preferred_element_type=F32)
    hidden = hidden + lax.dot_general(w_ref[...], axl[...], TN, preferred_element_type=F32)
    sig = jax.nn.sigmoid(hidden)
    actb[...] = (hidden * sig).astype(BF)
    slb[...] = (cotb[...].astype(F32) * sig * (1.0 + hidden * (1.0 - sig))).astype(BF)
    tg[z, k] = jnp.dot(w_ref[...], slb[...], preferred_element_type=F32).astype(BF)

    def gz_send(side, dist, j):
        owner = (z - dist + 8) % 8 if side == 0 else (z + dist) % 8
        piece = tg.at[owner, k, pl.ds(j * SUB, SUB)]
        send(piece, piece, gz_ss.at[side, dist, j], gz_rs.at[side, dist, j], at_z(1 if side == 0 else -1))

    def gz_got(side, dist, j):
        owner = (z - dist + 8) % 8 if side == 0 else (z + dist) % 8
        piece = tg.at[owner, k, pl.ds(j * SUB, SUB)]
        got(piece, gz_ss.at[side, dist - 1, j], gz_rs.at[side, dist - 1, j], at_z(-1 if side == 0 else 1))

    def gc_send(d):
        piece = tg.at[(z + d) % 8, k]
        send(piece, piece, gc_ss.at[d], gc_rs.at[d], twin)

    def gc_got(d):
        piece = tg.at[(z + d) % 8, 1 - k]
        got(piece, gc_ss.at[d], gc_rs.at[d], twin)

    for j in range(NS):
        for side in (0, 1):
            gz_send(side, 0, j)
    gc_send(0)

    def act_copy(i, peer, mine):
        return rc(
            actb.at[pl.ds(pl.multiple_of(peer * 32, 32), 32), :],
            act_ref.at[:, pl.ds(pl.multiple_of(mine * 128, 128), 128)],
            act_ss.at[i], act_rs.at[i], (r, peer),
        )

    def act_send(i, _):
        act_copy(i, (c + i) % 16, c).start()
        return 0

    lax.fori_loop(1, 16, act_send, 0)
    act_ref[:, pl.ds(pl.multiple_of(c * 128, 128), 128)] = actb[pl.ds(pl.multiple_of(c * 32, 32), 32), :]

    wp[...] = lax.dot_general(axb[...], slb[...], NT, preferred_element_type=F32).astype(BF)

    def w_rows(i):
        return pl.ds(pl.multiple_of(i * 32, 32), 32)

    def w1_copy(i, peer, mine):
        return rc(wp.at[w_rows(peer)], wr.at[mine], w1_ss.at[i], w1_rs.at[i], (peer, c))

    def w1_send(i, _):
        w1_copy(i, (r + i) % 16, r).start()
        return 0

    lax.fori_loop(1, 16, w1_send, 0)
    wr[r] = wp[w_rows(r)]

    def gather_step(dist):
        for j in range(NS):
            for side in (0, 1):
                if not z_rows(side, dist, j):
                    continue
                gz_got(side, dist, j)
                if dist < 4 and z_rows(side, dist + 1, j):
                    gz_send(side, dist, j)
        for d in (4,) if dist == 4 else (dist, 8 - dist):
            gc_send(d)

    def back_part(d):
        block = (z + d) % 8
        left = jnp.concatenate([tg[block, 0], tg[block, 1]], axis=1)
        rows = pl.ds(pl.multiple_of(block * 256, 256), 256)
        return jnp.dot(left, a[rows, :], preferred_element_type=F32)

    gc_got(0)
    acc[...] = back_part(0)
    for dist in (1, 2, 3, 4):
        gather_step(dist)
        for d in (4,) if dist == 4 else (dist, 8 - dist):
            gc_got(d)
            acc[...] += back_part(d)

    def q_rows(h, o1, o2):
        if h == 0:
            block = (x + o1) % 4 * 4 + (y + o2) % 4
        else:
            block = (x + o2) % 4 * 4 + (y + o1) % 4
        return block * 32

    def q(h, o1, o2, half):
        start = q_rows(h, o1, o2)
        if half is None:
            return acc[pl.ds(pl.multiple_of(start, 32), 32), h * 1024 : (h + 1) * 1024]
        return acc[pl.ds(pl.multiple_of(start + 16 * half, 16), 16), h * 1024 : (h + 1) * 1024]

    def rx_axis(h, ring):
        return (at_x, at_y)[(h + ring) % 2]

    def rx(src, dst, h, ring, lane, j, start):
        dev = rx_axis(h, ring)(1 if j % 2 == 0 else -1)
        if start:
            send(src, dst, rx_ss.at[h, lane, j], rx_rs.at[h, lane, j], dev)
        else:
            got(dst, rx_ss.at[h, lane, j], rx_rs.at[h, lane, j], dev)

    ORDER = (2, 1, 3, 0)
    for o2 in ORDER:
        for h in (0, 1):
            for j in (0, 1):
                xs1[h, o2, 0, 16 * j : 16 * j + 16] = q(h, 2, o2, j).astype(BF)
                rx(xs1.at[h, o2, 0, 16 * j : 16 * j + 16], xr1h.at[h, o2, j], h, 0, o2, j, True)

    def w1_wait(i, _):
        w1_copy(i, r, (r + 16 - i) % 16).wait_recv()
        return 0

    lax.fori_loop(1, 16, w1_wait, 0)
    total = wr[0].astype(F32)
    for i in range(1, 16):
        total = total + wr[i].astype(F32)
    wz[c] = total.astype(BF)

    def w2_copy(i, peer, mine):
        return rc(wz.at[mine], wz.at[mine], w2_ss.at[i], w2_rs.at[i], (r, peer))

    def w2_send(i, _):
        w2_copy(i, (c + i) % 16, c).start()
        return 0

    lax.fori_loop(1, 16, w2_send, 0)

    for o2 in ORDER:
        for h in (0, 1):
            for j, o in ((0, 1), (1, 3)):
                rx(None, xr1h.at[h, o2, j], h, 0, o2, j, False)
                xs1[h, o2, 1 + j, 16 * j : 16 * j + 16] = (q(h, o, o2, j) + xr1h[h, o2, j].astype(F32)).astype(BF)
                xs1[h, o2, 1 + j, 16 - 16 * j : 32 - 16 * j] = q(h, o, o2, 1 - j).astype(BF)
                rx(xs1.at[h, o2, 1 + j], xr1f.at[h, o2, j], h, 0, o2, 2 + j, True)

    for o2 in ORDER:
        for h in (0, 1):
            for j in (0, 1):
                rx(None, xr1f.at[h, o2, j], h, 0, o2, 2 + j, False)
            s1[h, o2] = q(h, 0, o2, None) + xr1f[h, o2, 0].astype(F32) + xr1f[h, o2, 1].astype(F32)
            if o2 == 2:
                for j in (0, 1):
                    xs2[h, 0, 16 * j : 16 * j + 16] = s1[h, 2, 16 * j : 16 * j + 16]
                    rx(xs2.at[h, 0, 16 * j : 16 * j + 16], xr2h.at[h, j], h, 1, 4, j, True)

    def w2_wait(i, _):
        w2_copy(i, c, (c + 16 - i) % 16).wait_recv()
        return 0

    lax.fori_loop(1, 16, w2_wait, 0)
    total = wz[0].astype(F32)
    for i in range(1, 16):
        total = total + wz[i].astype(F32)
    wg_ref[w_rows(r)] = total.astype(BF)

    def w3_copy(i, peer, mine):
        return rc(wg_ref.at[w_rows(mine)], wg_ref.at[w_rows(mine)], w3_ss.at[i], w3_rs.at[i], (peer, c))

    def w3_send(i, _):
        w3_copy(i, (r + i) % 16, r).start()
        return 0

    lax.fori_loop(1, 16, w3_send, 0)

    for h in (0, 1):
        for j, o in ((0, 1), (1, 3)):
            rx(None, xr2h.at[h, j], h, 1, 4, j, False)
            xs2[h, 1 + j, 16 * j : 16 * j + 16] = (s1[h, o, 16 * j : 16 * j + 16] + xr2h[h, j])
            xs2[h, 1 + j, 16 - 16 * j : 32 - 16 * j] = s1[h, o, 16 - 16 * j : 32 - 16 * j]
            rx(xs2.at[h, 1 + j], xr2f.at[h, j], h, 1, 4, 2 + j, True)
    for h in (0, 1):
        for j in (0, 1):
            rx(None, xr2f.at[h, j], h, 1, 4, 2 + j, False)
        value = s1[h, 0] + xr2f[h, 0] + xr2f[h, 1]
        fg_ref[:, h * 1024 : (h + 1) * 1024] = value.astype(BF)

    def last(i, _):
        act_copy(i, c, (c + 16 - i) % 16).wait_recv()
        w3_copy(i, r, (r + 16 - i) % 16).wait_recv()
        act_copy(i, (c + i) % 16, c).wait_send()
        cot_copy(i, (c + i) % 16, c).wait_send()
        w1_copy(i, (r + i) % 16, r).wait_send()
        w2_copy(i, (c + i) % 16, c).wait_send()
        w3_copy(i, (r + i) % 16, r).wait_send()
        return 0

    lax.fori_loop(1, 16, last, 0)
    for copy in sent:
        copy.wait_send()


def layer(cols, counts, src, dst, ew, xt, cot, weight):
    dma = pltpu.SemaphoreType.DMA
    vm = pltpu.VMEM
    vspec = pl.BlockSpec(memory_space=pltpu.VMEM)
    return pl.pallas_call(
        layer_kernel,
        out_shape=(
            jax.ShapeDtypeStruct((32, 2048), BF),
            jax.ShapeDtypeStruct((32, 2048), BF),
            jax.ShapeDtypeStruct((512, 512), BF),
        ),
        in_specs=[pl.BlockSpec(memory_space=pltpu.SMEM)] * 2 + [vspec] * 6,
        out_specs=(vspec,) * 3,
        scratch_shapes=[
            vm((2048, 2048), BF),
            vm((8, 128, 128), BF),
            vm((2, 4, 4, 32, 1024), BF),
            vm((512, 128), BF),
            vm((8, 512, 128), F32),
            vm((8, 512, 128), F32),
            vm((8, 512, 128), F32),
            vm((2, 4, 512, 128), BF),
            vm((2, 5, 512, 128), BF),
            vm((512, 128), BF),
            vm((512, 128), BF),
            vm((512, 128), BF),
            vm((512, 128), BF),
            vm((8, 2, 512, 128), BF),
            vm((512, 2048), F32),
            vm((2, 4, 3, 32, 1024), BF),
            vm((2, 4, 2, 16, 1024), BF),
            vm((2, 4, 2, 32, 1024), BF),
            vm((2, 4, 32, 1024), F32),
            vm((2, 3, 32, 1024), F32),
            vm((2, 2, 16, 1024), F32),
            vm((2, 2, 32, 1024), F32),
            vm((512, 512), BF),
            vm((16, 32, 512), BF),
            vm((16, 32, 512), BF),
        ]
        + [dma((16,))] * 2
        + [dma((2, 5, 4))] * 2
        + [dma((8,))] * 2
        + [dma((2, 5, NS))] * 2
        + [dma((16,))] * 2
        + [dma((2, 4, NS))] * 2
        + [dma((8,))] * 2
        + [dma((2, 5, 4))] * 2
        + [dma((16,))] * 6,
        compiler_params=pltpu.CompilerParams(
            collective_id=0, has_side_effects=True, vmem_limit_bytes=58 << 20
        ),
        name="layer",
    )(cols, counts, src, dst, ew, xt, cot, weight)


def finish_kernel(act_ref, fg_ref, wg_ref, act_out, fg_out, wg_out, wg_in, sems):
    copies = [
        pltpu.make_async_copy(wg_ref, wg_in, sems.at[0]),
        pltpu.make_async_copy(act_ref, act_out, sems.at[1]),
        pltpu.make_async_copy(fg_ref, fg_out, sems.at[2]),
    ]
    for copy in copies:
        copy.start()
    copies[0].wait()
    wg_out[...] = wg_in[...].astype(F32)
    copies[1].wait()
    copies[2].wait()


def finish(act, fg, wg):
    anywhere = pl.BlockSpec(memory_space=pl.ANY)
    return pl.pallas_call(
        finish_kernel,
        out_shape=(
            jax.ShapeDtypeStruct((32, 2048), BF),
            jax.ShapeDtypeStruct((32, 2048), BF),
            jax.ShapeDtypeStruct((512, 512), F32),
        ),
        in_specs=[anywhere] * 3,
        out_specs=(anywhere, anywhere, pl.BlockSpec(memory_space=pltpu.VMEM)),
        scratch_shapes=[pltpu.VMEM((512, 512), BF), pltpu.SemaphoreType.DMA((3,))],
        compiler_params=pltpu.CompilerParams(vmem_limit_bytes=58 << 20),
        name="finish",
    )(act, fg, wg)


def shards(features, weight, block_cols, block_count, edge_src, edge_dst, edge_weight, cotangent):
    outs = layer(
        block_cols[:, 0, :].T, block_count.T, edge_src[:, 0], edge_dst[:, 0], edge_weight[:, 0],
        features.T, cotangent.T, weight,
    )
    act, fg, wg = finish(*outs)
    return act.T, fg.T, wg


def solution(mesh):
    return jax.shard_map(
        shards,
        mesh=mesh,
        in_specs=(
            P("col", "row"),
            P(),
            P("row", "col", None),
            P("row", "col"),
            P("row", "col", None, None),
            P("row", "col", None, None),
            P("row", "col", None, None),
            P("row", "col"),
        ),
        out_specs=(P("row", "col"), P("col", "row"), P()),
        check_vma=False,
    )
```

```python
import jax
import jax.numpy as jnp
from jax import lax
from jax.experimental import pallas as pl
from jax.experimental.pallas import tpu as pltpu
from jax.sharding import PartitionSpec as P

MESH = pl.DeviceIdType.MESH
BF = jnp.bfloat16
F32 = jnp.float32
NT = (((1,), (1,)), ((), ()))
TN = (((0,), (0,)), ((), ()))
NS = 4
SUB = 512 // NS


def layer_kernel(
    cols_ref, counts_ref, src_ref, dst_ref, ew_ref, xt_ref, cot_ref, w_ref,
    act_ref, fg_ref, wg_ref,
    a, tiles, xg, cotb, pown, psend, precv, zr, zs, axb, axl, actb, slb, sll, tg, acc,
    xs1, xr1h, xr1f, s1, xs2, xr2h, xr2f,
    wp, w0r, w0s, w1r, wz,
    cot_ss, cot_rs, ag_ss, ag_rs, core_ss, core_rs, rz_ss, rz_rs,
    act_ss, act_rs, gz_ss, gz_rs, gc_ss, gc_rs, rx_ss, rx_rs,
    w0_ss, w0_rs, w1_ss, w1_rs, w2_ss, w2_rs, w3_ss, w3_rs,
):
    r = lax.axis_index("row")
    c = lax.axis_index("col")
    x, y = r // 4, r % 4
    z, k = c // 2, c % 2

    def at_x(o):
        return ((x + o) % 4 * 4 + y, c)

    def at_y(o):
        return (x * 4 + (y + o) % 4, c)

    def at_z(o):
        return (r, (z + o) % 8 * 2 + k)

    twin = (r, z * 2 + 1 - k)

    def rc(src, dst, ss, rs, dev):
        return pltpu.make_async_remote_copy(
            src_ref=src, dst_ref=dst, send_sem=ss, recv_sem=rs, device_id=dev, device_id_type=MESH
        )

    sent = []

    def send(src, dst, ss, rs, dev):
        copy = rc(src, dst, ss, rs, dev)
        copy.start()
        sent.append(copy)

    def got(ref, ss, rs, dev):
        rc(ref, ref, ss, rs, dev).wait_recv()

    barrier = pltpu.get_barrier_semaphore()

    def greet(i, _):
        pl.semaphore_signal(barrier, inc=1, device_id=((r + i) % 16, c), device_id_type=MESH)
        pl.semaphore_signal(barrier, inc=1, device_id=(r, (c + i) % 16), device_id_type=MESH)
        return 0

    lax.fori_loop(1, 16, greet, 0)
    for h in (0, 1):
        for b in range(h * 8, h * 8 + 8):
            xg[b, x, y] = xt_ref[:, b * 128 : (b + 1) * 128]
    pl.semaphore_wait(barrier, 30)

    spots = lax.broadcasted_iota(jnp.int32, (128, 512), 0).astype(F32).astype(BF)
    slots = lax.broadcasted_iota(jnp.int32, (8, 512), 0)

    def spread(row):
        piece = jnp.broadcast_to(row, (16, row.shape[1])).astype(BF)
        return jnp.concatenate([piece] * 8, axis=0)

    def make_block(g):
        src = src_ref[g].astype(F32)
        dst = dst_ref[g].astype(F32)
        wts = jnp.where(slots < counts_ref[0, g], ew_ref[g].astype(F32), 0.0)
        for s in range(8):
            left = jnp.where(spots == spread(dst[s : s + 1]), spread(wts[s : s + 1]), BF(0))
            right = jnp.where(spots == spread(src[s : s + 1]), BF(1), BF(0))
            tile = lax.dot_general(left, right, NT, preferred_element_type=F32)
            tiles[g, :, s * 128 : (s + 1) * 128] = tile.astype(BF)

    def place_block(g):
        names = [spread(jnp.full((1, 128), cols_ref[s, g].astype(F32), F32)) for s in range(8)]
        rows = pl.ds(pl.multiple_of(g * 128, 128), 128)
        for j in range(16):
            here = BF(j)
            t = [
                jnp.where(names[s] == here, tiles[g, :, s * 128 : (s + 1) * 128], BF(0))
                for s in range(8)
            ]
            total = ((t[0] + t[1]) + (t[2] + t[3])) + ((t[4] + t[5]) + (t[6] + t[7]))
            a[rows, j * 128 : (j + 1) * 128] = total

    def nth_block(i):
        n = i // 2
        step = (n + 1) // 2
        d = 4 + jnp.where(n % 2 == 1, -step, step)
        return (z + d) % 8 * 2 + i % 2

    def over(which, start, stop):
        def one(i, _):
            which(nth_block(i))
            return 0

        lax.fori_loop(start, stop, one, 0)

    def make(start, stop):
        over(make_block, start, stop)

    def place(start, stop):
        over(place_block, start, stop)

    def xg_at(h, o1, o2):
        if h == 0:
            return xg.at[0:8, (x + o2) % 4, (y + o1) % 4]
        return xg.at[8:16, (x + o1) % 4, (y + o2) % 4]

    def axis(h, ring):
        return (at_y, at_x)[(h + ring) % 2]

    def ag_send(h, ring, lane, j, piece):
        dev = axis(h, ring)(1 if j % 2 == 0 else -1)
        if j == 2:
            piece = piece.at[:, 0:16]
        if j == 3:
            piece = piece.at[:, 16:32]
        send(piece, piece, ag_ss.at[h, lane, j], ag_rs.at[h, lane, j], dev)

    def ag_got(h, ring, lane, j, piece):
        dev = axis(h, ring)(-1 if j % 2 == 0 else 1)
        if j == 2:
            piece = piece.at[:, 0:16]
        if j == 3:
            piece = piece.at[:, 16:32]
        got(piece, ag_ss.at[h, lane, j], ag_rs.at[h, lane, j], dev)

    def ag_ring2_own(h, o1):
        for j in (0, 1):
            ag_send(h, 1, 1 + o1, j, xg_at(h, o1, 0))

    def ag_ring2_pass(h, o1):
        for j, o in ((0, 3), (1, 1)):
            ag_got(h, 1, 1 + o1, j, xg_at(h, o1, o))
            ag_send(h, 1, 1 + o1, 2 + j, xg_at(h, o1, o))

    for h in (0, 1):
        for j in (0, 1):
            ag_send(h, 0, 0, j, xg_at(h, 0, 0))
    for h in (0, 1):
        ag_ring2_own(h, 0)

    def cot_copy(i, peer, mine):
        return rc(
            cot_ref.at[:, pl.ds(pl.multiple_of(peer * 128, 128), 128)],
            cotb.at[pl.ds(pl.multiple_of(mine * 32, 32), 32), :],
            cot_ss.at[i], cot_rs.at[i], (r, peer),
        )

    def cot_send(i, _):
        cot_copy(i, (c + i) % 16, c).start()
        return 0

    lax.fori_loop(1, 16, cot_send, 0)
    cotb[pl.ds(pl.multiple_of(c * 32, 32), 32), :] = cot_ref[:, pl.ds(pl.multiple_of(c * 128, 128), 128)]

    make(0, 3)
    for j, o in ((0, 3), (1, 1)):
        for h in (0, 1):
            ag_got(h, 0, 0, j, xg_at(h, o, 0))
            ag_send(h, 0, 0, 2 + j, xg_at(h, o, 0))
            ag_ring2_own(h, o)
    make(3, 6)
    for h in (0, 1):
        ag_ring2_pass(h, 0)
    for h in (0, 1):
        for j in (2, 3):
            ag_got(h, 0, 0, j, xg_at(h, 2, 0))
        ag_ring2_own(h, 2)
    make(6, 9)
    for o1 in (3, 1):
        for h in (0, 1):
            ag_ring2_pass(h, o1)
    make(9, 12)
    for h in (0, 1):
        ag_ring2_pass(h, 2)
    make(12, 16)
    for o1 in (0, 3, 1, 2):
        for h in (0, 1):
            for j in (2, 3):
                ag_got(h, 1, 1 + o1, j, xg_at(h, o1, 2))

    def block_product(g):
        picked = []
        for s in range(8):
            picked.append(xg[cols_ref[s, g]].reshape(512, 128))
        left = jnp.concatenate(picked, axis=1)
        return lax.dot_general(left, tiles[g], NT, preferred_element_type=F32)

    def product(d):
        first = (z + d) % 8 * 2
        psend[d] = block_product(first + 1 - k)
        send(psend.at[d], precv.at[d], core_ss.at[d], core_rs.at[d], twin)
        pown[d] = block_product(first + k)

    def twin_got(d):
        got(precv.at[d], core_ss.at[d], core_rs.at[d], twin)

    def z_rows(side, dist, j):
        return dist < 4 or (j < NS // 2) == (side == 0)

    def z_step(dist):
        offsets = (4,) if dist == 4 else (dist, 8 - dist)
        for d in offsets:
            twin_got(d)
        for j in range(NS):
            rows = pl.ds(j * SUB, SUB)
            for side in (0, 1):
                if not z_rows(side, dist, j):
                    continue
                d = dist if side == 0 else (8 - dist) % 8
                value = pown[d, rows] + precv[d, rows]
                if dist < 4 and z_rows(side, dist + 1, j):
                    got(zr.at[side, dist, rows], rz_ss.at[side, dist + 1, j], rz_rs.at[side, dist + 1, j], at_z(-1 if side == 0 else 1))
                    value = value + zr[side, dist, rows].astype(F32)
                zs[side, dist, rows] = value.astype(BF)
                send(
                    zs.at[side, dist, rows], zr.at[side, dist - 1, rows],
                    rz_ss.at[side, dist, j], rz_rs.at[side, dist, j], at_z(1 if side == 0 else -1),
                )

    product(4)
    product(3)
    product(5)
    z_step(4)
    product(2)
    product(6)
    place(0, 2)
    z_step(3)
    product(1)
    product(7)
    place(2, 5)
    z_step(2)
    product(0)
    place(5, 10)
    z_step(1)
    place(10, 16)
    twin_got(0)
    for j in range(NS):
        rows = pl.ds(j * SUB, SUB)
        value = pown[0, rows] + precv[0, rows]
        for side in (0, 1):
            got(zr.at[side, 0, rows], rz_ss.at[side, 1, j], rz_rs.at[side, 1, j], at_z(-1 if side == 0 else 1))
            value = value + zr[side, 0, rows].astype(F32)
        axb[rows] = value.astype(BF)
        axl[rows] = (value - axb[rows].astype(F32)).astype(BF)

    def cot_wait(i, _):
        cot_copy(i, c, (c + 16 - i) % 16).wait_recv()
        return 0

    lax.fori_loop(1, 16, cot_wait, 0)
    hidden = lax.dot_general(w_ref[...], axb[...], TN, preferred_element_type=F32)
    hidden = hidden + lax.dot_general(w_ref[...], axl[...], TN, preferred_element_type=F32)
    sig = jax.nn.sigmoid(hidden)
    actb[...] = (hidden * sig).astype(BF)
    slope = cotb[...].astype(F32) * sig * (1.0 + hidden * (1.0 - sig))
    slb[...] = slope.astype(BF)
    sll[...] = (slope - slb[...].astype(F32)).astype(BF)
    tg[z, k] = (
        jnp.dot(w_ref[...], slb[...], preferred_element_type=F32)
        + jnp.dot(w_ref[...], sll[...], preferred_element_type=F32)
    ).astype(BF)

    def gz_send(side, dist, j):
        owner = (z - dist + 8) % 8 if side == 0 else (z + dist) % 8
        piece = tg.at[owner, k, pl.ds(j * SUB, SUB)]
        send(piece, piece, gz_ss.at[side, dist, j], gz_rs.at[side, dist, j], at_z(1 if side == 0 else -1))

    def gz_got(side, dist, j):
        owner = (z - dist + 8) % 8 if side == 0 else (z + dist) % 8
        piece = tg.at[owner, k, pl.ds(j * SUB, SUB)]
        got(piece, gz_ss.at[side, dist - 1, j], gz_rs.at[side, dist - 1, j], at_z(-1 if side == 0 else 1))

    def gc_send(d):
        piece = tg.at[(z + d) % 8, k]
        send(piece, piece, gc_ss.at[d], gc_rs.at[d], twin)

    def gc_got(d):
        piece = tg.at[(z + d) % 8, 1 - k]
        got(piece, gc_ss.at[d], gc_rs.at[d], twin)

    for j in range(NS):
        for side in (0, 1):
            gz_send(side, 0, j)
    gc_send(0)

    def act_copy(i, peer, mine):
        return rc(
            actb.at[pl.ds(pl.multiple_of(peer * 32, 32), 32), :],
            act_ref.at[:, pl.ds(pl.multiple_of(mine * 128, 128), 128)],
            act_ss.at[i], act_rs.at[i], (r, peer),
        )

    def act_send(i, _):
        act_copy(i, (c + i) % 16, c).start()
        return 0

    wp[...] = (
        lax.dot_general(axb[...], slb[...], NT, preferred_element_type=F32)
        .astype(BF)
        .reshape(16, 2, 16, 512)
    )
    send(wp.at[:, 1 - k], w0r, w0_ss.at[0], w0_rs.at[0], twin)

    def w1_copy(i, peer, mine):
        return rc(w0s.at[peer], w1r.at[mine], w1_ss.at[i], w1_rs.at[i], (peer, c))

    def w1_send(i, _):
        w1_copy(i, (r + i) % 16, r).start()
        return 0

    def w1_wait(i, _):
        w1_copy(i, r, (r + 16 - i) % 16).wait_recv()
        return 0

    def w2_copy(i, peer, mine):
        return rc(wz.at[mine], wz.at[mine], w2_ss.at[i], w2_rs.at[i], (r, peer * 2 + k))

    def w2_send(i, _):
        w2_copy(i, (z + i) % 8, z).start()
        return 0

    def w2_wait(i, _):
        w2_copy(i, z, (z + 8 - i) % 8).wait_recv()
        return 0

    def w3_copy(i, peer, mine):
        return rc(wg_ref.at[mine, k], wg_ref.at[mine, k], w3_ss.at[i], w3_rs.at[i], (peer, c))

    def w3_send(i, _):
        w3_copy(i, (r + i) % 16, r).start()
        return 0

    def w3_wait(i, _):
        w3_copy(i, r, (r + 16 - i) % 16).wait_recv()
        return 0

    def w_start_row():
        got(w0r, w0_ss.at[0], w0_rs.at[0], twin)
        w0s[...] = (wp[:, k].astype(F32) + w0r[...].astype(F32)).astype(BF)
        lax.fori_loop(1, 16, w1_send, 0)
        w1r[r] = w0s[r]

    def w_start_z():
        lax.fori_loop(1, 16, w1_wait, 0)
        total = w1r[0].astype(F32)
        for i in range(1, 16):
            total = total + w1r[i].astype(F32)
        wz[z] = total.astype(BF)
        lax.fori_loop(1, 8, w2_send, 0)

    def w_start_last():
        lax.fori_loop(1, 8, w2_wait, 0)
        total = wz[0].astype(F32)
        for i in range(1, 8):
            total = total + wz[i].astype(F32)
        wg_ref[r, k] = total.astype(BF)
        lax.fori_loop(1, 16, w3_send, 0)

    def w_finish():
        lax.fori_loop(1, 16, w3_wait, 0)
        send(wg_ref.at[:, k], wg_ref.at[:, k], w0_ss.at[1], w0_rs.at[1], twin)
        got(wg_ref.at[:, 1 - k], w0_ss.at[1], w0_rs.at[1], twin)

    def gather_step(dist):
        for j in range(NS):
            for side in (0, 1):
                if not z_rows(side, dist, j):
                    continue
                gz_got(side, dist, j)
                if dist < 4 and z_rows(side, dist + 1, j):
                    gz_send(side, dist, j)
        for d in (4,) if dist == 4 else (dist, 8 - dist):
            gc_send(d)

    def back_part(d):
        block = (z + d) % 8
        left = jnp.concatenate([tg[block, 0], tg[block, 1]], axis=1)
        rows = pl.ds(pl.multiple_of(block * 256, 256), 256)
        return jnp.dot(left, a[rows, :], preferred_element_type=F32)

    gc_got(0)
    acc[...] = back_part(0)
    gather_step(1)
    w_start_row()
    gather_step(2)
    for dist in (1, 2):
        for d in (dist, 8 - dist):
            gc_got(d)
            acc[...] += back_part(d)
        gather_step(dist + 2)
    lax.fori_loop(1, 16, act_send, 0)
    act_ref[:, pl.ds(pl.multiple_of(c * 128, 128), 128)] = actb[pl.ds(pl.multiple_of(c * 32, 32), 32), :]
    w_start_z()
    for d in (3, 5):
        gc_got(d)
        acc[...] += back_part(d)
    gc_got(4)

    def last_part(o):
        block = (z + 4) % 8
        feats = pl.ds(pl.multiple_of((x + o) % 4 * 128, 128), 128)
        left = jnp.concatenate([tg[block, 0, feats], tg[block, 1, feats]], axis=1)
        rows = pl.ds(pl.multiple_of(block * 256, 256), 256)
        acc[feats] += jnp.dot(left, a[rows, :], preferred_element_type=F32)

    def q_rows(h, o1, o2):
        if h == 0:
            block = (x + o1) % 4 * 4 + (y + o2) % 4
        else:
            block = (x + o2) % 4 * 4 + (y + o1) % 4
        return block * 32

    def q(h, o1, o2, half):
        start = q_rows(h, o1, o2)
        if half is None:
            return acc[pl.ds(pl.multiple_of(start, 32), 32), h * 1024 : (h + 1) * 1024]
        return acc[pl.ds(pl.multiple_of(start + 16 * half, 16), 16), h * 1024 : (h + 1) * 1024]

    def rx_axis(h, ring):
        return (at_x, at_y)[(h + ring) % 2]

    def rx(src, dst, h, ring, lane, j, start):
        dev = rx_axis(h, ring)(1 if j % 2 == 0 else -1)
        if start:
            send(src, dst, rx_ss.at[h, lane, j], rx_rs.at[h, lane, j], dev)
        else:
            got(dst, rx_ss.at[h, lane, j], rx_rs.at[h, lane, j], dev)

    ORDER = (2, 1, 3, 0)

    def s1_halves(h, o2):
        for j in (0, 1):
            xs1[h, o2, 0, 16 * j : 16 * j + 16] = q(h, 2, o2, j).astype(BF)
            rx(xs1.at[h, o2, 0, 16 * j : 16 * j + 16], xr1h.at[h, o2, j], h, 0, o2, j, True)

    def s1_pass(h, o2, j):
        o = (1, 3)[j]
        rx(None, xr1h.at[h, o2, j], h, 0, o2, j, False)
        xs1[h, o2, 1 + j, 16 * j : 16 * j + 16] = (q(h, o, o2, j) + xr1h[h, o2, j].astype(F32)).astype(BF)
        xs1[h, o2, 1 + j, 16 - 16 * j : 32 - 16 * j] = q(h, o, o2, 1 - j).astype(BF)
        rx(xs1.at[h, o2, 1 + j], xr1f.at[h, o2, j], h, 0, o2, 2 + j, True)

    def s1_final(h, o2):
        for j in (0, 1):
            rx(None, xr1f.at[h, o2, j], h, 0, o2, 2 + j, False)
        s1[h, o2] = q(h, 0, o2, None) + xr1f[h, o2, 0].astype(F32) + xr1f[h, o2, 1].astype(F32)

    def s2_halves(h):
        for j in (0, 1):
            xs2[h, 0, 16 * j : 16 * j + 16] = s1[h, 2, 16 * j : 16 * j + 16].astype(BF)
            rx(xs2.at[h, 0, 16 * j : 16 * j + 16], xr2h.at[h, j], h, 1, 4, j, True)

    def s2_pass(h, j):
        o = (1, 3)[j]
        rx(None, xr2h.at[h, j], h, 1, 4, j, False)
        xs2[h, 1 + j, 16 * j : 16 * j + 16] = (s1[h, o, 16 * j : 16 * j + 16] + xr2h[h, j].astype(F32)).astype(BF)
        xs2[h, 1 + j, 16 - 16 * j : 32 - 16 * j] = s1[h, o, 16 - 16 * j : 32 - 16 * j].astype(BF)
        rx(xs2.at[h, 1 + j], xr2f.at[h, j], h, 1, 4, 2 + j, True)

    def s2_final(h):
        for j in (0, 1):
            rx(None, xr2f.at[h, j], h, 1, 4, 2 + j, False)
        value = s1[h, 0] + xr2f[h, 0].astype(F32) + xr2f[h, 1].astype(F32)
        fg_ref[:, h * 1024 : (h + 1) * 1024] = value.astype(BF)

    last_part(2)
    for o2 in ORDER:
        s1_halves(0, o2)
    s1_halves(1, 2)
    for o in (1, 3, 0):
        last_part(o)
        s1_halves(1, o)
    for o2 in ORDER:
        for h in (0, 1):
            for j in (0, 1):
                s1_pass(h, o2, j)
    w_start_last()
    for o2 in ORDER:
        for h in (0, 1):
            s1_final(h, o2)
            if o2 == 2:
                s2_halves(h)
    for h in (0, 1):
        for j in (0, 1):
            s2_pass(h, j)
    for h in (0, 1):
        s2_final(h)
    w_finish()

    def last(i, _):
        act_copy(i, c, (c + 16 - i) % 16).wait_recv()
        act_copy(i, (c + i) % 16, c).wait_send()
        cot_copy(i, (c + i) % 16, c).wait_send()
        w1_copy(i, (r + i) % 16, r).wait_send()
        w3_copy(i, (r + i) % 16, r).wait_send()
        return 0

    lax.fori_loop(1, 16, last, 0)

    def last_z(i, _):
        w2_copy(i, (z + i) % 8, z).wait_send()
        return 0

    lax.fori_loop(1, 8, last_z, 0)
    for copy in sent:
        copy.wait_send()


def layer(cols, counts, src, dst, ew, xt, cot, weight):
    dma = pltpu.SemaphoreType.DMA
    vm = pltpu.VMEM
    vspec = pl.BlockSpec(memory_space=pltpu.VMEM)
    return pl.pallas_call(
        layer_kernel,
        out_shape=(
            jax.ShapeDtypeStruct((32, 2048), BF),
            jax.ShapeDtypeStruct((32, 2048), BF),
            jax.ShapeDtypeStruct((16, 2, 16, 512), BF),
        ),
        in_specs=[pl.BlockSpec(memory_space=pltpu.SMEM)] * 2 + [vspec] * 6,
        out_specs=(vspec,) * 3,
        scratch_shapes=[
            vm((2048, 2048), BF),
            vm((16, 128, 1024), BF),
            vm((16, 4, 4, 32, 128), BF),
            vm((512, 128), BF),
            vm((8, 512, 128), F32),
            vm((8, 512, 128), F32),
            vm((8, 512, 128), F32),
            vm((2, 4, 512, 128), BF),
            vm((2, 5, 512, 128), BF),
            vm((512, 128), BF),
            vm((512, 128), BF),
            vm((512, 128), BF),
            vm((512, 128), BF),
            vm((512, 128), BF),
            vm((8, 2, 512, 128), BF),
            vm((512, 2048), F32),
            vm((2, 4, 3, 32, 1024), BF),
            vm((2, 4, 2, 16, 1024), BF),
            vm((2, 4, 2, 32, 1024), BF),
            vm((2, 4, 32, 1024), F32),
            vm((2, 3, 32, 1024), BF),
            vm((2, 2, 16, 1024), BF),
            vm((2, 2, 32, 1024), BF),
            vm((16, 2, 16, 512), BF),
            vm((16, 16, 512), BF),
            vm((16, 16, 512), BF),
            vm((16, 16, 512), BF),
            vm((8, 16, 512), BF),
        ]
        + [dma((16,))] * 2
        + [dma((2, 5, 4))] * 2
        + [dma((8,))] * 2
        + [dma((2, 5, NS))] * 2
        + [dma((16,))] * 2
        + [dma((2, 4, NS))] * 2
        + [dma((8,))] * 2
        + [dma((2, 5, 4))] * 2
        + [dma((2,))] * 2
        + [dma((16,))] * 2
        + [dma((8,))] * 2
        + [dma((16,))] * 2,
        compiler_params=pltpu.CompilerParams(
            collective_id=0, has_side_effects=True, vmem_limit_bytes=58 << 20
        ),
        name="layer",
    )(cols, counts, src, dst, ew, xt, cot, weight)


def finish_kernel(act_ref, fg_ref, wg_ref, act_out, fg_out, wg_out, act_in, fg_in, wg_in, sems):
    pairs = ((wg_ref, wg_in), (act_ref, act_in), (fg_ref, fg_in))
    copies = [pltpu.make_async_copy(src, dst, sems.at[i]) for i, (src, dst) in enumerate(pairs)]
    copies += [
        pltpu.make_async_copy(act_in, act_out, sems.at[3]),
        pltpu.make_async_copy(fg_in, fg_out, sems.at[4]),
    ]
    for copy in copies[:3]:
        copy.start()
    for i in (1, 2):
        copies[i].wait()
        copies[i + 2].start()
    copies[0].wait()
    wg_out[...] = wg_in[...].astype(F32)
    copies[3].wait()
    copies[4].wait()


def finish(act, fg, wg):
    anywhere = pl.BlockSpec(memory_space=pl.ANY)
    return pl.pallas_call(
        finish_kernel,
        out_shape=(
            jax.ShapeDtypeStruct((32, 2048), BF),
            jax.ShapeDtypeStruct((32, 2048), BF),
            jax.ShapeDtypeStruct((512, 512), F32),
        ),
        in_specs=[anywhere] * 3,
        out_specs=(anywhere, anywhere, pl.BlockSpec(memory_space=pltpu.VMEM)),
        scratch_shapes=[
            pltpu.VMEM((32, 2048), BF),
            pltpu.VMEM((32, 2048), BF),
            pltpu.VMEM((512, 512), BF),
            pltpu.SemaphoreType.DMA((5,)),
        ],
        compiler_params=pltpu.CompilerParams(vmem_limit_bytes=58 << 20),
        name="finish",
    )(act, fg, wg.reshape(512, 512))


def shards(features, weight, block_cols, block_count, edge_src, edge_dst, edge_weight, cotangent):
    outs = layer(
        block_cols[:, 0, :].T, block_count.T, edge_src[:, 0], edge_dst[:, 0], edge_weight[:, 0],
        features.T, cotangent.T, weight,
    )
    act, fg, wg = finish(*outs)
    return act.T, fg.T, wg


def solution(mesh):
    return jax.shard_map(
        shards,
        mesh=mesh,
        in_specs=(
            P("col", "row"),
            P(),
            P("row", "col", None),
            P("row", "col"),
            P("row", "col", None, None),
            P("row", "col", None, None),
            P("row", "col", None, None),
            P("row", "col"),
        ),
        out_specs=(P("row", "col"), P("col", "row"), P()),
        check_vma=False,
    )
```

```python
import jax
import jax.numpy as jnp
from jax import lax
from jax.experimental import pallas as pl
from jax.experimental.pallas import tpu as pltpu
from jax.sharding import PartitionSpec as P

MESH = pl.DeviceIdType.MESH
BF = jnp.bfloat16
F32 = jnp.float32
NT = (((1,), (1,)), ((), ()))
TN = (((0,), (0,)), ((), ()))
NS = 4
SUB = 512 // NS


def layer_kernel(
    cols_ref, counts_ref, src_ref, dst_ref, ew_ref, xt_ref, cot_ref, w_ref,
    act_ref, fg_ref, wg_ref,
    a, tiles, xg0, xg1, xg2, xg3, wt, cotb, pown, psend, precv, zr, zs, axb, axl, actb, slb, sll, tg, acc,
    xs1, xr1h, xr1f, s1, xs2, xr2,
    wp, w0r, w0s, w1r, wz,
    cot_ss, cot_rs, ag_ss, ag_rs, core_ss, core_rs, rz_ss, rz_rs,
    act_ss, act_rs, gz_ss, gz_rs, gc_ss, gc_rs, rx_ss, rx_rs,
    w0_ss, w0_rs, w1_ss, w1_rs, w2_ss, w2_rs, w3_ss, w3_rs,
):
    r = lax.axis_index("row")
    c = lax.axis_index("col")
    x, y = r // 4, r % 4
    z, k = c // 2, c % 2

    def at_x(o):
        return ((x + o) % 4 * 4 + y, c)

    def at_y(o):
        return (x * 4 + (y + o) % 4, c)

    def at_z(o):
        return (r, (z + o) % 8 * 2 + k)

    twin = (r, z * 2 + 1 - k)

    def rc(src, dst, ss, rs, dev):
        return pltpu.make_async_remote_copy(
            src_ref=src, dst_ref=dst, send_sem=ss, recv_sem=rs, device_id=dev, device_id_type=MESH
        )

    xg = (xg0, xg1, xg2, xg3)
    sent = []

    def send(src, dst, ss, rs, dev):
        copy = rc(src, dst, ss, rs, dev)
        copy.start()
        sent.append(copy)

    def got(ref, ss, rs, dev):
        rc(ref, ref, ss, rs, dev).wait_recv()

    barrier = pltpu.get_barrier_semaphore()

    def greet(i, _):
        pl.semaphore_signal(barrier, inc=1, device_id=((r + i) % 16, c), device_id_type=MESH)
        pl.semaphore_signal(barrier, inc=1, device_id=(r, (c + i) % 16), device_id_type=MESH)
        return 0

    lax.fori_loop(1, 16, greet, 0)
    for b in range(16):
        xg0[b, y] = xt_ref[:, b * 128 : (b + 1) * 128]

    spots = lax.broadcasted_iota(jnp.int32, (128, 512), 0).astype(F32).astype(BF)
    slots = lax.broadcasted_iota(jnp.int32, (8, 512), 0)

    def spread(row):
        piece = jnp.broadcast_to(row, (16, row.shape[1])).astype(BF)
        return jnp.concatenate([piece] * 8, axis=0)

    def make_block(g):
        src = src_ref[g].astype(F32)
        dst = dst_ref[g].astype(F32)
        wts = jnp.where(slots < counts_ref[0, g], ew_ref[g].astype(F32), 0.0)
        for s in range(8):
            left = jnp.where(spots == spread(dst[s : s + 1]), spread(wts[s : s + 1]), BF(0))
            right = jnp.where(spots == spread(src[s : s + 1]), BF(1), BF(0))
            tile = lax.dot_general(left, right, NT, preferred_element_type=F32)
            tiles[g, :, s * 128 : (s + 1) * 128] = tile.astype(BF)

    def place_block(g):
        names = [spread(jnp.full((1, 128), cols_ref[s, g].astype(F32), F32)) for s in range(8)]
        rows = pl.ds(pl.multiple_of(g * 128, 128), 128)
        for j in range(16):
            here = BF(j)
            t = [
                jnp.where(names[s] == here, tiles[g, :, s * 128 : (s + 1) * 128], BF(0))
                for s in range(8)
            ]
            total = ((t[0] + t[1]) + (t[2] + t[3])) + ((t[4] + t[5]) + (t[6] + t[7]))
            a[rows, j * 128 : (j + 1) * 128] = total

    def nth_block(i):
        n = i // 2
        step = (n + 1) // 2
        d = 4 + jnp.where(n % 2 == 1, -step, step)
        return (z + d) % 8 * 2 + i % 2

    def over(which, start, stop):
        def one(i, _):
            which(nth_block(i))
            return 0

        lax.fori_loop(start, stop, one, 0)

    def make(start, stop):
        over(make_block, start, stop)

    def place(start, stop):
        over(place_block, start, stop)

    eye = lax.broadcasted_iota(jnp.int32, (512, 512), 0) == lax.broadcasted_iota(jnp.int32, (512, 512), 1)
    wt[...] = lax.dot_general(
        jnp.where(eye, 1.0, 0.0).astype(BF), w_ref[...], NT, preferred_element_type=F32
    ).astype(BF)
    make(0, 5)
    pl.semaphore_wait(barrier, 30)

    def xg_at(h, o1, o2):
        ox, oy = ((o2, o1), (o1, o2))[h]
        return xg[ox % 4].at[8 * h : 8 * h + 8, (y + oy) % 4]

    def along_x(h, ring):
        return (h + ring) % 2 == 1

    def ag_send(h, ring, lane, j, o1, o2):
        step = (1, -1, 1, -1)[j] if ring == 1 else (1, -1, 2)[j]
        src = xg_at(h, o1, o2)
        if along_x(h, ring):
            dst = xg_at(h, o1 - step, o2) if ring == 0 else xg_at(h, o1, o2 - step)
            dev = at_x(step)
        else:
            dst = src
            dev = at_y(step)
        if ring == 1 and j >= 2:
            rows = slice(0, 16) if j == 2 else slice(16, 32)
            src, dst = src.at[:, rows], dst.at[:, rows]
        send(src, dst, ag_ss.at[h, lane, j], ag_rs.at[h, lane, j], dev)

    def ag_got(h, ring, lane, j):
        if ring == 0:
            step = (1, -1, 2)[j]
            piece = xg_at(h, -step, 0)
        else:
            step = (1, -1, 1, -1)[j]
            piece = xg_at(h, lane - 1, -step if j < 2 else 2)
            if j >= 2:
                piece = piece.at[:, slice(0, 16) if j == 2 else slice(16, 32)]
        dev = at_x(-step) if along_x(h, ring) else at_y(-step)
        got(piece, ag_ss.at[h, lane, j], ag_rs.at[h, lane, j], dev)

    def ag_ring2_own(h, o1):
        for j in (0, 1):
            ag_send(h, 1, 1 + o1, j, o1, 0)

    def ag_ring2_pass(h, o1):
        for j, o in ((0, 3), (1, 1)):
            ag_got(h, 1, 1 + o1, j)
            ag_send(h, 1, 1 + o1, 2 + j, o1, o)

    def ag_ring2_end(h, o1):
        for j in (2, 3):
            ag_got(h, 1, 1 + o1, j)

    for h in (0, 1):
        for j in (0, 1):
            ag_send(h, 0, 0, j, 0, 0)
    for h in (0, 1):
        ag_ring2_own(h, 0)
    for h in (0, 1):
        ag_send(h, 0, 0, 2, 0, 0)

    def cot_copy(i, peer, mine):
        return rc(
            cot_ref.at[:, pl.ds(pl.multiple_of(peer * 128, 128), 128)],
            cotb.at[pl.ds(pl.multiple_of(mine * 32, 32), 32), :],
            cot_ss.at[i], cot_rs.at[i], (r, peer),
        )

    def cot_send(i, _):
        cot_copy(i, (c + i) % 16, c).start()
        return 0

    lax.fori_loop(1, 16, cot_send, 0)
    cotb[pl.ds(pl.multiple_of(c * 32, 32), 32), :] = cot_ref[:, pl.ds(pl.multiple_of(c * 128, 128), 128)]

    make(5, 7)
    for j, o in ((0, 3), (1, 1)):
        for h in (0, 1):
            ag_got(h, 0, 0, j)
            ag_ring2_own(h, o)
    for h in (0, 1):
        ag_got(h, 0, 0, 2)
        ag_ring2_own(h, 2)
    for h in (1, 0):
        ag_ring2_pass(h, 0)
    make(7, 10)
    for o1 in (3, 1):
        for h in (0, 1):
            ag_ring2_pass(h, o1)
    ag_ring2_end(1, 0)

    def block_product(offsets, g):
        picked = []
        for s in range(8):
            col = cols_ref[s, g]
            rows = [xg[o][col].reshape(128, 128) for o in offsets]
            picked.append(rows[0] if len(rows) == 1 else jnp.concatenate(rows, axis=0))
        left = jnp.concatenate(picked, axis=1)
        return lax.dot_general(left, tiles[g], NT, preferred_element_type=F32)

    def product(offsets, *ds):
        for d in ds:
            first = (z + d) % 8 * 2
            value = block_product(offsets, first + 1 - k)
            for i, o in enumerate(offsets):
                psend[o, d] = value[128 * i : 128 * i + 128]
                send(psend.at[o, d], precv.at[o, d], core_ss.at[o, d], core_rs.at[o, d], twin)
            value = block_product(offsets, first + k)
            for i, o in enumerate(offsets):
                pown[o, d] = value[128 * i : 128 * i + 128]

    def twin_got(o, d):
        got(precv.at[o, d], core_ss.at[o, d], core_rs.at[o, d], twin)

    HALVES = (slice(0, 64), slice(64, 128))

    def z_step(offsets, dist):
        for o in offsets:
            for d in (4,) if dist == 4 else (dist, 8 - dist):
                twin_got(o, d)
            for side in (0, 1):
                d = dist if side == 0 else 8 - dist
                sems = (rz_ss.at[side, dist, o], rz_rs.at[side, dist, o])
                before = (rz_ss.at[side, dist + 1, o], rz_rs.at[side, dist + 1, o]) if dist < 4 else None
                came, goes = at_z(-1 if side == 0 else 1), at_z(1 if side == 0 else -1)
                if dist == 4:
                    half = HALVES[side]
                    zs[side, 4, o, half] = (pown[o, d, half] + precv[o, d, half]).astype(BF)
                    send(zs.at[side, 4, o, half], zr.at[side, 3, o, half], *sems, goes)
                    continue
                value = pown[o, d] + precv[o, d]
                if dist == 3:
                    half, other = HALVES[side], HALVES[1 - side]
                    got(zr.at[side, 3, o, half], *before, came)
                    zs[side, 3, o, half] = (value[half] + zr[side, 3, o, half].astype(F32)).astype(BF)
                    zs[side, 3, o, other] = value[other].astype(BF)
                else:
                    got(zr.at[side, dist, o], *before, came)
                    zs[side, dist, o] = (value + zr[side, dist, o].astype(F32)).astype(BF)
                send(zs.at[side, dist, o], zr.at[side, dist - 1, o], *sems, goes)

    def z_last(offsets):
        for o in offsets:
            twin_got(o, 0)
            value = pown[o, 0] + precv[o, 0]
            for side in (0, 1):
                got(zr.at[side, 0, o], rz_ss.at[side, 1, o], rz_rs.at[side, 1, o], at_z(-1 if side == 0 else 1))
                value = value + zr[side, 0, o].astype(F32)
            rows = pl.ds(pl.multiple_of((x + o) % 4 * 128, 128), 128)
            high = value.astype(BF)
            axb[rows] = high
            axl[rows] = (value - high.astype(F32)).astype(BF)

    G0, G1, G2 = (0,), (1, 3), (2,)
    product(G0, 4)
    for h in (0, 1):
        ag_ring2_pass(h, 2)
    make(10, 16)
    product(G0, 3, 5)
    z_step(G0, 4)
    product(G0, 2, 6)
    for o1 in (3, 1):
        ag_ring2_end(1, o1)
    product(G1, 4)
    z_step(G0, 3)
    product(G1, 3, 5)
    z_step(G1, 4)
    for o1 in (0, 3, 1, 2):
        ag_ring2_end(0, o1)
    ag_ring2_end(1, 2)
    product(G2, 4)
    product(G0, 1, 7)
    z_step(G0, 2)
    product(G1, 2, 6)
    z_step(G1, 3)
    product(G2, 3, 5)
    z_step(G2, 4)
    product(G0, 0)
    z_step(G0, 1)
    product(G1, 1, 7)
    z_step(G1, 2)
    product(G2, 2, 6)
    z_step(G2, 3)
    product(G1, 0)
    z_step(G1, 1)
    product(G2, 1, 7)
    z_step(G2, 2)
    product(G2, 0)
    place(0, 4)
    z_step(G2, 1)
    place(4, 10)
    z_last(G0 + G1)
    place(10, 16)
    z_last(G2)

    def cot_wait(i, _):
        cot_copy(i, c, (c + 16 - i) % 16).wait_recv()
        return 0

    lax.fori_loop(1, 16, cot_wait, 0)
    hidden = jnp.dot(wt[...], axb[...], preferred_element_type=F32)
    hidden = hidden + jnp.dot(wt[...], axl[...], preferred_element_type=F32)
    sig = jax.nn.sigmoid(hidden)
    actb[...] = (hidden * sig).astype(BF)
    slope = cotb[...].astype(F32) * sig * (1.0 + hidden * (1.0 - sig))
    slb[...] = slope.astype(BF)
    sll[...] = (slope - slb[...].astype(F32)).astype(BF)
    tg[z, k] = (
        jnp.dot(w_ref[...], slb[...], preferred_element_type=F32)
        + jnp.dot(w_ref[...], sll[...], preferred_element_type=F32)
    ).astype(BF)

    def gz_send(side, dist, j):
        owner = (z - dist + 8) % 8 if side == 0 else (z + dist) % 8
        piece = tg.at[owner, k, pl.ds(j * SUB, SUB)]
        send(piece, piece, gz_ss.at[side, dist, j], gz_rs.at[side, dist, j], at_z(1 if side == 0 else -1))

    def gz_got(side, dist, j):
        owner = (z - dist + 8) % 8 if side == 0 else (z + dist) % 8
        piece = tg.at[owner, k, pl.ds(j * SUB, SUB)]
        got(piece, gz_ss.at[side, dist - 1, j], gz_rs.at[side, dist - 1, j], at_z(-1 if side == 0 else 1))

    def gc_send(d):
        piece = tg.at[(z + d) % 8, k]
        send(piece, piece, gc_ss.at[d], gc_rs.at[d], twin)

    def gc_got(d):
        piece = tg.at[(z + d) % 8, 1 - k]
        got(piece, gc_ss.at[d], gc_rs.at[d], twin)

    for j in range(NS):
        for side in (0, 1):
            gz_send(side, 0, j)
    gc_send(0)

    def act_copy(i, peer, mine):
        return rc(
            actb.at[pl.ds(pl.multiple_of(peer * 32, 32), 32), :],
            act_ref.at[:, pl.ds(pl.multiple_of(mine * 128, 128), 128)],
            act_ss.at[i], act_rs.at[i], (r, peer),
        )

    def act_send(i, _):
        act_copy(i, (c + i) % 16, c).start()
        return 0

    wp[...] = (
        lax.dot_general(axb[...], slb[...], NT, preferred_element_type=F32)
        .astype(BF)
        .reshape(16, 2, 16, 512)
    )
    send(wp.at[:, 1 - k], w0r, w0_ss.at[0], w0_rs.at[0], twin)

    def w1_copy(i, peer, mine):
        return rc(w0s.at[peer], w1r.at[mine], w1_ss.at[i], w1_rs.at[i], (peer, c))

    def w1_send(i, _):
        w1_copy(i, (r + i) % 16, r).start()
        return 0

    def w1_wait(i, _):
        w1_copy(i, r, (r + 16 - i) % 16).wait_recv()
        return 0

    def w2_copy(i, peer, mine):
        return rc(wz.at[mine], wz.at[mine], w2_ss.at[i], w2_rs.at[i], (r, peer * 2 + k))

    def w2_send(i, _):
        w2_copy(i, (z + i) % 8, z).start()
        return 0

    def w2_wait(i, _):
        w2_copy(i, z, (z + 8 - i) % 8).wait_recv()
        return 0

    def w3_copy(i, peer, mine):
        return rc(wg_ref.at[mine, k], wg_ref.at[mine, k], w3_ss.at[i], w3_rs.at[i], (peer, c))

    def w3_send(i, _):
        w3_copy(i, (r + i) % 16, r).start()
        return 0

    def w3_wait(i, _):
        w3_copy(i, r, (r + 16 - i) % 16).wait_recv()
        return 0

    def w_start_row():
        got(w0r, w0_ss.at[0], w0_rs.at[0], twin)
        w0s[...] = (wp[:, k].astype(F32) + w0r[...].astype(F32)).astype(BF)
        lax.fori_loop(1, 16, w1_send, 0)
        w1r[r] = w0s[r]

    def w_start_z():
        lax.fori_loop(1, 16, w1_wait, 0)
        total = w1r[0].astype(F32)
        for i in range(1, 16):
            total = total + w1r[i].astype(F32)
        wz[z] = total.astype(BF)
        lax.fori_loop(1, 8, w2_send, 0)

    def w_start_last():
        lax.fori_loop(1, 8, w2_wait, 0)
        total = wz[0].astype(F32)
        for i in range(1, 8):
            total = total + wz[i].astype(F32)
        wg_ref[r, k] = total.astype(BF)
        lax.fori_loop(1, 16, w3_send, 0)

    def w_finish():
        lax.fori_loop(1, 16, w3_wait, 0)
        send(wg_ref.at[:, k], wg_ref.at[:, k], w0_ss.at[1], w0_rs.at[1], twin)
        got(wg_ref.at[:, 1 - k], w0_ss.at[1], w0_rs.at[1], twin)

    def z_rows(side, dist, j):
        return dist < 4 or (j < NS // 2) == (side == 0)

    def gather_step(dist):
        for j in range(NS):
            for side in (0, 1):
                if not z_rows(side, dist, j):
                    continue
                gz_got(side, dist, j)
                if dist < 4 and z_rows(side, dist + 1, j):
                    gz_send(side, dist, j)
        for d in (4,) if dist == 4 else (dist, 8 - dist):
            gc_send(d)

    def back_part(d):
        block = (z + d) % 8
        left = jnp.concatenate([tg[block, 0], tg[block, 1]], axis=1)
        rows = pl.ds(pl.multiple_of(block * 256, 256), 256)
        return jnp.dot(left, a[rows, :], preferred_element_type=F32)

    gc_got(0)
    acc[...] = back_part(0)
    gather_step(1)
    w_start_row()
    gather_step(2)
    for dist in (1, 2):
        for d in (dist, 8 - dist):
            gc_got(d)
            acc[...] += back_part(d)
        gather_step(dist + 2)
        if dist == 1:
            w_start_z()
    for d in (3, 5):
        gc_got(d)
        acc[...] += back_part(d)
    gc_got(4)

    def last_part(o):
        block = (z + 4) % 8
        feats = pl.ds(pl.multiple_of((x + o) % 4 * 128, 128), 128)
        left = jnp.concatenate([tg[block, 0, feats], tg[block, 1, feats]], axis=1)
        rows = pl.ds(pl.multiple_of(block * 256, 256), 256)
        acc[feats] += jnp.dot(left, a[rows, :], preferred_element_type=F32)

    def q_rows(h, o1, o2):
        if h == 0:
            block = (x + o1) % 4 * 4 + (y + o2) % 4
        else:
            block = (x + o2) % 4 * 4 + (y + o1) % 4
        return block * 32

    def q(h, o1, o2, half):
        start = q_rows(h, o1, o2)
        if half is None:
            return acc[pl.ds(pl.multiple_of(start, 32), 32), h * 1024 : (h + 1) * 1024]
        return acc[pl.ds(pl.multiple_of(start + 16 * half, 16), 16), h * 1024 : (h + 1) * 1024]

    def rx_axis(h, ring):
        return (at_x, at_y)[(h + ring) % 2]

    def rx(src, dst, h, ring, lane, j, start):
        dev = rx_axis(h, ring)(1 if j % 2 == 0 else -1)
        if start:
            send(src, dst, rx_ss.at[h, lane, j], rx_rs.at[h, lane, j], dev)
        else:
            got(dst, rx_ss.at[h, lane, j], rx_rs.at[h, lane, j], dev)

    ORDER = (2, 1, 3, 0)

    def s1_halves(h, o2):
        for j in (0, 1):
            xs1[h, o2, 0, 16 * j : 16 * j + 16] = q(h, 2, o2, j).astype(BF)
            rx(xs1.at[h, o2, 0, 16 * j : 16 * j + 16], xr1h.at[h, o2, j], h, 0, o2, j, True)

    def s1_pass(h, o2, j):
        o = (1, 3)[j]
        rx(None, xr1h.at[h, o2, j], h, 0, o2, j, False)
        xs1[h, o2, 1 + j, 16 * j : 16 * j + 16] = (q(h, o, o2, j) + xr1h[h, o2, j].astype(F32)).astype(BF)
        xs1[h, o2, 1 + j, 16 - 16 * j : 32 - 16 * j] = q(h, o, o2, 1 - j).astype(BF)
        rx(xs1.at[h, o2, 1 + j], xr1f.at[h, o2, j], h, 0, o2, 2 + j, True)

    def s1_final(h, o2):
        for j in (0, 1):
            rx(None, xr1f.at[h, o2, j], h, 0, o2, 2 + j, False)
        s1[h, o2] = q(h, 0, o2, None) + xr1f[h, o2, 0].astype(F32) + xr1f[h, o2, 1].astype(F32)

    def s2_send(h, o2):
        xs2[h, o2 - 1] = s1[h, o2].astype(BF)
        send(xs2.at[h, o2 - 1], xr2.at[h, o2 - 1], rx_ss.at[h, 4, o2], rx_rs.at[h, 4, o2], rx_axis(h, 1)(o2))

    def s2_final(h):
        value = s1[h, 0]
        for o2 in (2, 1, 3):
            got(xr2.at[h, o2 - 1], rx_ss.at[h, 4, o2], rx_rs.at[h, 4, o2], rx_axis(h, 1)(-o2))
            value = value + xr2[h, o2 - 1].astype(F32)
        fg_ref[:, h * 1024 : (h + 1) * 1024] = value.astype(BF)

    last_part(2)
    for o2 in ORDER:
        s1_halves(0, o2)
    s1_halves(1, 2)
    for o in (1, 3, 0):
        last_part(o)
        s1_halves(1, o)
    lax.fori_loop(1, 16, act_send, 0)
    act_ref[:, pl.ds(pl.multiple_of(c * 128, 128), 128)] = actb[pl.ds(pl.multiple_of(c * 32, 32), 32), :]
    for o2 in ORDER:
        for h in (0, 1):
            for j in (0, 1):
                s1_pass(h, o2, j)
    w_start_last()
    for o2 in ORDER:
        for h in (0, 1):
            s1_final(h, o2)
            if o2 > 0:
                s2_send(h, o2)
    for h in (0, 1):
        s2_final(h)
    w_finish()

    def last(i, _):
        act_copy(i, c, (c + 16 - i) % 16).wait_recv()
        act_copy(i, (c + i) % 16, c).wait_send()
        cot_copy(i, (c + i) % 16, c).wait_send()
        w1_copy(i, (r + i) % 16, r).wait_send()
        w3_copy(i, (r + i) % 16, r).wait_send()
        return 0

    lax.fori_loop(1, 16, last, 0)

    def last_z(i, _):
        w2_copy(i, (z + i) % 8, z).wait_send()
        return 0

    lax.fori_loop(1, 8, last_z, 0)
    for copy in sent:
        copy.wait_send()


def layer(cols, counts, src, dst, ew, xt, cot, weight):
    dma = pltpu.SemaphoreType.DMA
    vm = pltpu.VMEM
    vspec = pl.BlockSpec(memory_space=pltpu.VMEM)
    return pl.pallas_call(
        layer_kernel,
        out_shape=(
            jax.ShapeDtypeStruct((32, 2048), BF),
            jax.ShapeDtypeStruct((32, 2048), BF),
            jax.ShapeDtypeStruct((16, 2, 16, 512), BF),
        ),
        in_specs=[pl.BlockSpec(memory_space=pltpu.SMEM)] * 2 + [vspec] * 6,
        out_specs=(vspec,) * 3,
        scratch_shapes=[
            vm((2048, 2048), BF),
            vm((16, 128, 1024), BF),
            vm((16, 4, 32, 128), BF),
            vm((16, 4, 32, 128), BF),
            vm((16, 4, 32, 128), BF),
            vm((16, 4, 32, 128), BF),
            vm((512, 512), BF),
            vm((512, 128), BF),
            vm((4, 8, 128, 128), F32),
            vm((4, 8, 128, 128), F32),
            vm((4, 8, 128, 128), F32),
            vm((2, 4, 4, 128, 128), BF),
            vm((2, 5, 4, 128, 128), BF),
            vm((512, 128), BF),
            vm((512, 128), BF),
            vm((512, 128), BF),
            vm((512, 128), BF),
            vm((512, 128), BF),
            vm((8, 2, 512, 128), BF),
            vm((512, 2048), F32),
            vm((2, 4, 3, 32, 1024), BF),
            vm((2, 4, 2, 16, 1024), BF),
            vm((2, 4, 2, 32, 1024), BF),
            vm((2, 4, 32, 1024), F32),
            vm((2, 3, 32, 1024), BF),
            vm((2, 3, 32, 1024), BF),
            vm((16, 2, 16, 512), BF),
            vm((16, 16, 512), BF),
            vm((16, 16, 512), BF),
            vm((16, 16, 512), BF),
            vm((8, 16, 512), BF),
        ]
        + [dma((16,))] * 2
        + [dma((2, 5, 4))] * 2
        + [dma((4, 8))] * 2
        + [dma((2, 5, 4))] * 2
        + [dma((16,))] * 2
        + [dma((2, 4, NS))] * 2
        + [dma((8,))] * 2
        + [dma((2, 5, 4))] * 2
        + [dma((2,))] * 2
        + [dma((16,))] * 2
        + [dma((8,))] * 2
        + [dma((16,))] * 2,
        compiler_params=pltpu.CompilerParams(
            collective_id=0, has_side_effects=True, vmem_limit_bytes=58 << 20
        ),
        name="layer",
    )(cols, counts, src, dst, ew, xt, cot, weight)


def finish_kernel(act_ref, fg_ref, wg_ref, act_out, fg_out, wg_out, act_in, fg_in, wg_in, sems):
    pairs = ((wg_ref, wg_in), (act_ref, act_in), (fg_ref, fg_in))
    copies = [pltpu.make_async_copy(src, dst, sems.at[i]) for i, (src, dst) in enumerate(pairs)]
    copies += [
        pltpu.make_async_copy(act_in, act_out, sems.at[3]),
        pltpu.make_async_copy(fg_in, fg_out, sems.at[4]),
    ]
    for copy in copies[:3]:
        copy.start()
    for i in (1, 2):
        copies[i].wait()
        copies[i + 2].start()
    copies[0].wait()
    wg_out[...] = wg_in[...].astype(F32)
    copies[3].wait()
    copies[4].wait()


def finish(act, fg, wg):
    anywhere = pl.BlockSpec(memory_space=pl.ANY)
    return pl.pallas_call(
        finish_kernel,
        out_shape=(
            jax.ShapeDtypeStruct((32, 2048), BF),
            jax.ShapeDtypeStruct((32, 2048), BF),
            jax.ShapeDtypeStruct((512, 512), F32),
        ),
        in_specs=[anywhere] * 3,
        out_specs=(anywhere, anywhere, pl.BlockSpec(memory_space=pltpu.VMEM)),
        scratch_shapes=[
            pltpu.VMEM((32, 2048), BF),
            pltpu.VMEM((32, 2048), BF),
            pltpu.VMEM((512, 512), BF),
            pltpu.SemaphoreType.DMA((5,)),
        ],
        compiler_params=pltpu.CompilerParams(vmem_limit_bytes=58 << 20),
        name="finish",
    )(act, fg, wg.reshape(512, 512))


def shards(features, weight, block_cols, block_count, edge_src, edge_dst, edge_weight, cotangent):
    outs = layer(
        block_cols[:, 0, :].T, block_count.T, edge_src[:, 0], edge_dst[:, 0], edge_weight[:, 0],
        features.T, cotangent.T, weight,
    )
    act, fg, wg = finish(*outs)
    return act.T, fg.T, wg


def solution(mesh):
    return jax.shard_map(
        shards,
        mesh=mesh,
        in_specs=(
            P("col", "row"),
            P(),
            P("row", "col", None),
            P("row", "col"),
            P("row", "col", None, None),
            P("row", "col", None, None),
            P("row", "col", None, None),
            P("row", "col"),
        ),
        out_specs=(P("row", "col"), P("col", "row"), P()),
        check_vma=False,
    )
```

```python
import jax
import jax.numpy as jnp
from jax import lax
from jax.experimental import pallas as pl
from jax.experimental.pallas import tpu as pltpu
from jax.sharding import PartitionSpec as P

MESH = pl.DeviceIdType.MESH
BF = jnp.bfloat16
F32 = jnp.float32
NT = (((1,), (1,)), ((), ()))
NS = 4
SUB = 512 // NS


def layer_kernel(
    cols_in, counts_in, src_in, dst_in, ew_in, xt_in, cot_in, w_in,
    act_out, fg_out, wg_out,
    cols_ref, counts_ref, src_ref, dst_ref, ew_ref, xt_ref, cot_ref, w_ref, act_ref, fg_ref, wg_ref,
    a, tiles, xg0, xg1, xg2, xg3, wt, cotb, pown, psend, precv, zr, zs, axb, axl, actb, slb, sll, tg, acc,
    xs1, xr1h, xr1f, s1, xs2, xr2,
    wp, w0r, w0s, w1r, wz,
    in_sem, out_sem,
    cot_ss, cot_rs, ag_ss, ag_rs, core_ss, core_rs, rz_ss, rz_rs,
    act_ss, act_rs, gz_ss, gz_rs, gc_ss, gc_rs, rx_ss, rx_rs,
    w0_ss, w0_rs, w1_ss, w1_rs, w2_ss, w2_rs, w3_ss, w3_rs,
):
    r = lax.axis_index("row")
    c = lax.axis_index("col")
    x, y = r // 4, r % 4
    z, k = c // 2, c % 2

    def at_x(o):
        return ((x + o) % 4 * 4 + y, c)

    def at_y(o):
        return (x * 4 + (y + o) % 4, c)

    def at_z(o):
        return (r, (z + o) % 8 * 2 + k)

    twin = (r, z * 2 + 1 - k)

    def rc(src, dst, ss, rs, dev):
        return pltpu.make_async_remote_copy(
            src_ref=src, dst_ref=dst, send_sem=ss, recv_sem=rs, device_id=dev, device_id_type=MESH
        )

    xg = (xg0, xg1, xg2, xg3)
    sent = []

    def send(src, dst, ss, rs, dev):
        copy = rc(src, dst, ss, rs, dev)
        copy.start()
        sent.append(copy)

    def got(ref, ss, rs, dev):
        rc(ref, ref, ss, rs, dev).wait_recv()

    pairs = (
        (xt_in, xt_ref), (w_in, w_ref), (cols_in, cols_ref), (counts_in, counts_ref),
        (src_in, src_ref), (dst_in, dst_ref), (ew_in, ew_ref), (cot_in, cot_ref),
    )
    loads = [pltpu.make_async_copy(src, dst, in_sem.at[i]) for i, (src, dst) in enumerate(pairs)]
    for load in loads:
        load.start()

    barrier = pltpu.get_barrier_semaphore()

    def greet(i, _):
        pl.semaphore_signal(barrier, inc=1, device_id=((r + i) % 16, c), device_id_type=MESH)
        pl.semaphore_signal(barrier, inc=1, device_id=(r, (c + i) % 16), device_id_type=MESH)
        return 0

    lax.fori_loop(1, 16, greet, 0)
    loads[0].wait()
    for b in range(16):
        xg0[b, y] = xt_ref[:, b * 128 : (b + 1) * 128]

    spots = lax.broadcasted_iota(jnp.int32, (128, 512), 0).astype(F32).astype(BF)
    slots = lax.broadcasted_iota(jnp.int32, (8, 512), 0)

    def spread(row):
        piece = jnp.broadcast_to(row, (16, row.shape[1])).astype(BF)
        return jnp.concatenate([piece] * 8, axis=0)

    def make_block(g):
        src = src_ref[g].astype(F32)
        dst = dst_ref[g].astype(F32)
        wts = jnp.where(slots < counts_ref[0, g], ew_ref[g].astype(F32), 0.0)
        for s in range(8):
            left = jnp.where(spots == spread(dst[s : s + 1]), spread(wts[s : s + 1]), BF(0))
            right = jnp.where(spots == spread(src[s : s + 1]), BF(1), BF(0))
            tile = lax.dot_general(left, right, NT, preferred_element_type=F32)
            tiles[g, :, s * 128 : (s + 1) * 128] = tile.astype(BF)

    def place_block(g):
        names = [spread(jnp.full((1, 128), cols_ref[s, g].astype(F32), F32)) for s in range(8)]
        rows = pl.ds(pl.multiple_of(g * 128, 128), 128)
        for j in range(16):
            here = BF(j)
            t = [
                jnp.where(names[s] == here, tiles[g, :, s * 128 : (s + 1) * 128], BF(0))
                for s in range(8)
            ]
            total = ((t[0] + t[1]) + (t[2] + t[3])) + ((t[4] + t[5]) + (t[6] + t[7]))
            a[rows, j * 128 : (j + 1) * 128] = total

    def nth_block(i):
        n = i // 2
        step = (n + 1) // 2
        d = 4 + jnp.where(n % 2 == 1, -step, step)
        return (z + d) % 8 * 2 + i % 2

    def over(which, start, stop):
        def one(i, _):
            which(nth_block(i))
            return 0

        lax.fori_loop(start, stop, one, 0)

    def make(start, stop):
        over(make_block, start, stop)

    def place(start, stop):
        over(place_block, start, stop)

    loads[1].wait()
    eye = lax.broadcasted_iota(jnp.int32, (512, 512), 0) == lax.broadcasted_iota(jnp.int32, (512, 512), 1)
    wt[...] = lax.dot_general(
        jnp.where(eye, 1.0, 0.0).astype(BF), w_ref[...], NT, preferred_element_type=F32
    ).astype(BF)
    for load in loads[2:]:
        load.wait()
    make(0, 4)
    pl.semaphore_wait(barrier, 30)

    def xg_at(h, o1, o2):
        ox, oy = ((o2, o1), (o1, o2))[h]
        return xg[ox % 4].at[8 * h : 8 * h + 8, (y + oy) % 4]

    def along_x(h, ring):
        return (h + ring) % 2 == 1

    def ag_send(h, ring, lane, j, o1, o2):
        step = (1, -1, 1, -1)[j] if ring == 1 else (1, -1, 2)[j]
        src = xg_at(h, o1, o2)
        if along_x(h, ring):
            dst = xg_at(h, o1 - step, o2) if ring == 0 else xg_at(h, o1, o2 - step)
            dev = at_x(step)
        else:
            dst = src
            dev = at_y(step)
        if ring == 1 and j >= 2:
            rows = slice(0, 16) if j == 2 else slice(16, 32)
            src, dst = src.at[:, rows], dst.at[:, rows]
        send(src, dst, ag_ss.at[h, lane, j], ag_rs.at[h, lane, j], dev)

    def ag_got(h, ring, lane, j):
        if ring == 0:
            step = (1, -1, 2)[j]
            piece = xg_at(h, -step, 0)
        else:
            step = (1, -1, 1, -1)[j]
            piece = xg_at(h, lane - 1, -step if j < 2 else 2)
            if j >= 2:
                piece = piece.at[:, slice(0, 16) if j == 2 else slice(16, 32)]
        dev = at_x(-step) if along_x(h, ring) else at_y(-step)
        got(piece, ag_ss.at[h, lane, j], ag_rs.at[h, lane, j], dev)

    def ag_ring2_own(h, o1):
        for j in (0, 1):
            ag_send(h, 1, 1 + o1, j, o1, 0)

    def ag_ring2_pass(h, o1):
        for j, o in ((0, 3), (1, 1)):
            ag_got(h, 1, 1 + o1, j)
            ag_send(h, 1, 1 + o1, 2 + j, o1, o)

    def ag_ring2_end(h, o1):
        for j in (2, 3):
            ag_got(h, 1, 1 + o1, j)

    for h in (0, 1):
        for j in (0, 1):
            ag_send(h, 0, 0, j, 0, 0)
    for h in (0, 1):
        ag_ring2_own(h, 0)
    for h in (0, 1):
        ag_send(h, 0, 0, 2, 0, 0)

    def cot_copy(i, peer, mine):
        return rc(
            cot_ref.at[:, pl.ds(pl.multiple_of(peer * 128, 128), 128)],
            cotb.at[pl.ds(pl.multiple_of(mine * 32, 32), 32), :],
            cot_ss.at[i], cot_rs.at[i], (r, peer),
        )

    def cot_send(i, _):
        cot_copy(i, (c + i) % 16, c).start()
        return 0

    lax.fori_loop(1, 16, cot_send, 0)
    cotb[pl.ds(pl.multiple_of(c * 32, 32), 32), :] = cot_ref[:, pl.ds(pl.multiple_of(c * 128, 128), 128)]

    make(4, 7)
    for j, o in ((0, 3), (1, 1)):
        for h in (0, 1):
            ag_got(h, 0, 0, j)
            ag_ring2_own(h, o)
    for h in (1, 0):
        ag_ring2_pass(h, 0)
    for h in (0, 1):
        ag_got(h, 0, 0, 2)
        ag_ring2_own(h, 2)
    make(7, 10)
    for o1 in (3, 1):
        for h in (0, 1):
            ag_ring2_pass(h, o1)
    ag_ring2_end(1, 0)

    def block_product(offsets, g):
        picked = []
        for s in range(8):
            col = cols_ref[s, g]
            rows = [xg[o][col].reshape(128, 128) for o in offsets]
            picked.append(rows[0] if len(rows) == 1 else jnp.concatenate(rows, axis=0))
        left = jnp.concatenate(picked, axis=1)
        return lax.dot_general(left, tiles[g], NT, preferred_element_type=F32)

    def product(offsets, *ds):
        for d in ds:
            first = (z + d) % 8 * 2
            value = block_product(offsets, first + 1 - k)
            for i, o in enumerate(offsets):
                psend[o, d] = value[128 * i : 128 * i + 128]
                send(psend.at[o, d], precv.at[o, d], core_ss.at[o, d], core_rs.at[o, d], twin)
            value = block_product(offsets, first + k)
            for i, o in enumerate(offsets):
                pown[o, d] = value[128 * i : 128 * i + 128]

    def twin_got(o, d):
        got(precv.at[o, d], core_ss.at[o, d], core_rs.at[o, d], twin)

    HALVES = (slice(0, 64), slice(64, 128))

    def z_step(offsets, dist):
        for o in offsets:
            for d in (4,) if dist == 4 else (dist, 8 - dist):
                twin_got(o, d)
            for side in (0, 1):
                d = dist if side == 0 else 8 - dist
                sems = (rz_ss.at[side, dist, o], rz_rs.at[side, dist, o])
                before = (rz_ss.at[side, dist + 1, o], rz_rs.at[side, dist + 1, o]) if dist < 4 else None
                came, goes = at_z(-1 if side == 0 else 1), at_z(1 if side == 0 else -1)
                if dist == 4:
                    half = HALVES[side]
                    zs[side, 4, o, half] = (pown[o, d, half] + precv[o, d, half]).astype(BF)
                    send(zs.at[side, 4, o, half], zr.at[side, 3, o, half], *sems, goes)
                    continue
                value = pown[o, d] + precv[o, d]
                if dist == 3:
                    half, other = HALVES[side], HALVES[1 - side]
                    got(zr.at[side, 3, o, half], *before, came)
                    zs[side, 3, o, half] = (value[half] + zr[side, 3, o, half].astype(F32)).astype(BF)
                    zs[side, 3, o, other] = value[other].astype(BF)
                else:
                    got(zr.at[side, dist, o], *before, came)
                    zs[side, dist, o] = (value + zr[side, dist, o].astype(F32)).astype(BF)
                send(zs.at[side, dist, o], zr.at[side, dist - 1, o], *sems, goes)

    def z_last(offsets):
        for o in offsets:
            twin_got(o, 0)
            value = pown[o, 0] + precv[o, 0]
            for side in (0, 1):
                got(zr.at[side, 0, o], rz_ss.at[side, 1, o], rz_rs.at[side, 1, o], at_z(-1 if side == 0 else 1))
                value = value + zr[side, 0, o].astype(F32)
            rows = pl.ds(pl.multiple_of((x + o) % 4 * 128, 128), 128)
            high = value.astype(BF)
            axb[rows] = high
            axl[rows] = (value - high.astype(F32)).astype(BF)

    G0, G1, G2 = (0,), (1, 3), (2,)
    product(G0, 4, 3, 5)
    z_step(G0, 4)
    for h in (0, 1):
        ag_ring2_pass(h, 2)
    make(10, 13)
    for o1 in (3, 1):
        ag_ring2_end(1, o1)
    product(G1, 4)
    z_step(G0, 3)
    product(G1, 3, 5)
    z_step(G1, 4)
    make(13, 16)
    for o1 in (0, 3, 1, 2):
        ag_ring2_end(0, o1)
    ag_ring2_end(1, 2)
    product(G2, 4)
    product(G0, 2, 6)
    z_step(G2, 4)
    z_step(G0, 2)
    product(G1, 2, 6)
    z_step(G1, 3)
    product(G2, 3, 5)
    z_step(G2, 3)
    product(G0, 1, 7)
    z_step(G0, 1)
    product(G1, 1, 7)
    z_step(G1, 2)
    product(G2, 2, 6)
    z_step(G2, 2)
    product(G1, 0)
    z_step(G1, 1)
    product(G2, 1, 7)
    z_step(G2, 1)
    product(G0, 0)
    product(G2, 0)
    place(14, 16)
    z_last(G0 + G1)
    place(10, 14)
    z_last(G2)

    def cot_wait(i, _):
        cot_copy(i, c, (c + 16 - i) % 16).wait_recv()
        return 0

    lax.fori_loop(1, 16, cot_wait, 0)
    hidden = jnp.dot(wt[...], axb[...], preferred_element_type=F32)
    hidden = hidden + jnp.dot(wt[...], axl[...], preferred_element_type=F32)
    sig = jax.nn.sigmoid(hidden)
    actb[...] = (hidden * sig).astype(BF)
    slope = cotb[...].astype(F32) * sig * (1.0 + hidden * (1.0 - sig))
    slb[...] = slope.astype(BF)
    sll[...] = (slope - slb[...].astype(F32)).astype(BF)
    ORDER = (2, 1, 3, 0)

    def gz_piece(side, dist, j):
        owner = (z - dist + 8) % 8 if side == 0 else (z + dist) % 8
        feats = pl.ds(pl.multiple_of((x + ORDER[j]) % 4 * 128, 128), 128)
        return tg.at[owner, k, feats]

    def gz_send(side, dist, j):
        piece = gz_piece(side, dist, j)
        send(piece, piece, gz_ss.at[side, dist, j], gz_rs.at[side, dist, j], at_z(1 if side == 0 else -1))

    def gz_got(side, dist, j):
        piece = gz_piece(side, dist, j)
        got(piece, gz_ss.at[side, dist - 1, j], gz_rs.at[side, dist - 1, j], at_z(-1 if side == 0 else 1))

    def gc_send(d):
        piece = tg.at[(z + d) % 8, k]
        send(piece, piece, gc_ss.at[d], gc_rs.at[d], twin)

    def gc_got(d):
        piece = tg.at[(z + d) % 8, 1 - k]
        got(piece, gc_ss.at[d], gc_rs.at[d], twin)

    for j in range(NS):
        feats = pl.ds(pl.multiple_of((x + ORDER[j]) % 4 * 128, 128), 128)
        tg[z, k, feats] = (
            jnp.dot(w_ref[feats], slb[...], preferred_element_type=F32)
            + jnp.dot(w_ref[feats], sll[...], preferred_element_type=F32)
        ).astype(BF)
        for side in (0, 1):
            gz_send(side, 0, j)
    gc_send(0)

    def act_copy(i, peer, mine):
        return rc(
            actb.at[pl.ds(pl.multiple_of(peer * 32, 32), 32), :],
            act_ref.at[:, pl.ds(pl.multiple_of(mine * 128, 128), 128)],
            act_ss.at[i], act_rs.at[i], (r, peer),
        )

    def act_send(i, _):
        act_copy(i, (c + i) % 16, c).start()
        return 0

    wp[...] = (
        lax.dot_general(axb[...], slb[...], NT, preferred_element_type=F32)
        .astype(BF)
        .reshape(16, 2, 16, 512)
    )
    send(wp.at[:, 1 - k], w0r, w0_ss.at[0], w0_rs.at[0], twin)

    def w1_copy(i, peer, mine):
        return rc(w0s.at[peer], w1r.at[mine], w1_ss.at[i], w1_rs.at[i], (peer, c))

    def w1_send(i, _):
        w1_copy(i, (r + i) % 16, r).start()
        return 0

    def w1_wait(i, _):
        w1_copy(i, r, (r + 16 - i) % 16).wait_recv()
        return 0

    def w2_copy(i, peer, mine):
        return rc(wz.at[mine], wz.at[mine], w2_ss.at[i], w2_rs.at[i], (r, peer * 2 + k))

    def w2_send(i, _):
        w2_copy(i, (z + i) % 8, z).start()
        return 0

    def w2_wait(i, _):
        w2_copy(i, z, (z + 8 - i) % 8).wait_recv()
        return 0

    def w3_copy(i, peer, mine):
        return rc(wg_ref.at[mine, k], wg_ref.at[mine, k], w3_ss.at[i], w3_rs.at[i], (peer, c))

    def w3_send(i, _):
        w3_copy(i, (r + i) % 16, r).start()
        return 0

    def w3_wait(i, _):
        w3_copy(i, r, (r + 16 - i) % 16).wait_recv()
        return 0

    def w_start_row():
        got(w0r, w0_ss.at[0], w0_rs.at[0], twin)
        w0s[...] = (wp[:, k].astype(F32) + w0r[...].astype(F32)).astype(BF)
        lax.fori_loop(1, 16, w1_send, 0)
        w1r[r] = w0s[r]

    def w_start_z():
        lax.fori_loop(1, 16, w1_wait, 0)
        total = w1r[0].astype(F32)
        for i in range(1, 16):
            total = total + w1r[i].astype(F32)
        wz[z] = total.astype(BF)
        lax.fori_loop(1, 8, w2_send, 0)

    def w_start_last():
        lax.fori_loop(1, 8, w2_wait, 0)
        total = wz[0].astype(F32)
        for i in range(1, 8):
            total = total + wz[i].astype(F32)
        wg_ref[r, k] = total.astype(BF)
        lax.fori_loop(1, 16, w3_send, 0)

    def w_finish():
        lax.fori_loop(1, 16, w3_wait, 0)
        send(wg_ref.at[:, k], wg_ref.at[:, k], w0_ss.at[1], w0_rs.at[1], twin)
        got(wg_ref.at[:, 1 - k], w0_ss.at[1], w0_rs.at[1], twin)

    def z_rows(side, dist, j):
        return dist < 4 or (j < NS // 2) == (side == 0)

    def gather_step(dist):
        for j in range(NS):
            for side in (0, 1):
                if not z_rows(side, dist, j):
                    continue
                gz_got(side, dist, j)
                if dist < 4 and z_rows(side, dist + 1, j):
                    gz_send(side, dist, j)
        for d in (4,) if dist == 4 else (dist, 8 - dist):
            gc_send(d)

    def back_part(d):
        block = (z + d) % 8
        left = jnp.concatenate([tg[block, 0], tg[block, 1]], axis=1)
        rows = pl.ds(pl.multiple_of(block * 256, 256), 256)
        return jnp.dot(left, a[rows, :], preferred_element_type=F32)

    gc_got(0)
    acc[...] = back_part(0)
    gather_step(1)
    w_start_row()
    place(6, 10)
    gather_step(2)
    for d in (1, 7):
        gc_got(d)
        acc[...] += back_part(d)
    place(2, 6)
    gather_step(3)
    w_start_z()
    for d in (2, 6):
        gc_got(d)
        acc[...] += back_part(d)
    place(0, 2)
    for d in (3, 5):
        gc_got(d)
        acc[...] += back_part(d)
    gather_step(4)
    gc_got(4)

    def last_part(o):
        block = (z + 4) % 8
        feats = pl.ds(pl.multiple_of((x + o) % 4 * 128, 128), 128)
        left = jnp.concatenate([tg[block, 0, feats], tg[block, 1, feats]], axis=1)
        rows = pl.ds(pl.multiple_of(block * 256, 256), 256)
        acc[feats] += jnp.dot(left, a[rows, :], preferred_element_type=F32)

    def q_rows(h, o1, o2):
        if h == 0:
            block = (x + o1) % 4 * 4 + (y + o2) % 4
        else:
            block = (x + o2) % 4 * 4 + (y + o1) % 4
        return block * 32

    def q(h, o1, o2, half):
        start = q_rows(h, o1, o2)
        if half is None:
            return acc[pl.ds(pl.multiple_of(start, 32), 32), h * 1024 : (h + 1) * 1024]
        return acc[pl.ds(pl.multiple_of(start + 16 * half, 16), 16), h * 1024 : (h + 1) * 1024]

    def rx_axis(h, ring):
        return (at_x, at_y)[(h + ring) % 2]

    def rx(src, dst, h, ring, lane, j, start):
        dev = rx_axis(h, ring)(1 if j % 2 == 0 else -1)
        if start:
            send(src, dst, rx_ss.at[h, lane, j], rx_rs.at[h, lane, j], dev)
        else:
            got(dst, rx_ss.at[h, lane, j], rx_rs.at[h, lane, j], dev)

    def s1_halves(h, o2):
        for j in (0, 1):
            xs1[h, o2, 0, 16 * j : 16 * j + 16] = q(h, 2, o2, j).astype(BF)
            rx(xs1.at[h, o2, 0, 16 * j : 16 * j + 16], xr1h.at[h, o2, j], h, 0, o2, j, True)

    def s1_pass(h, o2, j):
        o = (1, 3)[j]
        rx(None, xr1h.at[h, o2, j], h, 0, o2, j, False)
        xs1[h, o2, 1 + j, 16 * j : 16 * j + 16] = (q(h, o, o2, j) + xr1h[h, o2, j].astype(F32)).astype(BF)
        xs1[h, o2, 1 + j, 16 - 16 * j : 32 - 16 * j] = q(h, o, o2, 1 - j).astype(BF)
        rx(xs1.at[h, o2, 1 + j], xr1f.at[h, o2, j], h, 0, o2, 2 + j, True)

    def s1_final(h, o2):
        for j in (0, 1):
            rx(None, xr1f.at[h, o2, j], h, 0, o2, 2 + j, False)
        s1[h, o2] = q(h, 0, o2, None) + xr1f[h, o2, 0].astype(F32) + xr1f[h, o2, 1].astype(F32)

    def s2_send(h, o2):
        xs2[h, o2 - 1] = s1[h, o2].astype(BF)
        send(xs2.at[h, o2 - 1], xr2.at[h, o2 - 1], rx_ss.at[h, 4, o2], rx_rs.at[h, 4, o2], rx_axis(h, 1)(o2))

    def s2_final(h):
        value = s1[h, 0]
        for o2 in (2, 1, 3):
            got(xr2.at[h, o2 - 1], rx_ss.at[h, 4, o2], rx_rs.at[h, 4, o2], rx_axis(h, 1)(-o2))
            value = value + xr2[h, o2 - 1].astype(F32)
        fg_ref[:, h * 1024 : (h + 1) * 1024] = value.astype(BF)

    last_part(2)
    for o2 in ORDER:
        s1_halves(0, o2)
    s1_halves(1, 2)
    for o in (1, 3, 0):
        last_part(o)
        s1_halves(1, o)
    lax.fori_loop(1, 16, act_send, 0)
    act_ref[:, pl.ds(pl.multiple_of(c * 128, 128), 128)] = actb[pl.ds(pl.multiple_of(c * 32, 32), 32), :]
    for o2 in ORDER:
        for h in (0, 1):
            for j in (0, 1):
                s1_pass(h, o2, j)
        if o2 == 1:
            w_start_last()
    for o2 in ORDER:
        for h in (0, 1):
            s1_final(h, o2)
            if o2 > 0:
                s2_send(h, o2)
    w_finish()
    wg_copy = pltpu.make_async_copy(wg_ref, wg_out, out_sem.at[0])
    wg_copy.start()

    def act_wait(i, _):
        act_copy(i, c, (c + 16 - i) % 16).wait_recv()
        return 0

    lax.fori_loop(1, 16, act_wait, 0)
    act_store = pltpu.make_async_copy(act_ref, act_out, out_sem.at[1])
    act_store.start()
    for h in (0, 1):
        s2_final(h)
    fg_store = pltpu.make_async_copy(fg_ref, fg_out, out_sem.at[2])
    fg_store.start()

    def last(i, _):
        act_copy(i, (c + i) % 16, c).wait_send()
        cot_copy(i, (c + i) % 16, c).wait_send()
        w1_copy(i, (r + i) % 16, r).wait_send()
        w3_copy(i, (r + i) % 16, r).wait_send()
        return 0

    lax.fori_loop(1, 16, last, 0)

    def last_z(i, _):
        w2_copy(i, (z + i) % 8, z).wait_send()
        return 0

    lax.fori_loop(1, 8, last_z, 0)
    for copy in sent:
        copy.wait_send()
    for store in (wg_copy, act_store, fg_store):
        store.wait()


def layer(cols, counts, src, dst, ew, xt, cot, weight):
    dma = pltpu.SemaphoreType.DMA
    vm = pltpu.VMEM
    anywhere = pl.BlockSpec(memory_space=pl.ANY)
    return pl.pallas_call(
        layer_kernel,
        out_shape=(
            jax.ShapeDtypeStruct((32, 2048), BF),
            jax.ShapeDtypeStruct((32, 2048), BF),
            jax.ShapeDtypeStruct((16, 2, 16, 512), BF),
        ),
        in_specs=[anywhere] * 8,
        out_specs=(anywhere,) * 3,
        scratch_shapes=[
            pltpu.SMEM((8, 16), jnp.int32),
            pltpu.SMEM((1, 16), jnp.int32),
            vm((16, 8, 512), jnp.int32),
            vm((16, 8, 512), jnp.int32),
            vm((16, 8, 512), BF),
            vm((32, 2048), BF),
            vm((32, 2048), BF),
            vm((512, 512), BF),
            vm((32, 2048), BF),
            vm((32, 2048), BF),
            vm((16, 2, 16, 512), BF),
            vm((2048, 2048), BF),
            vm((16, 128, 1024), BF),
            vm((16, 4, 32, 128), BF),
            vm((16, 4, 32, 128), BF),
            vm((16, 4, 32, 128), BF),
            vm((16, 4, 32, 128), BF),
            vm((512, 512), BF),
            vm((512, 128), BF),
            vm((4, 8, 128, 128), F32),
            vm((4, 8, 128, 128), F32),
            vm((4, 8, 128, 128), F32),
            vm((2, 4, 4, 128, 128), BF),
            vm((2, 5, 4, 128, 128), BF),
            vm((512, 128), BF),
            vm((512, 128), BF),
            vm((512, 128), BF),
            vm((512, 128), BF),
            vm((512, 128), BF),
            vm((8, 2, 512, 128), BF),
            vm((512, 2048), F32),
            vm((2, 4, 3, 32, 1024), BF),
            vm((2, 4, 2, 16, 1024), BF),
            vm((2, 4, 2, 32, 1024), BF),
            vm((2, 4, 32, 1024), F32),
            vm((2, 3, 32, 1024), BF),
            vm((2, 3, 32, 1024), BF),
            vm((16, 2, 16, 512), BF),
            vm((16, 16, 512), BF),
            vm((16, 16, 512), BF),
            vm((16, 16, 512), BF),
            vm((8, 16, 512), BF),
            dma((8,)),
            dma((3,)),
        ]
        + [dma((16,))] * 2
        + [dma((2, 5, 4))] * 2
        + [dma((4, 8))] * 2
        + [dma((2, 5, 4))] * 2
        + [dma((16,))] * 2
        + [dma((2, 4, NS))] * 2
        + [dma((8,))] * 2
        + [dma((2, 5, 4))] * 2
        + [dma((2,))] * 2
        + [dma((16,))] * 2
        + [dma((8,))] * 2
        + [dma((16,))] * 2,
        compiler_params=pltpu.CompilerParams(
            collective_id=0, has_side_effects=True, vmem_limit_bytes=58 << 20
        ),
        name="layer",
    )(cols, counts, src, dst, ew, xt, cot, weight)


def finish_kernel(act_ref, fg_ref, wg_ref, act_out, fg_out, wg_out, act_in, fg_in, wg_in, sems):
    pairs = ((wg_ref, wg_in), (act_ref, act_in), (fg_ref, fg_in))
    copies = [pltpu.make_async_copy(src, dst, sems.at[i]) for i, (src, dst) in enumerate(pairs)]
    copies += [
        pltpu.make_async_copy(act_in, act_out, sems.at[3]),
        pltpu.make_async_copy(fg_in, fg_out, sems.at[4]),
    ]
    for copy in copies[:3]:
        copy.start()
    for i in (1, 2):
        copies[i].wait()
        copies[i + 2].start()
    copies[0].wait()
    wg_out[...] = wg_in[...].astype(F32)
    copies[3].wait()
    copies[4].wait()


def finish(act, fg, wg):
    anywhere = pl.BlockSpec(memory_space=pl.ANY)
    return pl.pallas_call(
        finish_kernel,
        out_shape=(
            jax.ShapeDtypeStruct((32, 2048), BF),
            jax.ShapeDtypeStruct((32, 2048), BF),
            jax.ShapeDtypeStruct((512, 512), F32),
        ),
        in_specs=[anywhere] * 3,
        out_specs=(anywhere, anywhere, pl.BlockSpec(memory_space=pltpu.VMEM)),
        scratch_shapes=[
            pltpu.VMEM((32, 2048), BF),
            pltpu.VMEM((32, 2048), BF),
            pltpu.VMEM((512, 512), BF),
            pltpu.SemaphoreType.DMA((5,)),
        ],
        compiler_params=pltpu.CompilerParams(vmem_limit_bytes=58 << 20),
        name="finish",
    )(act, fg, wg.reshape(512, 512))


def shards(features, weight, block_cols, block_count, edge_src, edge_dst, edge_weight, cotangent):
    outs = layer(
        block_cols[:, 0, :].T, block_count.T, edge_src[:, 0], edge_dst[:, 0], edge_weight[:, 0],
        features.T, cotangent.T, weight,
    )
    act, fg, wg = finish(*outs)
    return act.T, fg.T, wg


def solution(mesh):
    return jax.shard_map(
        shards,
        mesh=mesh,
        in_specs=(
            P("col", "row"),
            P(),
            P("row", "col", None),
            P("row", "col"),
            P("row", "col", None, None),
            P("row", "col", None, None),
            P("row", "col", None, None),
            P("row", "col"),
        ),
        out_specs=(P("row", "col"), P("col", "row"), P()),
        check_vma=False,
    )
```

```python
import jax
import jax.numpy as jnp
from jax import lax
from jax.experimental import pallas as pl
from jax.experimental.pallas import tpu as pltpu
from jax.sharding import PartitionSpec as P

MESH = pl.DeviceIdType.MESH
BF = jnp.bfloat16
F32 = jnp.float32
NT = (((1,), (1,)), ((), ()))


def layer_kernel(
    cols_in, counts_in, src_in, dst_in, ew_in, xt_in, cot_in, w_in,
    act_out, fg_out, wg_out,
    cols_ref, counts_ref, src_ref, dst_ref, ew_ref, xt_ref, cot_ref, w_ref, act_ref, fg_ref, wg_ref,
    a, tiles, xg0, xg1, xg2, xg3, wt, cotb, pown, psend, precv, zr, zs, zfr, zfs, hid, axb, actb, slb, sll, tg, acc,
    xs1, xr1h, xr1f, s1, xs2, xr2,
    wp, w0r, w0s, w1r, wz,
    in_sem, out_sem,
    cot_ss, cot_rs, ag_ss, ag_rs, core_ss, core_rs, rz_ss, rz_rs, zf_ss, zf_rs,
    act_ss, act_rs, gz_ss, gz_rs, gf_ss, gf_rs, gc_ss, gc_rs, rx_ss, rx_rs,
    w0_ss, w0_rs, w1_ss, w1_rs, w2_ss, w2_rs, w3_ss, w3_rs,
):
    r = lax.axis_index("row")
    c = lax.axis_index("col")
    x, y = r // 4, r % 4
    z, k = c // 2, c % 2

    def at_x(o):
        return ((x + o) % 4 * 4 + y, c)

    def at_y(o):
        return (x * 4 + (y + o) % 4, c)

    def at_z(o):
        return (r, (z + o) % 8 * 2 + k)

    twin = (r, z * 2 + 1 - k)

    def rc(src, dst, ss, rs, dev):
        return pltpu.make_async_remote_copy(
            src_ref=src, dst_ref=dst, send_sem=ss, recv_sem=rs, device_id=dev, device_id_type=MESH
        )

    xg = (xg0, xg1, xg2, xg3)
    sent = []

    def send(src, dst, ss, rs, dev):
        copy = rc(src, dst, ss, rs, dev)
        copy.start()
        sent.append(copy)

    def got(ref, ss, rs, dev):
        rc(ref, ref, ss, rs, dev).wait_recv()

    pairs = (
        (xt_in, xt_ref), (w_in, w_ref), (cols_in, cols_ref), (counts_in, counts_ref),
        (src_in, src_ref), (dst_in, dst_ref), (ew_in, ew_ref), (cot_in, cot_ref),
    )
    loads = [pltpu.make_async_copy(src, dst, in_sem.at[i]) for i, (src, dst) in enumerate(pairs)]
    for load in loads:
        load.start()

    barrier = pltpu.get_barrier_semaphore()

    for i in (8, 7, 9, 6, 10, 5, 11, 4, 12, 3, 13, 2, 14, 1, 15):
        pl.semaphore_signal(barrier, inc=1, device_id=(r, (c + i) % 16), device_id_type=MESH)
        pl.semaphore_signal(barrier, inc=1, device_id=((r + i) % 16, c), device_id_type=MESH)
    loads[0].wait()
    for b in range(16):
        xg0[b, y] = xt_ref[:, b * 128 : (b + 1) * 128]

    spots = lax.broadcasted_iota(jnp.int32, (128, 512), 0).astype(F32).astype(BF)
    slots = lax.broadcasted_iota(jnp.int32, (8, 512), 0)

    def spread(row):
        piece = jnp.broadcast_to(row, (16, row.shape[1])).astype(BF)
        return jnp.concatenate([piece] * 8, axis=0)

    def make_block(g):
        src = src_ref[g].astype(F32)
        dst = dst_ref[g].astype(F32)
        wts = jnp.where(slots < counts_ref[0, g], ew_ref[g].astype(F32), 0.0)
        for s in range(8):
            left = jnp.where(spots == spread(dst[s : s + 1]), spread(wts[s : s + 1]), BF(0))
            right = jnp.where(spots == spread(src[s : s + 1]), BF(1), BF(0))
            tile = lax.dot_general(left, right, NT, preferred_element_type=F32)
            tiles[g, :, s * 128 : (s + 1) * 128] = tile.astype(BF)

    def place_block(g):
        names = [spread(jnp.full((1, 128), cols_ref[s, g].astype(F32), F32)) for s in range(8)]
        rows = pl.ds(pl.multiple_of(g * 128, 128), 128)
        for j in range(16):
            here = BF(j)
            t = [
                jnp.where(names[s] == here, tiles[g, :, s * 128 : (s + 1) * 128], BF(0))
                for s in range(8)
            ]
            total = ((t[0] + t[1]) + (t[2] + t[3])) + ((t[4] + t[5]) + (t[6] + t[7]))
            a[rows, j * 128 : (j + 1) * 128] = total

    def nth_block(i):
        n = i // 2
        step = (n + 1) // 2
        d = 4 + jnp.where(n % 2 == 1, -step, step)
        return (z + d) % 8 * 2 + i % 2

    def over(which, start, stop):
        def one(i, _):
            which(nth_block(i))
            return 0

        lax.fori_loop(start, stop, one, 0)

    def make(start, stop):
        over(make_block, start, stop)

    def place(start, stop):
        over(place_block, start, stop)

    loads[1].wait()
    eye = lax.broadcasted_iota(jnp.int32, (512, 512), 0) == lax.broadcasted_iota(jnp.int32, (512, 512), 1)
    wt[...] = lax.dot_general(
        jnp.where(eye, 1.0, 0.0).astype(BF), w_ref[...], NT, preferred_element_type=F32
    ).astype(BF)
    for load in loads[2:]:
        load.wait()
    make(0, 4)
    pl.semaphore_wait(barrier, 30)

    def xg_at(h, o1, o2):
        ox, oy = ((o2, o1), (o1, o2))[h]
        return xg[ox % 4].at[8 * h : 8 * h + 8, (y + oy) % 4]

    def along_x(h, ring):
        return (h + ring) % 2 == 1

    def ag_send(h, ring, lane, j, o1, o2):
        step = (1, -1, 1, -1)[j] if ring == 1 else (1, -1, 2)[j]
        src = xg_at(h, o1, o2)
        if along_x(h, ring):
            dst = xg_at(h, o1 - step, o2) if ring == 0 else xg_at(h, o1, o2 - step)
            dev = at_x(step)
        else:
            dst = src
            dev = at_y(step)
        if ring == 1 and j >= 2:
            rows = slice(0, 16) if j == 2 else slice(16, 32)
            src, dst = src.at[:, rows], dst.at[:, rows]
        send(src, dst, ag_ss.at[h, lane, j], ag_rs.at[h, lane, j], dev)

    def ag_got(h, ring, lane, j):
        if ring == 0:
            step = (1, -1, 2)[j]
            piece = xg_at(h, -step, 0)
        else:
            step = (1, -1, 1, -1)[j]
            piece = xg_at(h, lane - 1, -step if j < 2 else 2)
            if j >= 2:
                piece = piece.at[:, slice(0, 16) if j == 2 else slice(16, 32)]
        dev = at_x(-step) if along_x(h, ring) else at_y(-step)
        got(piece, ag_ss.at[h, lane, j], ag_rs.at[h, lane, j], dev)

    def ag_ring2_own(h, o1):
        for j in (0, 1):
            ag_send(h, 1, 1 + o1, j, o1, 0)

    def ag_ring2_pass(h, o1):
        for j, o in ((0, 3), (1, 1)):
            ag_got(h, 1, 1 + o1, j)
            ag_send(h, 1, 1 + o1, 2 + j, o1, o)

    def ag_ring2_end(h, o1):
        for j in (2, 3):
            ag_got(h, 1, 1 + o1, j)

    for h in (0, 1):
        for j in (0, 1):
            ag_send(h, 0, 0, j, 0, 0)
    for h in (0, 1):
        ag_ring2_own(h, 0)
    for h in (0, 1):
        ag_send(h, 0, 0, 2, 0, 0)

    def cot_copy(i, peer, mine):
        return rc(
            cot_ref.at[:, pl.ds(pl.multiple_of(peer * 128, 128), 128)],
            cotb.at[pl.ds(pl.multiple_of(mine * 32, 32), 32), :],
            cot_ss.at[i], cot_rs.at[i], (r, peer),
        )

    def cot_send(i, _):
        cot_copy(i, (c + i) % 16, c).start()
        return 0

    lax.fori_loop(1, 16, cot_send, 0)
    cotb[pl.ds(pl.multiple_of(c * 32, 32), 32), :] = cot_ref[:, pl.ds(pl.multiple_of(c * 128, 128), 128)]

    make(4, 7)
    for j, o in ((0, 3), (1, 1)):
        for h in (0, 1):
            ag_got(h, 0, 0, j)
            ag_ring2_own(h, o)
    for h in (1, 0):
        ag_ring2_pass(h, 0)
    for h in (0, 1):
        ag_got(h, 0, 0, 2)
        ag_ring2_own(h, 2)
    make(7, 10)
    for o1 in (3, 1):
        for h in (0, 1):
            ag_ring2_pass(h, o1)
    ag_ring2_end(1, 0)

    def block_product(offsets, g):
        picked = []
        for s in range(8):
            col = cols_ref[s, g]
            rows = [xg[o][col].reshape(128, 128) for o in offsets]
            picked.append(rows[0] if len(rows) == 1 else jnp.concatenate(rows, axis=0))
        left = jnp.concatenate(picked, axis=1)
        return lax.dot_general(left, tiles[g], NT, preferred_element_type=F32)

    def product(offsets, *ds):
        for d in ds:
            first = (z + d) % 8 * 2
            value = block_product(offsets, first + 1 - k)
            for i, o in enumerate(offsets):
                psend[o, d] = value[128 * i : 128 * i + 128]
                send(psend.at[o, d], precv.at[o, d], core_ss.at[o, d], core_rs.at[o, d], twin)
            value = block_product(offsets, first + k)
            for i, o in enumerate(offsets):
                pown[o, d] = value[128 * i : 128 * i + 128]

    def twin_got(o, d):
        got(precv.at[o, d], core_ss.at[o, d], core_rs.at[o, d], twin)

    HALVES = (slice(0, 64), slice(64, 128))

    def z_step(offsets, dist):
        for o in offsets:
            for d in (4,) if dist == 4 else (dist, 8 - dist):
                twin_got(o, d)
            for side in (0, 1):
                d = dist if side == 0 else 8 - dist
                sems = (rz_ss.at[side, dist, o], rz_rs.at[side, dist, o])
                before = (rz_ss.at[side, dist + 1, o], rz_rs.at[side, dist + 1, o]) if dist < 4 else None
                first = dist == 2 and o == 2
                came, goes = at_z(-1 if side == 0 else 1), at_z(1 if side == 0 else -1)
                if dist == 4:
                    half = HALVES[side]
                    zs[side, 4, o, half] = (pown[o, d, half] + precv[o, d, half]).astype(BF)
                    send(zs.at[side, 4, o, half], zr.at[side, 3, o, half], *sems, goes)
                    continue
                value = pown[o, d] + precv[o, d]
                if dist == 3:
                    half, other = HALVES[side], HALVES[1 - side]
                    got(zr.at[side, 3, o, half], *before, came)
                    zs[side, 3, o, half] = (value[half] + zr[side, 3, o, half].astype(F32)).astype(BF)
                    zs[side, 3, o, other] = value[other].astype(BF)
                elif first:
                    zs[side, dist, o] = value.astype(BF)
                else:
                    got(zr.at[side, dist, o], *before, came)
                    zs[side, dist, o] = (value + zr[side, dist, o].astype(F32)).astype(BF)
                send(zs.at[side, dist, o], zr.at[side, dist - 1, o], *sems, goes)

    FAR = (4, 3, 5)

    def z_far():
        for i, d in enumerate(FAR):
            twin_got(2, d)
            zfs[i] = (pown[2, d] + precv[2, d]).astype(BF)
            send(zfs.at[i], zfr.at[i], zf_ss.at[i], zf_rs.at[i], at_z(d))

    def z_last(offsets):
        for o in offsets:
            twin_got(o, 0)
            value = pown[o, 0] + precv[o, 0]
            if o == 2:
                for i, d in enumerate(FAR):
                    got(zfr.at[i], zf_ss.at[i], zf_rs.at[i], at_z(-d))
                    value = value + zfr[i].astype(F32)
            for side in (0, 1):
                got(zr.at[side, 0, o], rz_ss.at[side, 1, o], rz_rs.at[side, 1, o], at_z(-1 if side == 0 else 1))
                value = value + zr[side, 0, o].astype(F32)
            start = pl.multiple_of((x + o) % 4 * 128, 128)
            high = value.astype(BF)
            low = (value - high.astype(F32)).astype(BF)
            axb[pl.ds(start, 128)] = high
            weights = wt[:, pl.ds(start, 128)]
            part = jnp.dot(
                jnp.concatenate([weights, weights], axis=1),
                jnp.concatenate([high, low], axis=0),
                preferred_element_type=F32,
            )
            hid[...] = part if o == 0 else hid[...] + part

    G0, G1, G2 = (0,), (1, 3), (2,)
    product(G0, 4, 3, 5)
    z_step(G0, 4)
    for h in (0, 1):
        ag_ring2_pass(h, 2)
    make(10, 13)
    for o1 in (3, 1):
        ag_ring2_end(1, o1)
    product(G1, 4)
    z_step(G0, 3)
    product(G1, 3, 5)
    z_step(G1, 4)
    make(13, 16)
    for o1 in (0, 3, 1, 2):
        ag_ring2_end(0, o1)
    ag_ring2_end(1, 2)
    product(G2, 4, 3, 5)
    product(G0, 2, 6)
    z_far()
    z_step(G0, 2)
    product(G1, 2, 6)
    z_step(G1, 3)
    product(G2, 2, 6)
    product(G0, 1, 7)
    z_step(G2, 2)
    z_step(G0, 1)
    product(G1, 1, 7)
    z_step(G1, 2)
    product(G2, 1, 7)
    product(G1, 0)
    z_step(G2, 1)
    z_step(G1, 1)
    product(G0, 0)
    product(G2, 0)
    place(13, 16)
    z_last(G0)
    place(10, 13)
    z_last(G1)
    z_last(G2)

    def cot_wait(i, _):
        cot_copy(i, c, (c + 16 - i) % 16).wait_recv()
        return 0

    lax.fori_loop(1, 16, cot_wait, 0)
    hidden = hid[...]
    sig = jax.nn.sigmoid(hidden)
    actb[...] = (hidden * sig).astype(BF)
    slope = cotb[...].astype(F32) * sig * (1.0 + hidden * (1.0 - sig))
    slb[...] = slope.astype(BF)
    sll[...] = (slope - slb[...].astype(F32)).astype(BF)
    ORDER = (2, 1, 3, 0)

    def feats_of(o):
        return pl.ds(pl.multiple_of((x + o) % 4 * 128, 128), 128)

    def gz_piece(d, o, half=None):
        start, size = (x + o) % 4 * 128, 128
        if half is not None:
            start, size = start + 64 * half, 64
        return tg.at[(z + d + 8) % 8, k, pl.ds(pl.multiple_of(start, size), size)]

    def gz_send(side, dist, o):
        piece = gz_piece(-dist if side == 0 else dist, o, side if dist == 3 else None)
        send(piece, piece, gz_ss.at[side, dist, o], gz_rs.at[side, dist, o], at_z(1 if side == 0 else -1))

    def gz_got(side, dist, o):
        piece = gz_piece(-dist if side == 0 else dist, o, side if dist == 4 else None)
        got(piece, gz_ss.at[side, dist - 1, o], gz_rs.at[side, dist - 1, o], at_z(-1 if side == 0 else 1))

    def gc_send(d, o):
        piece = gz_piece(d, o)
        send(piece, piece, gc_ss.at[o, d], gc_rs.at[o, d], twin)

    def gc_got(d, o):
        piece = tg.at[(z + d) % 8, 1 - k, feats_of(o)]
        got(piece, gc_ss.at[o, d], gc_rs.at[o, d], twin)

    def gather(o, dist):
        for side in (0, 1):
            gz_got(side, dist, o)
            if dist < 4 and (o, dist) != (2, 2):
                gz_send(side, dist, o)
        for d in (4,) if dist == 4 else (dist, 8 - dist):
            gc_send(d, o)

    def gather_far():
        for i, d in enumerate(FAR):
            got(gz_piece(-d, 2), gf_ss.at[i], gf_rs.at[i], at_z(-d))
            gc_send(8 - d, 2)

    for o in ORDER:
        feats = feats_of(o)
        tg[z, k, feats] = (
            jnp.dot(w_ref[feats], slb[...], preferred_element_type=F32)
            + jnp.dot(w_ref[feats], sll[...], preferred_element_type=F32)
        ).astype(BF)
        for side in (0, 1):
            gz_send(side, 0, o)
        if o == 2:
            for i, d in enumerate(FAR):
                piece = gz_piece(0, 2)
                send(piece, piece, gf_ss.at[i], gf_rs.at[i], at_z(d))
        gc_send(0, o)

    def act_copy(i, peer, mine):
        return rc(
            actb.at[pl.ds(pl.multiple_of(peer * 32, 32), 32), :],
            act_ref.at[:, pl.ds(pl.multiple_of(mine * 128, 128), 128)],
            act_ss.at[i], act_rs.at[i], (r, peer),
        )

    def act_send(i, _):
        act_copy(i, (c + i) % 16, c).start()
        return 0

    wp[...] = (
        lax.dot_general(axb[...], slb[...], NT, preferred_element_type=F32)
        .astype(BF)
        .reshape(16, 2, 16, 512)
    )
    send(wp.at[:, 1 - k], w0r, w0_ss.at[0], w0_rs.at[0], twin)

    def w1_copy(i, peer, mine):
        return rc(w0s.at[peer], w1r.at[mine], w1_ss.at[i], w1_rs.at[i], (peer, c))

    def w1_send(i, _):
        w1_copy(i, (r + i) % 16, r).start()
        return 0

    def w1_wait(i, _):
        w1_copy(i, r, (r + 16 - i) % 16).wait_recv()
        return 0

    def w2_copy(i, peer, mine):
        return rc(wz.at[mine], wz.at[mine], w2_ss.at[i], w2_rs.at[i], (r, peer * 2 + k))

    def w2_send(i, _):
        w2_copy(i, (z + i) % 8, z).start()
        return 0

    def w2_wait(i, _):
        w2_copy(i, z, (z + 8 - i) % 8).wait_recv()
        return 0

    def w3_copy(i, peer, mine):
        return rc(wg_ref.at[mine, k], wg_ref.at[mine, k], w3_ss.at[i], w3_rs.at[i], (peer, c))

    def w3_send(i, _):
        w3_copy(i, (r + i) % 16, r).start()
        return 0

    def w3_wait(i, _):
        w3_copy(i, r, (r + 16 - i) % 16).wait_recv()
        return 0

    def w_start_row():
        got(w0r, w0_ss.at[0], w0_rs.at[0], twin)
        w0s[...] = (wp[:, k].astype(F32) + w0r[...].astype(F32)).astype(BF)
        lax.fori_loop(1, 16, w1_send, 0)
        w1r[r] = w0s[r]

    def w_start_z():
        lax.fori_loop(1, 16, w1_wait, 0)
        total = w1r[0].astype(F32)
        for i in range(1, 16):
            total = total + w1r[i].astype(F32)
        wz[z] = total.astype(BF)
        lax.fori_loop(1, 8, w2_send, 0)

    def w_start_last():
        lax.fori_loop(1, 8, w2_wait, 0)
        total = wz[0].astype(F32)
        for i in range(1, 8):
            total = total + wz[i].astype(F32)
        wg_ref[r, k] = total.astype(BF)
        lax.fori_loop(1, 16, w3_send, 0)

    def w_finish():
        lax.fori_loop(1, 16, w3_wait, 0)
        send(wg_ref.at[:, k], wg_ref.at[:, k], w0_ss.at[1], w0_rs.at[1], twin)
        got(wg_ref.at[:, 1 - k], w0_ss.at[1], w0_rs.at[1], twin)

    def add_back(o, *ds):
        feats = feats_of(o)
        total = None
        for d in ds:
            gc_got(d, o)
            block = (z + d) % 8
            left = jnp.concatenate([tg[block, 0, feats], tg[block, 1, feats]], axis=1)
            rows = pl.ds(pl.multiple_of(block * 256, 256), 256)
            part = jnp.dot(left, a[rows, :], preferred_element_type=F32)
            total = part if total is None else total + part
        if 0 in ds:
            acc[feats] = total
        else:
            acc[feats] += total

    def q_rows(h, o1, o2):
        if h == 0:
            block = (x + o1) % 4 * 4 + (y + o2) % 4
        else:
            block = (x + o2) % 4 * 4 + (y + o1) % 4
        return block * 32

    def q(h, o1, o2, half):
        start = q_rows(h, o1, o2)
        if half is None:
            return acc[pl.ds(pl.multiple_of(start, 32), 32), h * 1024 : (h + 1) * 1024]
        return acc[pl.ds(pl.multiple_of(start + 16 * half, 16), 16), h * 1024 : (h + 1) * 1024]

    def rx_axis(h, ring):
        return (at_x, at_y)[(h + ring) % 2]

    def rx(src, dst, h, ring, lane, j, start):
        dev = rx_axis(h, ring)(1 if j % 2 == 0 else -1)
        if start:
            send(src, dst, rx_ss.at[h, lane, j], rx_rs.at[h, lane, j], dev)
        else:
            got(dst, rx_ss.at[h, lane, j], rx_rs.at[h, lane, j], dev)

    def s1_halves(h, o2):
        for j in (0, 1):
            xs1[h, o2, 0, 16 * j : 16 * j + 16] = q(h, 2, o2, j).astype(BF)
            rx(xs1.at[h, o2, 0, 16 * j : 16 * j + 16], xr1h.at[h, o2, j], h, 0, o2, j, True)

    def s1_pass(h, o2, j):
        o = (1, 3)[j]
        rx(None, xr1h.at[h, o2, j], h, 0, o2, j, False)
        xs1[h, o2, 1 + j, 16 * j : 16 * j + 16] = (q(h, o, o2, j) + xr1h[h, o2, j].astype(F32)).astype(BF)
        xs1[h, o2, 1 + j, 16 - 16 * j : 32 - 16 * j] = q(h, o, o2, 1 - j).astype(BF)
        rx(xs1.at[h, o2, 1 + j], xr1f.at[h, o2, j], h, 0, o2, 2 + j, True)

    def s1_final(h, o2):
        for j in (0, 1):
            rx(None, xr1f.at[h, o2, j], h, 0, o2, 2 + j, False)
        s1[h, o2] = q(h, 0, o2, None) + xr1f[h, o2, 0].astype(F32) + xr1f[h, o2, 1].astype(F32)

    def s2_send(h, o2):
        xs2[h, o2 - 1] = s1[h, o2].astype(BF)
        send(xs2.at[h, o2 - 1], xr2.at[h, o2 - 1], rx_ss.at[h, 4, o2], rx_rs.at[h, 4, o2], rx_axis(h, 1)(o2))

    def s2_final(h):
        value = s1[h, 0]
        for o2 in (2, 1, 3):
            got(xr2.at[h, o2 - 1], rx_ss.at[h, 4, o2], rx_rs.at[h, 4, o2], rx_axis(h, 1)(-o2))
            value = value + xr2[h, o2 - 1].astype(F32)
        fg_ref[:, h * 1024 : (h + 1) * 1024] = value.astype(BF)

    gather(2, 1)
    add_back(2, 0)
    for o in (1, 3, 0):
        gather(o, 1)
    w_start_row()
    place(6, 10)
    gather(2, 2)
    gather_far()
    add_back(2, 1, 7)
    for o in (1, 3, 0):
        gather(o, 2)
    place(0, 6)
    add_back(2, 2, 6, 3, 5, 4)
    for o2 in ORDER:
        s1_halves(0, o2)
    s1_halves(1, 2)
    for o in (1, 3, 0):
        gather(o, 3)
    w_start_z()
    for o in (1, 3):
        add_back(o, 0, 1, 7, 2, 6)
    for j in (0, 1):
        s1_pass(1, 2, j)
    for o in (1, 3, 0):
        gather(o, 4)
    lax.fori_loop(1, 16, act_send, 0)
    for o, j in ((1, 0), (3, 1)):
        add_back(o, 3, 5, 4)
        s1_halves(1, o)
        for o2 in ORDER:
            s1_pass(0, o2, j)
    s1_final(1, 2)
    s2_send(1, 2)
    add_back(0, 0, 1, 7, 2, 6, 3, 5, 4)
    s1_halves(1, 0)
    act_ref[:, pl.ds(pl.multiple_of(c * 128, 128), 128)] = actb[pl.ds(pl.multiple_of(c * 32, 32), 32), :]
    for o2 in (1, 3):
        for j in (0, 1):
            s1_pass(1, o2, j)
    w_start_last()
    for o2 in ORDER:
        s1_final(0, o2)
        if o2 > 0:
            s2_send(0, o2)
    for j in (0, 1):
        s1_pass(1, 0, j)
    for o2 in (1, 3):
        s1_final(1, o2)
        s2_send(1, o2)
    s1_final(1, 0)
    w_finish()
    wg_copy = pltpu.make_async_copy(wg_ref, wg_out, out_sem.at[0])
    wg_copy.start()

    def act_wait(i, _):
        act_copy(i, c, (c + 16 - i) % 16).wait_recv()
        return 0

    lax.fori_loop(1, 16, act_wait, 0)
    act_store = pltpu.make_async_copy(act_ref, act_out, out_sem.at[1])
    act_store.start()
    for h in (0, 1):
        s2_final(h)
    fg_store = pltpu.make_async_copy(fg_ref, fg_out, out_sem.at[2])
    fg_store.start()

    def last(i, _):
        act_copy(i, (c + i) % 16, c).wait_send()
        cot_copy(i, (c + i) % 16, c).wait_send()
        w1_copy(i, (r + i) % 16, r).wait_send()
        w3_copy(i, (r + i) % 16, r).wait_send()
        return 0

    lax.fori_loop(1, 16, last, 0)

    def last_z(i, _):
        w2_copy(i, (z + i) % 8, z).wait_send()
        return 0

    lax.fori_loop(1, 8, last_z, 0)
    for copy in sent:
        copy.wait_send()
    for store in (wg_copy, act_store, fg_store):
        store.wait()


def layer(cols, counts, src, dst, ew, xt, cot, weight):
    dma = pltpu.SemaphoreType.DMA
    vm = pltpu.VMEM
    anywhere = pl.BlockSpec(memory_space=pl.ANY)
    return pl.pallas_call(
        layer_kernel,
        out_shape=(
            jax.ShapeDtypeStruct((32, 2048), BF),
            jax.ShapeDtypeStruct((32, 2048), BF),
            jax.ShapeDtypeStruct((16, 2, 16, 512), BF),
        ),
        in_specs=[anywhere] * 8,
        out_specs=(anywhere,) * 3,
        scratch_shapes=[
            pltpu.SMEM((8, 16), jnp.int32),
            pltpu.SMEM((1, 16), jnp.int32),
            vm((16, 8, 512), jnp.int32),
            vm((16, 8, 512), jnp.int32),
            vm((16, 8, 512), BF),
            vm((32, 2048), BF),
            vm((32, 2048), BF),
            vm((512, 512), BF),
            vm((32, 2048), BF),
            vm((32, 2048), BF),
            vm((16, 2, 16, 512), BF),
            vm((2048, 2048), BF),
            vm((16, 128, 1024), BF),
            vm((16, 4, 32, 128), BF),
            vm((16, 4, 32, 128), BF),
            vm((16, 4, 32, 128), BF),
            vm((16, 4, 32, 128), BF),
            vm((512, 512), BF),
            vm((512, 128), BF),
            vm((4, 8, 128, 128), F32),
            vm((4, 8, 128, 128), F32),
            vm((4, 8, 128, 128), F32),
            vm((2, 4, 4, 128, 128), BF),
            vm((2, 5, 4, 128, 128), BF),
            vm((3, 128, 128), BF),
            vm((3, 128, 128), BF),
            vm((512, 128), F32),
            vm((512, 128), BF),
            vm((512, 128), BF),
            vm((512, 128), BF),
            vm((512, 128), BF),
            vm((8, 2, 512, 128), BF),
            vm((512, 2048), F32),
            vm((2, 4, 3, 32, 1024), BF),
            vm((2, 4, 2, 16, 1024), BF),
            vm((2, 4, 2, 32, 1024), BF),
            vm((2, 4, 32, 1024), F32),
            vm((2, 3, 32, 1024), BF),
            vm((2, 3, 32, 1024), BF),
            vm((16, 2, 16, 512), BF),
            vm((16, 16, 512), BF),
            vm((16, 16, 512), BF),
            vm((16, 16, 512), BF),
            vm((8, 16, 512), BF),
            dma((8,)),
            dma((3,)),
        ]
        + [dma((16,))] * 2
        + [dma((2, 5, 4))] * 2
        + [dma((4, 8))] * 2
        + [dma((2, 5, 4))] * 2
        + [dma((3,))] * 2
        + [dma((16,))] * 2
        + [dma((2, 4, 4))] * 2
        + [dma((3,))] * 2
        + [dma((4, 8))] * 2
        + [dma((2, 5, 4))] * 2
        + [dma((2,))] * 2
        + [dma((16,))] * 2
        + [dma((8,))] * 2
        + [dma((16,))] * 2,
        compiler_params=pltpu.CompilerParams(
            collective_id=0, has_side_effects=True, vmem_limit_bytes=58 << 20
        ),
        name="layer",
    )(cols, counts, src, dst, ew, xt, cot, weight)


def finish_kernel(act_ref, fg_ref, wg_ref, act_out, fg_out, wg_out, act_in, fg_in, wg_in, sems):
    pairs = ((wg_ref, wg_in), (act_ref, act_in), (fg_ref, fg_in))
    copies = [pltpu.make_async_copy(src, dst, sems.at[i]) for i, (src, dst) in enumerate(pairs)]
    copies += [
        pltpu.make_async_copy(act_in, act_out, sems.at[3]),
        pltpu.make_async_copy(fg_in, fg_out, sems.at[4]),
    ]
    for copy in copies[:3]:
        copy.start()
    for i in (1, 2):
        copies[i].wait()
        copies[i + 2].start()
    copies[0].wait()
    wg_out[...] = wg_in[...].astype(F32)
    copies[3].wait()
    copies[4].wait()


def finish(act, fg, wg):
    anywhere = pl.BlockSpec(memory_space=pl.ANY)
    return pl.pallas_call(
        finish_kernel,
        out_shape=(
            jax.ShapeDtypeStruct((32, 2048), BF),
            jax.ShapeDtypeStruct((32, 2048), BF),
            jax.ShapeDtypeStruct((512, 512), F32),
        ),
        in_specs=[anywhere] * 3,
        out_specs=(anywhere, anywhere, pl.BlockSpec(memory_space=pltpu.VMEM)),
        scratch_shapes=[
            pltpu.VMEM((32, 2048), BF),
            pltpu.VMEM((32, 2048), BF),
            pltpu.VMEM((512, 512), BF),
            pltpu.SemaphoreType.DMA((5,)),
        ],
        compiler_params=pltpu.CompilerParams(vmem_limit_bytes=58 << 20),
        name="finish",
    )(act, fg, wg.reshape(512, 512))


def shards(features, weight, block_cols, block_count, edge_src, edge_dst, edge_weight, cotangent):
    outs = layer(
        block_cols[:, 0, :].T, block_count.T, edge_src[:, 0], edge_dst[:, 0], edge_weight[:, 0],
        features.T, cotangent.T, weight,
    )
    act, fg, wg = finish(*outs)
    return act.T, fg.T, wg


def solution(mesh):
    return jax.shard_map(
        shards,
        mesh=mesh,
        in_specs=(
            P("col", "row"),
            P(),
            P("row", "col", None),
            P("row", "col"),
            P("row", "col", None, None),
            P("row", "col", None, None),
            P("row", "col", None, None),
            P("row", "col"),
        ),
        out_specs=(P("row", "col"), P("col", "row"), P()),
        check_vma=False,
    )
```

```python
import jax
import jax.numpy as jnp
from jax import lax
from jax.experimental import pallas as pl
from jax.experimental.pallas import tpu as pltpu
from jax.sharding import PartitionSpec as P

MESH = pl.DeviceIdType.MESH
BF = jnp.bfloat16
F32 = jnp.float32
NT = (((1,), (1,)), ((), ()))
NS = 4
SUB = 512 // NS


def layer_kernel(
    cols_in, counts_in, src_in, dst_in, ew_in, xt_in, cot_in, w_in,
    act_out, fg_out, wg_out,
    cols_ref, counts_ref, src_ref, dst_ref, ew_ref, xt_ref, cot_ref, w_ref, act_ref, fg_ref, wg_ref,
    a, tiles, xg0, xg1, xg2, xg3, wt, cotb, pown, psend, precv, zr, zs, hid, axb, actb, slb, sll, tg, acc,
    xs1, xr1h, xr1f, s1, xs2, xr2,
    wp, w0r, w0s, w1r, wz,
    in_sem, out_sem,
    cot_ss, cot_rs, ag_ss, ag_rs, core_ss, core_rs, rz_ss, rz_rs,
    act_ss, act_rs, gz_ss, gz_rs, gc_ss, gc_rs, rx_ss, rx_rs,
    w0_ss, w0_rs, w1_ss, w1_rs, w2_ss, w2_rs, w3_ss, w3_rs,
):
    r = lax.axis_index("row")
    c = lax.axis_index("col")
    x, y = r // 4, r % 4
    z, k = c // 2, c % 2

    def at_x(o):
        return ((x + o) % 4 * 4 + y, c)

    def at_y(o):
        return (x * 4 + (y + o) % 4, c)

    def at_z(o):
        return (r, (z + o) % 8 * 2 + k)

    twin = (r, z * 2 + 1 - k)

    def rc(src, dst, ss, rs, dev):
        return pltpu.make_async_remote_copy(
            src_ref=src, dst_ref=dst, send_sem=ss, recv_sem=rs, device_id=dev, device_id_type=MESH
        )

    xg = (xg0, xg1, xg2, xg3)
    sent = []

    def send(src, dst, ss, rs, dev):
        copy = rc(src, dst, ss, rs, dev)
        copy.start()
        sent.append(copy)

    def got(ref, ss, rs, dev):
        rc(ref, ref, ss, rs, dev).wait_recv()

    pairs = (
        (xt_in, xt_ref), (w_in, w_ref), (cols_in, cols_ref), (counts_in, counts_ref),
        (src_in, src_ref), (dst_in, dst_ref), (ew_in, ew_ref), (cot_in, cot_ref),
    )
    loads = [pltpu.make_async_copy(src, dst, in_sem.at[i]) for i, (src, dst) in enumerate(pairs)]
    for load in loads:
        load.start()

    barrier = pltpu.get_barrier_semaphore()

    for i in (8, 7, 9, 6, 10, 5, 11, 4, 12, 3, 13, 2, 14, 1, 15):
        pl.semaphore_signal(barrier, inc=1, device_id=(r, (c + i) % 16), device_id_type=MESH)
        pl.semaphore_signal(barrier, inc=1, device_id=((r + i) % 16, c), device_id_type=MESH)
    loads[0].wait()
    for b in range(16):
        xg0[b, y] = xt_ref[:, b * 128 : (b + 1) * 128]

    spots = lax.broadcasted_iota(jnp.int32, (128, 512), 0).astype(F32).astype(BF)
    slots = lax.broadcasted_iota(jnp.int32, (8, 512), 0)

    def spread(row):
        piece = jnp.broadcast_to(row, (16, row.shape[1])).astype(BF)
        return jnp.concatenate([piece] * 8, axis=0)

    def make_block(g):
        src = src_ref[g].astype(F32)
        dst = dst_ref[g].astype(F32)
        wts = jnp.where(slots < counts_ref[0, g], ew_ref[g].astype(F32), 0.0)
        for s in range(8):
            left = jnp.where(spots == spread(dst[s : s + 1]), spread(wts[s : s + 1]), BF(0))
            right = jnp.where(spots == spread(src[s : s + 1]), BF(1), BF(0))
            tile = lax.dot_general(left, right, NT, preferred_element_type=F32)
            tiles[g, :, s * 128 : (s + 1) * 128] = tile.astype(BF)

    def place_block(g):
        names = [spread(jnp.full((1, 128), cols_ref[s, g].astype(F32), F32)) for s in range(8)]
        rows = pl.ds(pl.multiple_of(g * 128, 128), 128)
        for j in range(16):
            here = BF(j)
            t = [
                jnp.where(names[s] == here, tiles[g, :, s * 128 : (s + 1) * 128], BF(0))
                for s in range(8)
            ]
            total = ((t[0] + t[1]) + (t[2] + t[3])) + ((t[4] + t[5]) + (t[6] + t[7]))
            a[rows, j * 128 : (j + 1) * 128] = total

    def nth_block(i):
        n = i // 2
        step = (n + 1) // 2
        d = 4 + jnp.where(n % 2 == 1, -step, step)
        return (z + d) % 8 * 2 + i % 2

    def over(which, start, stop):
        def one(i, _):
            which(nth_block(i))
            return 0

        lax.fori_loop(start, stop, one, 0)

    def make(start, stop):
        over(make_block, start, stop)

    def place(start, stop):
        over(place_block, start, stop)

    pl.semaphore_wait(barrier, 30)

    def xg_at(h, o1, o2):
        ox, oy = ((o2, o1), (o1, o2))[h]
        return xg[ox % 4].at[8 * h : 8 * h + 8, (y + oy) % 4]

    def along_x(h, ring):
        return (h + ring) % 2 == 1

    def ag_send(h, ring, lane, j, o1, o2):
        step = (1, -1, 1, -1)[j] if ring == 1 else (1, -1, 2)[j]
        src = xg_at(h, o1, o2)
        if along_x(h, ring):
            dst = xg_at(h, o1 - step, o2) if ring == 0 else xg_at(h, o1, o2 - step)
            dev = at_x(step)
        else:
            dst = src
            dev = at_y(step)
        if ring == 1 and j >= 2:
            rows = slice(0, 16) if j == 2 else slice(16, 32)
            src, dst = src.at[:, rows], dst.at[:, rows]
        send(src, dst, ag_ss.at[h, lane, j], ag_rs.at[h, lane, j], dev)

    def ag_got(h, ring, lane, j):
        if ring == 0:
            step = (1, -1, 2)[j]
            piece = xg_at(h, -step, 0)
        else:
            step = (1, -1, 1, -1)[j]
            piece = xg_at(h, lane - 1, -step if j < 2 else 2)
            if j >= 2:
                piece = piece.at[:, slice(0, 16) if j == 2 else slice(16, 32)]
        dev = at_x(-step) if along_x(h, ring) else at_y(-step)
        got(piece, ag_ss.at[h, lane, j], ag_rs.at[h, lane, j], dev)

    def ag_ring2_own(h, o1):
        for j in (0, 1):
            ag_send(h, 1, 1 + o1, j, o1, 0)

    def ag_ring2_pass(h, o1):
        for j, o in ((0, 3), (1, 1)):
            ag_got(h, 1, 1 + o1, j)
            ag_send(h, 1, 1 + o1, 2 + j, o1, o)

    def ag_ring2_end(h, o1):
        for j in (2, 3):
            ag_got(h, 1, 1 + o1, j)

    for h in (0, 1):
        for j in (0, 1):
            ag_send(h, 0, 0, j, 0, 0)
    for h in (0, 1):
        ag_ring2_own(h, 0)
    for h in (0, 1):
        ag_send(h, 0, 0, 2, 0, 0)

    def cot_copy(i, peer, mine):
        return rc(
            cot_ref.at[:, pl.ds(pl.multiple_of(peer * 128, 128), 128)],
            cotb.at[pl.ds(pl.multiple_of(mine * 32, 32), 32), :],
            cot_ss.at[i], cot_rs.at[i], (r, peer),
        )

    def cot_send(i, _):
        cot_copy(i, (c + i) % 16, c).start()
        return 0

    loads[7].wait()
    lax.fori_loop(1, 16, cot_send, 0)
    cotb[pl.ds(pl.multiple_of(c * 32, 32), 32), :] = cot_ref[:, pl.ds(pl.multiple_of(c * 128, 128), 128)]

    loads[1].wait()
    eye = lax.broadcasted_iota(jnp.int32, (512, 512), 0) == lax.broadcasted_iota(jnp.int32, (512, 512), 1)
    wt[...] = lax.dot_general(
        jnp.where(eye, 1.0, 0.0).astype(BF), w_ref[...], NT, preferred_element_type=F32
    ).astype(BF)
    for load in loads[2:7]:
        load.wait()
    make(0, 4)
    for j, o in ((0, 3), (1, 1)):
        for h in (0, 1):
            ag_got(h, 0, 0, j)
            ag_ring2_own(h, o)
    for h in (1, 0):
        ag_ring2_pass(h, 0)
    for h in (0, 1):
        ag_got(h, 0, 0, 2)
        ag_ring2_own(h, 2)
    make(4, 8)
    for o1 in (3, 1):
        for h in (0, 1):
            ag_ring2_pass(h, o1)
    ag_ring2_end(1, 0)

    def block_product(offsets, g):
        picked = []
        for s in range(8):
            col = cols_ref[s, g]
            rows = [xg[o][col].reshape(128, 128) for o in offsets]
            picked.append(rows[0] if len(rows) == 1 else jnp.concatenate(rows, axis=0))
        left = jnp.concatenate(picked, axis=1)
        return lax.dot_general(left, tiles[g], NT, preferred_element_type=F32)

    def product(offsets, *ds):
        for d in ds:
            first = (z + d) % 8 * 2
            value = block_product(offsets, first + 1 - k)
            for i, o in enumerate(offsets):
                psend[o, d] = value[128 * i : 128 * i + 128]
                send(psend.at[o, d], precv.at[o, d], core_ss.at[o, d], core_rs.at[o, d], twin)
            value = block_product(offsets, first + k)
            for i, o in enumerate(offsets):
                pown[o, d] = value[128 * i : 128 * i + 128]

    def twin_got(o, d):
        got(precv.at[o, d], core_ss.at[o, d], core_rs.at[o, d], twin)

    HALVES = (slice(0, 64), slice(64, 128))

    def z_step(offsets, dist):
        for o in offsets:
            for d in (4,) if dist == 4 else (dist, 8 - dist):
                twin_got(o, d)
            for side in (0, 1):
                d = dist if side == 0 else 8 - dist
                sems = (rz_ss.at[side, dist, o], rz_rs.at[side, dist, o])
                before = (rz_ss.at[side, dist + 1, o], rz_rs.at[side, dist + 1, o]) if dist < 4 else None
                came, goes = at_z(-1 if side == 0 else 1), at_z(1 if side == 0 else -1)
                if dist == 4:
                    half = HALVES[side]
                    zs[side, 4, o, half] = (pown[o, d, half] + precv[o, d, half]).astype(BF)
                    send(zs.at[side, 4, o, half], zr.at[side, 3, o, half], *sems, goes)
                    continue
                value = pown[o, d] + precv[o, d]
                if dist == 3:
                    half, other = HALVES[side], HALVES[1 - side]
                    got(zr.at[side, 3, o, half], *before, came)
                    zs[side, 3, o, half] = (value[half] + zr[side, 3, o, half].astype(F32)).astype(BF)
                    zs[side, 3, o, other] = value[other].astype(BF)
                else:
                    got(zr.at[side, dist, o], *before, came)
                    zs[side, dist, o] = (value + zr[side, dist, o].astype(F32)).astype(BF)
                send(zs.at[side, dist, o], zr.at[side, dist - 1, o], *sems, goes)

    def z_last(offsets):
        for o in offsets:
            twin_got(o, 0)
            value = pown[o, 0] + precv[o, 0]
            for side in (0, 1):
                got(zr.at[side, 0, o], rz_ss.at[side, 1, o], rz_rs.at[side, 1, o], at_z(-1 if side == 0 else 1))
                value = value + zr[side, 0, o].astype(F32)
            start = pl.multiple_of((x + o) % 4 * 128, 128)
            high = value.astype(BF)
            low = (value - high.astype(F32)).astype(BF)
            axb[pl.ds(start, 128)] = high
            weights = wt[:, pl.ds(start, 128)]
            part = jnp.dot(
                jnp.concatenate([weights, weights], axis=1),
                jnp.concatenate([high, low], axis=0),
                preferred_element_type=F32,
            )
            hid[...] = part if o == 0 else hid[...] + part

    G0, G1, G2 = (0,), (1, 3), (2,)
    product(G0, 4, 3, 5)
    z_step(G0, 4)
    for h in (0, 1):
        ag_ring2_pass(h, 2)
    make(8, 13)
    for o1 in (3, 1):
        ag_ring2_end(1, o1)
    product(G1, 4)
    z_step(G0, 3)
    product(G1, 3, 5)
    z_step(G1, 4)
    make(13, 16)
    product(G0, 2, 6)
    for o1 in (0, 3, 1, 2):
        ag_ring2_end(0, o1)
    ag_ring2_end(1, 2)
    product(G2, 4)
    z_step(G0, 2)
    z_step(G2, 4)
    product(G1, 2, 6)
    z_step(G1, 3)
    product(G2, 3, 5)
    z_step(G2, 3)
    product(G0, 1, 7)
    z_step(G0, 1)
    product(G1, 1, 7)
    z_step(G1, 2)
    product(G2, 2, 6)
    z_step(G2, 2)
    product(G1, 0)
    z_step(G1, 1)
    product(G2, 1, 7)
    z_step(G2, 1)
    product(G0, 0)
    product(G2, 0)
    place(14, 16)
    z_last(G0 + G1)
    place(10, 14)
    z_last(G2)

    def cot_wait(i, _):
        cot_copy(i, c, (c + 16 - i) % 16).wait_recv()
        return 0

    lax.fori_loop(1, 16, cot_wait, 0)
    hidden = hid[...]
    sig = jax.nn.sigmoid(hidden)
    actb[...] = (hidden * sig).astype(BF)
    slope = cotb[...].astype(F32) * sig * (1.0 + hidden * (1.0 - sig))
    slb[...] = slope.astype(BF)
    sll[...] = (slope - slb[...].astype(F32)).astype(BF)
    ORDER = (2, 1, 3, 0)

    def gz_piece(side, dist, j):
        owner = (z - dist + 8) % 8 if side == 0 else (z + dist) % 8
        feats = pl.ds(pl.multiple_of((x + ORDER[j]) % 4 * 128, 128), 128)
        return tg.at[owner, k, feats]

    def gz_send(side, dist, j):
        piece = gz_piece(side, dist, j)
        send(piece, piece, gz_ss.at[side, dist, j], gz_rs.at[side, dist, j], at_z(1 if side == 0 else -1))

    def gz_got(side, dist, j):
        piece = gz_piece(side, dist, j)
        got(piece, gz_ss.at[side, dist - 1, j], gz_rs.at[side, dist - 1, j], at_z(-1 if side == 0 else 1))

    def gc_send(d):
        piece = tg.at[(z + d) % 8, k]
        send(piece, piece, gc_ss.at[d], gc_rs.at[d], twin)

    def gc_got(d):
        piece = tg.at[(z + d) % 8, 1 - k]
        got(piece, gc_ss.at[d], gc_rs.at[d], twin)

    for j in range(NS):
        feats = pl.ds(pl.multiple_of((x + ORDER[j]) % 4 * 128, 128), 128)
        tg[z, k, feats] = (
            jnp.dot(w_ref[feats], slb[...], preferred_element_type=F32)
            + jnp.dot(w_ref[feats], sll[...], preferred_element_type=F32)
        ).astype(BF)
        for side in (0, 1):
            gz_send(side, 0, j)
    gc_send(0)

    def act_copy(i, peer, mine):
        return rc(
            actb.at[pl.ds(pl.multiple_of(peer * 32, 32), 32), :],
            act_ref.at[:, pl.ds(pl.multiple_of(mine * 128, 128), 128)],
            act_ss.at[i], act_rs.at[i], (r, peer),
        )

    def act_send(i, _):
        act_copy(i, (c + i) % 16, c).start()
        return 0

    wp[...] = (
        lax.dot_general(axb[...], slb[...], NT, preferred_element_type=F32)
        .astype(BF)
        .reshape(16, 2, 16, 512)
    )
    send(wp.at[:, 1 - k], w0r, w0_ss.at[0], w0_rs.at[0], twin)

    def w1_copy(i, peer, mine):
        return rc(w0s.at[peer], w1r.at[mine], w1_ss.at[i], w1_rs.at[i], (peer, c))

    def w1_send(i, _):
        w1_copy(i, (r + i) % 16, r).start()
        return 0

    def w1_wait(i, _):
        w1_copy(i, r, (r + 16 - i) % 16).wait_recv()
        return 0

    def w2_copy(i, peer, mine):
        return rc(wz.at[mine], wz.at[mine], w2_ss.at[i], w2_rs.at[i], (r, peer * 2 + k))

    def w2_send(i, _):
        w2_copy(i, (z + i) % 8, z).start()
        return 0

    def w2_wait(i, _):
        w2_copy(i, z, (z + 8 - i) % 8).wait_recv()
        return 0

    def w3_copy(i, peer, mine):
        return rc(wg_ref.at[mine, k], wg_ref.at[mine, k], w3_ss.at[i], w3_rs.at[i], (peer, c))

    def w3_send(i, _):
        w3_copy(i, (r + i) % 16, r).start()
        return 0

    def w3_wait(i, _):
        w3_copy(i, r, (r + 16 - i) % 16).wait_recv()
        return 0

    def w_start_row():
        got(w0r, w0_ss.at[0], w0_rs.at[0], twin)
        w0s[...] = (wp[:, k].astype(F32) + w0r[...].astype(F32)).astype(BF)
        lax.fori_loop(1, 16, w1_send, 0)
        w1r[r] = w0s[r]

    def w_start_z():
        lax.fori_loop(1, 16, w1_wait, 0)
        total = w1r[0].astype(F32)
        for i in range(1, 16):
            total = total + w1r[i].astype(F32)
        wz[z] = total.astype(BF)
        lax.fori_loop(1, 8, w2_send, 0)

    def w_start_last():
        lax.fori_loop(1, 8, w2_wait, 0)
        total = wz[0].astype(F32)
        for i in range(1, 8):
            total = total + wz[i].astype(F32)
        wg_ref[r, k] = total.astype(BF)
        lax.fori_loop(1, 16, w3_send, 0)

    def w_finish():
        lax.fori_loop(1, 16, w3_wait, 0)
        send(wg_ref.at[:, k], wg_ref.at[:, k], w0_ss.at[1], w0_rs.at[1], twin)
        got(wg_ref.at[:, 1 - k], w0_ss.at[1], w0_rs.at[1], twin)

    def z_rows(side, dist, j):
        return dist < 4 or (j < NS // 2) == (side == 0)

    def gather_step(dist):
        for j in range(NS):
            for side in (0, 1):
                if not z_rows(side, dist, j):
                    continue
                gz_got(side, dist, j)
                if dist < 4 and z_rows(side, dist + 1, j):
                    gz_send(side, dist, j)
        for d in (4,) if dist == 4 else (dist, 8 - dist):
            gc_send(d)

    def back_part(d):
        block = (z + d) % 8
        left = jnp.concatenate([tg[block, 0], tg[block, 1]], axis=1)
        rows = pl.ds(pl.multiple_of(block * 256, 256), 256)
        return jnp.dot(left, a[rows, :], preferred_element_type=F32)

    gc_got(0)
    acc[...] = back_part(0)
    gather_step(1)
    w_start_row()
    place(6, 10)
    gather_step(2)
    for d in (1, 7):
        gc_got(d)
        acc[...] += back_part(d)
    place(2, 6)
    gather_step(3)
    w_start_z()
    for d in (2, 6):
        gc_got(d)
        acc[...] += back_part(d)
    place(0, 2)
    for d in (3, 5):
        gc_got(d)
        acc[...] += back_part(d)
    gather_step(4)
    gc_got(4)

    def last_part(o):
        block = (z + 4) % 8
        feats = pl.ds(pl.multiple_of((x + o) % 4 * 128, 128), 128)
        left = jnp.concatenate([tg[block, 0, feats], tg[block, 1, feats]], axis=1)
        rows = pl.ds(pl.multiple_of(block * 256, 256), 256)
        acc[feats] += jnp.dot(left, a[rows, :], preferred_element_type=F32)

    def q_rows(h, o1, o2):
        if h == 0:
            block = (x + o1) % 4 * 4 + (y + o2) % 4
        else:
            block = (x + o2) % 4 * 4 + (y + o1) % 4
        return block * 32

    def q(h, o1, o2, half):
        start = q_rows(h, o1, o2)
        if half is None:
            return acc[pl.ds(pl.multiple_of(start, 32), 32), h * 1024 : (h + 1) * 1024]
        return acc[pl.ds(pl.multiple_of(start + 16 * half, 16), 16), h * 1024 : (h + 1) * 1024]

    def rx_axis(h, ring):
        return (at_x, at_y)[(h + ring) % 2]

    def rx(src, dst, h, ring, lane, j, start):
        dev = rx_axis(h, ring)(1 if j % 2 == 0 else -1)
        if start:
            send(src, dst, rx_ss.at[h, lane, j], rx_rs.at[h, lane, j], dev)
        else:
            got(dst, rx_ss.at[h, lane, j], rx_rs.at[h, lane, j], dev)

    def s1_halves(h, o2):
        for j in (0, 1):
            xs1[h, o2, 0, 16 * j : 16 * j + 16] = q(h, 2, o2, j).astype(BF)
            rx(xs1.at[h, o2, 0, 16 * j : 16 * j + 16], xr1h.at[h, o2, j], h, 0, o2, j, True)

    def s1_pass(h, o2, j):
        o = (1, 3)[j]
        rx(None, xr1h.at[h, o2, j], h, 0, o2, j, False)
        xs1[h, o2, 1 + j, 16 * j : 16 * j + 16] = (q(h, o, o2, j) + xr1h[h, o2, j].astype(F32)).astype(BF)
        xs1[h, o2, 1 + j, 16 - 16 * j : 32 - 16 * j] = q(h, o, o2, 1 - j).astype(BF)
        rx(xs1.at[h, o2, 1 + j], xr1f.at[h, o2, j], h, 0, o2, 2 + j, True)

    def s1_final(h, o2):
        for j in (0, 1):
            rx(None, xr1f.at[h, o2, j], h, 0, o2, 2 + j, False)
        s1[h, o2] = q(h, 0, o2, None) + xr1f[h, o2, 0].astype(F32) + xr1f[h, o2, 1].astype(F32)

    def s2_send(h, o2):
        xs2[h, o2 - 1] = s1[h, o2].astype(BF)
        send(xs2.at[h, o2 - 1], xr2.at[h, o2 - 1], rx_ss.at[h, 4, o2], rx_rs.at[h, 4, o2], rx_axis(h, 1)(o2))

    def s2_final(h):
        value = s1[h, 0]
        for o2 in (2, 1, 3):
            got(xr2.at[h, o2 - 1], rx_ss.at[h, 4, o2], rx_rs.at[h, 4, o2], rx_axis(h, 1)(-o2))
            value = value + xr2[h, o2 - 1].astype(F32)
        fg_ref[:, h * 1024 : (h + 1) * 1024] = value.astype(BF)

    last_part(2)
    for o2 in ORDER:
        s1_halves(0, o2)
    s1_halves(1, 2)
    for o in (1, 3, 0):
        last_part(o)
        s1_halves(1, o)
    lax.fori_loop(1, 16, act_send, 0)
    act_ref[:, pl.ds(pl.multiple_of(c * 128, 128), 128)] = actb[pl.ds(pl.multiple_of(c * 32, 32), 32), :]
    for o2 in ORDER:
        for h in (0, 1):
            for j in (0, 1):
                s1_pass(h, o2, j)
        if o2 == 1:
            w_start_last()
    for o2 in ORDER:
        for h in (0, 1):
            s1_final(h, o2)
            if o2 > 0:
                s2_send(h, o2)
    w_finish()
    wg_copy = pltpu.make_async_copy(wg_ref, wg_out, out_sem.at[0])
    wg_copy.start()

    def act_wait(i, _):
        act_copy(i, c, (c + 16 - i) % 16).wait_recv()
        return 0

    lax.fori_loop(1, 16, act_wait, 0)
    act_store = pltpu.make_async_copy(act_ref, act_out, out_sem.at[1])
    act_store.start()
    for h in (0, 1):
        s2_final(h)
    fg_store = pltpu.make_async_copy(fg_ref, fg_out, out_sem.at[2])
    fg_store.start()

    def last(i, _):
        act_copy(i, (c + i) % 16, c).wait_send()
        cot_copy(i, (c + i) % 16, c).wait_send()
        w1_copy(i, (r + i) % 16, r).wait_send()
        w3_copy(i, (r + i) % 16, r).wait_send()
        return 0

    lax.fori_loop(1, 16, last, 0)

    def last_z(i, _):
        w2_copy(i, (z + i) % 8, z).wait_send()
        return 0

    lax.fori_loop(1, 8, last_z, 0)
    for copy in sent:
        copy.wait_send()
    for store in (wg_copy, act_store, fg_store):
        store.wait()


def layer(cols, counts, src, dst, ew, xt, cot, weight):
    dma = pltpu.SemaphoreType.DMA
    vm = pltpu.VMEM
    anywhere = pl.BlockSpec(memory_space=pl.ANY)
    return pl.pallas_call(
        layer_kernel,
        out_shape=(
            jax.ShapeDtypeStruct((32, 2048), BF),
            jax.ShapeDtypeStruct((32, 2048), BF),
            jax.ShapeDtypeStruct((16, 2, 16, 512), BF),
        ),
        in_specs=[anywhere] * 8,
        out_specs=(anywhere,) * 3,
        scratch_shapes=[
            pltpu.SMEM((8, 16), jnp.int32),
            pltpu.SMEM((1, 16), jnp.int32),
            vm((16, 8, 512), jnp.int32),
            vm((16, 8, 512), jnp.int32),
            vm((16, 8, 512), BF),
            vm((32, 2048), BF),
            vm((32, 2048), BF),
            vm((512, 512), BF),
            vm((32, 2048), BF),
            vm((32, 2048), BF),
            vm((16, 2, 16, 512), BF),
            vm((2048, 2048), BF),
            vm((16, 128, 1024), BF),
            vm((16, 4, 32, 128), BF),
            vm((16, 4, 32, 128), BF),
            vm((16, 4, 32, 128), BF),
            vm((16, 4, 32, 128), BF),
            vm((512, 512), BF),
            vm((512, 128), BF),
            vm((4, 8, 128, 128), F32),
            vm((4, 8, 128, 128), F32),
            vm((4, 8, 128, 128), F32),
            vm((2, 4, 4, 128, 128), BF),
            vm((2, 5, 4, 128, 128), BF),
            vm((512, 128), F32),
            vm((512, 128), BF),
            vm((512, 128), BF),
            vm((512, 128), BF),
            vm((512, 128), BF),
            vm((8, 2, 512, 128), BF),
            vm((512, 2048), F32),
            vm((2, 4, 3, 32, 1024), BF),
            vm((2, 4, 2, 16, 1024), BF),
            vm((2, 4, 2, 32, 1024), BF),
            vm((2, 4, 32, 1024), F32),
            vm((2, 3, 32, 1024), BF),
            vm((2, 3, 32, 1024), BF),
            vm((16, 2, 16, 512), BF),
            vm((16, 16, 512), BF),
            vm((16, 16, 512), BF),
            vm((16, 16, 512), BF),
            vm((8, 16, 512), BF),
            dma((8,)),
            dma((3,)),
        ]
        + [dma((16,))] * 2
        + [dma((2, 5, 4))] * 2
        + [dma((4, 8))] * 2
        + [dma((2, 5, 4))] * 2
        + [dma((16,))] * 2
        + [dma((2, 4, NS))] * 2
        + [dma((8,))] * 2
        + [dma((2, 5, 4))] * 2
        + [dma((2,))] * 2
        + [dma((16,))] * 2
        + [dma((8,))] * 2
        + [dma((16,))] * 2,
        compiler_params=pltpu.CompilerParams(
            collective_id=0, has_side_effects=True, vmem_limit_bytes=58 << 20
        ),
        name="layer",
    )(cols, counts, src, dst, ew, xt, cot, weight)


def finish_kernel(act_ref, fg_ref, wg_ref, act_out, fg_out, wg_out, act_in, fg_in, wg_in, sems):
    pairs = ((wg_ref, wg_in), (act_ref, act_in), (fg_ref, fg_in))
    copies = [pltpu.make_async_copy(src, dst, sems.at[i]) for i, (src, dst) in enumerate(pairs)]
    copies += [
        pltpu.make_async_copy(act_in, act_out, sems.at[3]),
        pltpu.make_async_copy(fg_in, fg_out, sems.at[4]),
    ]
    for copy in copies[:3]:
        copy.start()
    for i in (1, 2):
        copies[i].wait()
        copies[i + 2].start()
    copies[0].wait()
    wg_out[...] = wg_in[...].astype(F32)
    copies[3].wait()
    copies[4].wait()


def finish(act, fg, wg):
    anywhere = pl.BlockSpec(memory_space=pl.ANY)
    return pl.pallas_call(
        finish_kernel,
        out_shape=(
            jax.ShapeDtypeStruct((32, 2048), BF),
            jax.ShapeDtypeStruct((32, 2048), BF),
            jax.ShapeDtypeStruct((512, 512), F32),
        ),
        in_specs=[anywhere] * 3,
        out_specs=(anywhere, anywhere, pl.BlockSpec(memory_space=pltpu.VMEM)),
        scratch_shapes=[
            pltpu.VMEM((32, 2048), BF),
            pltpu.VMEM((32, 2048), BF),
            pltpu.VMEM((512, 512), BF),
            pltpu.SemaphoreType.DMA((5,)),
        ],
        compiler_params=pltpu.CompilerParams(vmem_limit_bytes=58 << 20),
        name="finish",
    )(act, fg, wg.reshape(512, 512))


def shards(features, weight, block_cols, block_count, edge_src, edge_dst, edge_weight, cotangent):
    outs = layer(
        block_cols[:, 0, :].T, block_count.T, edge_src[:, 0], edge_dst[:, 0], edge_weight[:, 0],
        features.T, cotangent.T, weight,
    )
    act, fg, wg = finish(*outs)
    return act.T, fg.T, wg


def solution(mesh):
    return jax.shard_map(
        shards,
        mesh=mesh,
        in_specs=(
            P("col", "row"),
            P(),
            P("row", "col", None),
            P("row", "col"),
            P("row", "col", None, None),
            P("row", "col", None, None),
            P("row", "col", None, None),
            P("row", "col"),
        ),
        out_specs=(P("row", "col"), P("col", "row"), P()),
        check_vma=False,
    )
```

```python
import jax
import jax.numpy as jnp
from jax import lax
from jax.experimental import pallas as pl
from jax.experimental.pallas import tpu as pltpu
from jax.sharding import PartitionSpec as P

MESH = pl.DeviceIdType.MESH
BF = jnp.bfloat16
F32 = jnp.float32
NT = (((1,), (1,)), ((), ()))
NS = 4
SUB = 512 // NS


def layer_kernel(
    cols_in, counts_in, src_in, dst_in, ew_in, xt_in, cot_in, w_in,
    act_out, fg_out, wg_out,
    cols_ref, counts_ref, src_ref, dst_ref, ew_ref, xt_ref, cot_ref, w_ref, act_ref, fg_ref, wg_ref,
    a, tiles, xg0, xg1, xg2, xg3, wt, cotb, pown, psend, precv, zr, zs, hid, axb, actb, slb, sll, tg, acc,
    xs1, xr1h, xr1f, s1, xs2, xr2,
    wp, w0r, w0s, w1r, wz,
    in_sem, out_sem,
    cot_ss, cot_rs, ag_ss, ag_rs, core_ss, core_rs, rz_ss, rz_rs,
    act_ss, act_rs, gz_ss, gz_rs, gc_ss, gc_rs, rx_ss, rx_rs,
    w0_ss, w0_rs, w1_ss, w1_rs, w2_ss, w2_rs, w3_ss, w3_rs,
):
    r = lax.axis_index("row")
    c = lax.axis_index("col")
    x, y = r // 4, r % 4
    z, k = c // 2, c % 2

    def at_x(o):
        return ((x + o) % 4 * 4 + y, c)

    def at_y(o):
        return (x * 4 + (y + o) % 4, c)

    def at_z(o):
        return (r, (z + o) % 8 * 2 + k)

    twin = (r, z * 2 + 1 - k)

    def rc(src, dst, ss, rs, dev):
        return pltpu.make_async_remote_copy(
            src_ref=src, dst_ref=dst, send_sem=ss, recv_sem=rs, device_id=dev, device_id_type=MESH
        )

    xg = (xg0, xg1, xg2, xg3)
    sent = []

    def send(src, dst, ss, rs, dev):
        copy = rc(src, dst, ss, rs, dev)
        copy.start()
        sent.append(copy)

    def got(ref, ss, rs, dev):
        rc(ref, ref, ss, rs, dev).wait_recv()

    pairs = (
        (xt_in, xt_ref), (w_in, w_ref), (cols_in, cols_ref), (counts_in, counts_ref),
        (src_in, src_ref), (dst_in, dst_ref), (ew_in, ew_ref), (cot_in, cot_ref),
    )
    loads = [pltpu.make_async_copy(src, dst, in_sem.at[i]) for i, (src, dst) in enumerate(pairs)]
    for load in loads:
        load.start()

    barrier = pltpu.get_barrier_semaphore()

    for i in (8, 7, 9, 6, 10, 5, 11, 4, 12, 3, 13, 2, 14, 1, 15):
        pl.semaphore_signal(barrier, inc=1, device_id=(r, (c + i) % 16), device_id_type=MESH)
        pl.semaphore_signal(barrier, inc=1, device_id=((r + i) % 16, c), device_id_type=MESH)
    loads[0].wait()
    for b in range(16):
        xg0[b, y] = xt_ref[:, b * 128 : (b + 1) * 128]

    spots = lax.broadcasted_iota(jnp.int32, (128, 512), 0).astype(F32).astype(BF)
    slots = lax.broadcasted_iota(jnp.int32, (8, 512), 0)

    def spread(row):
        piece = jnp.broadcast_to(row, (16, row.shape[1])).astype(BF)
        return jnp.concatenate([piece] * 8, axis=0)

    def make_block(g):
        src = src_ref[g].astype(F32)
        dst = dst_ref[g].astype(F32)
        wts = jnp.where(slots < counts_ref[0, g], ew_ref[g].astype(F32), 0.0)
        for s in range(8):
            left = jnp.where(spots == spread(dst[s : s + 1]), spread(wts[s : s + 1]), BF(0))
            right = jnp.where(spots == spread(src[s : s + 1]), BF(1), BF(0))
            tile = lax.dot_general(right, left, NT, preferred_element_type=F32)
            tiles[g, s * 128 : (s + 1) * 128] = tile.astype(BF)

    def place_block(g):
        names = [spread(jnp.full((1, 128), cols_ref[s, g].astype(F32), F32)) for s in range(8)]
        rows = pl.ds(pl.multiple_of(g * 128, 128), 128)
        for j in range(16):
            here = BF(j)
            t = [
                jnp.where(names[s] == here, tiles[g, s * 128 : (s + 1) * 128], BF(0))
                for s in range(8)
            ]
            total = ((t[0] + t[1]) + (t[2] + t[3])) + ((t[4] + t[5]) + (t[6] + t[7]))
            a[j * 128 : (j + 1) * 128, rows] = total

    def nth_block(i):
        n = i // 2
        step = (n + 1) // 2
        d = 4 + jnp.where(n % 2 == 1, -step, step)
        return (z + d) % 8 * 2 + i % 2

    def over(which, start, stop):
        def one(i, _):
            which(nth_block(i))
            return 0

        lax.fori_loop(start, stop, one, 0)

    def make(start, stop):
        over(make_block, start, stop)

    def place(start, stop):
        over(place_block, start, stop)

    pl.semaphore_wait(barrier, 30)

    def xg_at(h, o1, o2):
        ox, oy = ((o2, o1), (o1, o2))[h]
        return xg[ox % 4].at[8 * h : 8 * h + 8, (y + oy) % 4]

    def along_x(h, ring):
        return (h + ring) % 2 == 1

    def ag_send(h, ring, lane, j, o1, o2):
        step = (1, -1, 1, -1)[j] if ring == 1 else (1, -1, 2)[j]
        src = xg_at(h, o1, o2)
        if along_x(h, ring):
            dst = xg_at(h, o1 - step, o2) if ring == 0 else xg_at(h, o1, o2 - step)
            dev = at_x(step)
        else:
            dst = src
            dev = at_y(step)
        if ring == 1 and j >= 2:
            rows = slice(0, 16) if j == 2 else slice(16, 32)
            src, dst = src.at[:, rows], dst.at[:, rows]
        send(src, dst, ag_ss.at[h, lane, j], ag_rs.at[h, lane, j], dev)

    def ag_got(h, ring, lane, j):
        if ring == 0:
            step = (1, -1, 2)[j]
            piece = xg_at(h, -step, 0)
        else:
            step = (1, -1, 1, -1)[j]
            piece = xg_at(h, lane - 1, -step if j < 2 else 2)
            if j >= 2:
                piece = piece.at[:, slice(0, 16) if j == 2 else slice(16, 32)]
        dev = at_x(-step) if along_x(h, ring) else at_y(-step)
        got(piece, ag_ss.at[h, lane, j], ag_rs.at[h, lane, j], dev)

    def ag_ring2_own(h, o1):
        for j in (0, 1):
            ag_send(h, 1, 1 + o1, j, o1, 0)

    def ag_ring2_pass(h, o1):
        for j, o in ((0, 3), (1, 1)):
            ag_got(h, 1, 1 + o1, j)
            ag_send(h, 1, 1 + o1, 2 + j, o1, o)

    def ag_ring2_end(h, o1):
        for j in (2, 3):
            ag_got(h, 1, 1 + o1, j)

    for h in (0, 1):
        for j in (0, 1):
            ag_send(h, 0, 0, j, 0, 0)
    for h in (0, 1):
        ag_ring2_own(h, 0)
    for h in (0, 1):
        ag_send(h, 0, 0, 2, 0, 0)

    def cot_copy(i, peer, mine):
        return rc(
            cot_ref.at[:, pl.ds(pl.multiple_of(peer * 128, 128), 128)],
            cotb.at[pl.ds(pl.multiple_of(mine * 32, 32), 32), :],
            cot_ss.at[i], cot_rs.at[i], (r, peer),
        )

    def cot_send(i, _):
        cot_copy(i, (c + i) % 16, c).start()
        return 0

    loads[7].wait()
    lax.fori_loop(1, 16, cot_send, 0)
    cotb[pl.ds(pl.multiple_of(c * 32, 32), 32), :] = cot_ref[:, pl.ds(pl.multiple_of(c * 128, 128), 128)]

    loads[1].wait()
    eye = lax.broadcasted_iota(jnp.int32, (512, 512), 0) == lax.broadcasted_iota(jnp.int32, (512, 512), 1)
    wt[...] = lax.dot_general(
        jnp.where(eye, 1.0, 0.0).astype(BF), w_ref[...], NT, preferred_element_type=F32
    ).astype(BF)
    for load in loads[2:7]:
        load.wait()
    make(0, 4)
    for j, o in ((0, 3), (1, 1)):
        for h in (0, 1):
            ag_got(h, 0, 0, j)
            ag_ring2_own(h, o)
    for h in (1, 0):
        ag_ring2_pass(h, 0)
    for h in (0, 1):
        ag_got(h, 0, 0, 2)
        ag_ring2_own(h, 2)
    make(4, 8)
    for o1 in (3, 1):
        for h in (0, 1):
            ag_ring2_pass(h, o1)
    ag_ring2_end(1, 0)

    def block_product(offsets, g):
        picked = []
        for s in range(8):
            col = cols_ref[s, g]
            rows = [xg[o][col].reshape(128, 128) for o in offsets]
            picked.append(rows[0] if len(rows) == 1 else jnp.concatenate(rows, axis=0))
        left = jnp.concatenate(picked, axis=1)
        return jnp.dot(left, tiles[g], preferred_element_type=F32)

    def product(offsets, *ds):
        for d in ds:
            first = (z + d) % 8 * 2
            value = block_product(offsets, first + 1 - k)
            for i, o in enumerate(offsets):
                psend[o, d] = value[128 * i : 128 * i + 128]
                send(psend.at[o, d], precv.at[o, d], core_ss.at[o, d], core_rs.at[o, d], twin)
            value = block_product(offsets, first + k)
            for i, o in enumerate(offsets):
                pown[o, d] = value[128 * i : 128 * i + 128]

    def twin_got(o, d):
        got(precv.at[o, d], core_ss.at[o, d], core_rs.at[o, d], twin)

    HALVES = (slice(0, 64), slice(64, 128))

    def z_step(offsets, dist):
        for o in offsets:
            for d in (4,) if dist == 4 else (dist, 8 - dist):
                twin_got(o, d)
            for side in (0, 1):
                d = dist if side == 0 else 8 - dist
                sems = (rz_ss.at[side, dist, o], rz_rs.at[side, dist, o])
                before = (rz_ss.at[side, dist + 1, o], rz_rs.at[side, dist + 1, o]) if dist < 4 else None
                came, goes = at_z(-1 if side == 0 else 1), at_z(1 if side == 0 else -1)
                if dist == 4:
                    half = HALVES[side]
                    zs[side, 4, o, half] = (pown[o, d, half] + precv[o, d, half]).astype(BF)
                    send(zs.at[side, 4, o, half], zr.at[side, 3, o, half], *sems, goes)
                    continue
                value = pown[o, d] + precv[o, d]
                if dist == 3:
                    half, other = HALVES[side], HALVES[1 - side]
                    got(zr.at[side, 3, o, half], *before, came)
                    zs[side, 3, o, half] = (value[half] + zr[side, 3, o, half].astype(F32)).astype(BF)
                    zs[side, 3, o, other] = value[other].astype(BF)
                else:
                    got(zr.at[side, dist, o], *before, came)
                    zs[side, dist, o] = (value + zr[side, dist, o].astype(F32)).astype(BF)
                send(zs.at[side, dist, o], zr.at[side, dist - 1, o], *sems, goes)

    def z_last(offsets):
        for o in offsets:
            twin_got(o, 0)
            value = pown[o, 0] + precv[o, 0]
            for side in (0, 1):
                got(zr.at[side, 0, o], rz_ss.at[side, 1, o], rz_rs.at[side, 1, o], at_z(-1 if side == 0 else 1))
                value = value + zr[side, 0, o].astype(F32)
            start = pl.multiple_of((x + o) % 4 * 128, 128)
            high = value.astype(BF)
            low = (value - high.astype(F32)).astype(BF)
            axb[pl.ds(start, 128)] = high
            weights = wt[:, pl.ds(start, 128)]
            part = jnp.dot(
                jnp.concatenate([weights, weights], axis=1),
                jnp.concatenate([high, low], axis=0),
                preferred_element_type=F32,
            )
            hid[...] = part if o == 0 else hid[...] + part

    G0, G1, G2 = (0,), (1, 3), (2,)
    product(G0, 4, 3, 5)
    z_step(G0, 4)
    for h in (0, 1):
        ag_ring2_pass(h, 2)
    make(8, 13)
    for o1 in (3, 1):
        ag_ring2_end(1, o1)
    product(G1, 4)
    z_step(G0, 3)
    product(G1, 3, 5)
    z_step(G1, 4)
    make(13, 16)
    product(G0, 2, 6)
    for o1 in (0, 3, 1, 2):
        ag_ring2_end(0, o1)
    ag_ring2_end(1, 2)
    product(G2, 4)
    z_step(G0, 2)
    z_step(G2, 4)
    product(G1, 2, 6)
    z_step(G1, 3)
    product(G2, 3, 5)
    z_step(G2, 3)
    product(G0, 1, 7)
    z_step(G0, 1)
    product(G1, 1, 7)
    z_step(G1, 2)
    product(G2, 2, 6)
    z_step(G2, 2)
    product(G1, 0)
    z_step(G1, 1)
    product(G2, 1, 7)
    z_step(G2, 1)
    product(G0, 0)
    product(G2, 0)
    place(14, 16)
    z_last(G0 + G1)
    place(10, 14)
    z_last(G2)

    def cot_wait(i, _):
        cot_copy(i, c, (c + 16 - i) % 16).wait_recv()
        return 0

    lax.fori_loop(1, 16, cot_wait, 0)
    hidden = hid[...]
    sig = jax.nn.sigmoid(hidden)
    actb[...] = (hidden * sig).astype(BF)
    slope = cotb[...].astype(F32) * sig * (1.0 + hidden * (1.0 - sig))
    slb[...] = slope.astype(BF)
    sll[...] = (slope - slb[...].astype(F32)).astype(BF)
    ORDER = (2, 1, 3, 0)

    def gz_piece(side, dist, j):
        owner = (z - dist + 8) % 8 if side == 0 else (z + dist) % 8
        feats = pl.ds(pl.multiple_of((x + ORDER[j]) % 4 * 128, 128), 128)
        return tg.at[owner, k, feats]

    def gz_send(side, dist, j):
        piece = gz_piece(side, dist, j)
        send(piece, piece, gz_ss.at[side, dist, j], gz_rs.at[side, dist, j], at_z(1 if side == 0 else -1))

    def gz_got(side, dist, j):
        piece = gz_piece(side, dist, j)
        got(piece, gz_ss.at[side, dist - 1, j], gz_rs.at[side, dist - 1, j], at_z(-1 if side == 0 else 1))

    def gc_send(d):
        piece = tg.at[(z + d) % 8, k]
        send(piece, piece, gc_ss.at[d], gc_rs.at[d], twin)

    def gc_got(d):
        piece = tg.at[(z + d) % 8, 1 - k]
        got(piece, gc_ss.at[d], gc_rs.at[d], twin)

    for j in range(NS):
        feats = pl.ds(pl.multiple_of((x + ORDER[j]) % 4 * 128, 128), 128)
        tg[z, k, feats] = (
            jnp.dot(w_ref[feats], slb[...], preferred_element_type=F32)
            + jnp.dot(w_ref[feats], sll[...], preferred_element_type=F32)
        ).astype(BF)
        for side in (0, 1):
            gz_send(side, 0, j)
    gc_send(0)

    def act_copy(i, peer, mine):
        return rc(
            actb.at[pl.ds(pl.multiple_of(peer * 32, 32), 32), :],
            act_ref.at[:, pl.ds(pl.multiple_of(mine * 128, 128), 128)],
            act_ss.at[i], act_rs.at[i], (r, peer),
        )

    def act_send(i, _):
        act_copy(i, (c + i) % 16, c).start()
        return 0

    wp[...] = (
        lax.dot_general(axb[...], slb[...], NT, preferred_element_type=F32)
        .astype(BF)
        .reshape(16, 2, 16, 512)
    )
    send(wp.at[:, 1 - k], w0r, w0_ss.at[0], w0_rs.at[0], twin)

    def w1_copy(i, peer, mine):
        return rc(w0s.at[peer], w1r.at[mine], w1_ss.at[i], w1_rs.at[i], (peer, c))

    def w1_send(i, _):
        w1_copy(i, (r + i) % 16, r).start()
        return 0

    def w1_wait(i, _):
        w1_copy(i, r, (r + 16 - i) % 16).wait_recv()
        return 0

    def w2_copy(i, peer, mine):
        return rc(wz.at[mine], wz.at[mine], w2_ss.at[i], w2_rs.at[i], (r, peer * 2 + k))

    def w2_send(i, _):
        w2_copy(i, (z + i) % 8, z).start()
        return 0

    def w2_wait(i, _):
        w2_copy(i, z, (z + 8 - i) % 8).wait_recv()
        return 0

    def w3_copy(i, peer, mine):
        return rc(wg_ref.at[mine, k], wg_ref.at[mine, k], w3_ss.at[i], w3_rs.at[i], (peer, c))

    def w3_send(i, _):
        w3_copy(i, (r + i) % 16, r).start()
        return 0

    def w3_wait(i, _):
        w3_copy(i, r, (r + 16 - i) % 16).wait_recv()
        return 0

    def w_start_row():
        got(w0r, w0_ss.at[0], w0_rs.at[0], twin)
        w0s[...] = (wp[:, k].astype(F32) + w0r[...].astype(F32)).astype(BF)
        lax.fori_loop(1, 16, w1_send, 0)
        w1r[r] = w0s[r]

    def w_start_z():
        lax.fori_loop(1, 16, w1_wait, 0)
        total = w1r[0].astype(F32)
        for i in range(1, 16):
            total = total + w1r[i].astype(F32)
        wz[z] = total.astype(BF)
        lax.fori_loop(1, 8, w2_send, 0)

    def w_start_last():
        lax.fori_loop(1, 8, w2_wait, 0)
        total = wz[0].astype(F32)
        for i in range(1, 8):
            total = total + wz[i].astype(F32)
        wg_ref[r, k] = total.astype(BF)
        lax.fori_loop(1, 16, w3_send, 0)

    def w_finish():
        lax.fori_loop(1, 16, w3_wait, 0)
        send(wg_ref.at[:, k], wg_ref.at[:, k], w0_ss.at[1], w0_rs.at[1], twin)
        got(wg_ref.at[:, 1 - k], w0_ss.at[1], w0_rs.at[1], twin)

    def z_rows(side, dist, j):
        return dist < 4 or (j < NS // 2) == (side == 0)

    def gather_step(dist):
        for j in range(NS):
            for side in (0, 1):
                if not z_rows(side, dist, j):
                    continue
                gz_got(side, dist, j)
                if dist < 4 and z_rows(side, dist + 1, j):
                    gz_send(side, dist, j)
        for d in (4,) if dist == 4 else (dist, 8 - dist):
            gc_send(d)

    def back_part(d):
        block = (z + d) % 8
        left = jnp.concatenate([tg[block, 0], tg[block, 1]], axis=1)
        rows = pl.ds(pl.multiple_of(block * 256, 256), 256)
        return lax.dot_general(left, a[:, rows], NT, preferred_element_type=F32)

    gc_got(0)
    acc[...] = back_part(0)
    gather_step(1)
    w_start_row()
    place(6, 10)
    gather_step(2)
    for d in (1, 7):
        gc_got(d)
        acc[...] += back_part(d)
    place(2, 6)
    gather_step(3)
    w_start_z()
    for d in (2, 6):
        gc_got(d)
        acc[...] += back_part(d)
    place(0, 2)
    for d in (3, 5):
        gc_got(d)
        acc[...] += back_part(d)
    gather_step(4)
    gc_got(4)

    acc[...] += back_part(4)
    early = len(sent)

    def q_rows(h, o1, o2):
        if h == 0:
            block = (x + o1) % 4 * 4 + (y + o2) % 4
        else:
            block = (x + o2) % 4 * 4 + (y + o1) % 4
        return block * 32

    def q(h, o1, o2, half):
        start = q_rows(h, o1, o2)
        if half is None:
            return acc[pl.ds(pl.multiple_of(start, 32), 32), h * 1024 : (h + 1) * 1024]
        return acc[pl.ds(pl.multiple_of(start + 16 * half, 16), 16), h * 1024 : (h + 1) * 1024]

    def rx_axis(h, ring):
        return (at_x, at_y)[(h + ring) % 2]

    def rx(src, dst, h, ring, lane, j, start):
        dev = rx_axis(h, ring)(1 if j % 2 == 0 else -1)
        if start:
            send(src, dst, rx_ss.at[h, lane, j], rx_rs.at[h, lane, j], dev)
        else:
            got(dst, rx_ss.at[h, lane, j], rx_rs.at[h, lane, j], dev)

    def s1_halves(h, o2):
        for j in (0, 1):
            xs1[h, o2, 0, 16 * j : 16 * j + 16] = q(h, 2, o2, j).astype(BF)
            rx(xs1.at[h, o2, 0, 16 * j : 16 * j + 16], xr1h.at[h, o2, j], h, 0, o2, j, True)

    def s1_pass(h, o2, j):
        o = (1, 3)[j]
        rx(None, xr1h.at[h, o2, j], h, 0, o2, j, False)
        xs1[h, o2, 1 + j, 16 * j : 16 * j + 16] = (q(h, o, o2, j) + xr1h[h, o2, j].astype(F32)).astype(BF)
        xs1[h, o2, 1 + j, 16 - 16 * j : 32 - 16 * j] = q(h, o, o2, 1 - j).astype(BF)
        rx(xs1.at[h, o2, 1 + j], xr1f.at[h, o2, j], h, 0, o2, 2 + j, True)

    def s1_final(h, o2):
        for j in (0, 1):
            rx(None, xr1f.at[h, o2, j], h, 0, o2, 2 + j, False)
        s1[h, o2] = q(h, 0, o2, None) + xr1f[h, o2, 0].astype(F32) + xr1f[h, o2, 1].astype(F32)

    def s2_send(h, o2):
        xs2[h, o2 - 1] = s1[h, o2].astype(BF)
        send(xs2.at[h, o2 - 1], xr2.at[h, o2 - 1], rx_ss.at[h, 4, o2], rx_rs.at[h, 4, o2], rx_axis(h, 1)(o2))

    def s2_final(h):
        value = s1[h, 0]
        for o2 in (2, 1, 3):
            got(xr2.at[h, o2 - 1], rx_ss.at[h, 4, o2], rx_rs.at[h, 4, o2], rx_axis(h, 1)(-o2))
            value = value + xr2[h, o2 - 1].astype(F32)
        fg_ref[:, h * 1024 : (h + 1) * 1024] = value.astype(BF)

    for o2 in ORDER:
        s1_halves(0, o2)
        s1_halves(1, o2)
    lax.fori_loop(1, 16, act_send, 0)
    act_ref[:, pl.ds(pl.multiple_of(c * 128, 128), 128)] = actb[pl.ds(pl.multiple_of(c * 32, 32), 32), :]
    for o2 in ORDER:
        for h in (0, 1):
            for j in (0, 1):
                s1_pass(h, o2, j)
        if o2 == 1:
            w_start_last()
    for copy in sent[:early]:
        copy.wait_send()
    for o2 in ORDER:
        for h in (0, 1):
            s1_final(h, o2)
            if o2 > 0:
                s2_send(h, o2)
    w_finish()
    wg_copy = pltpu.make_async_copy(wg_ref, wg_out, out_sem.at[0])
    wg_copy.start()

    def act_wait(i, _):
        act_copy(i, c, (c + 16 - i) % 16).wait_recv()
        return 0

    lax.fori_loop(1, 16, act_wait, 0)
    act_store = pltpu.make_async_copy(act_ref, act_out, out_sem.at[1])
    act_store.start()
    for h in (0, 1):
        s2_final(h)
    fg_store = pltpu.make_async_copy(fg_ref, fg_out, out_sem.at[2])
    fg_store.start()

    def last(i, _):
        act_copy(i, (c + i) % 16, c).wait_send()
        cot_copy(i, (c + i) % 16, c).wait_send()
        w1_copy(i, (r + i) % 16, r).wait_send()
        w3_copy(i, (r + i) % 16, r).wait_send()
        return 0

    lax.fori_loop(1, 16, last, 0)

    def last_z(i, _):
        w2_copy(i, (z + i) % 8, z).wait_send()
        return 0

    lax.fori_loop(1, 8, last_z, 0)
    for copy in sent[early:]:
        copy.wait_send()
    for store in (wg_copy, act_store, fg_store):
        store.wait()


def layer(cols, counts, src, dst, ew, xt, cot, weight):
    dma = pltpu.SemaphoreType.DMA
    vm = pltpu.VMEM
    anywhere = pl.BlockSpec(memory_space=pl.ANY)
    return pl.pallas_call(
        layer_kernel,
        out_shape=(
            jax.ShapeDtypeStruct((32, 2048), BF),
            jax.ShapeDtypeStruct((32, 2048), BF),
            jax.ShapeDtypeStruct((16, 2, 16, 512), BF),
        ),
        in_specs=[anywhere] * 8,
        out_specs=(anywhere,) * 3,
        scratch_shapes=[
            pltpu.SMEM((8, 16), jnp.int32),
            pltpu.SMEM((1, 16), jnp.int32),
            vm((16, 8, 512), jnp.int32),
            vm((16, 8, 512), jnp.int32),
            vm((16, 8, 512), BF),
            vm((32, 2048), BF),
            vm((32, 2048), BF),
            vm((512, 512), BF),
            vm((32, 2048), BF),
            vm((32, 2048), BF),
            vm((16, 2, 16, 512), BF),
            vm((2048, 2048), BF),
            vm((16, 1024, 128), BF),
            vm((16, 4, 32, 128), BF),
            vm((16, 4, 32, 128), BF),
            vm((16, 4, 32, 128), BF),
            vm((16, 4, 32, 128), BF),
            vm((512, 512), BF),
            vm((512, 128), BF),
            vm((4, 8, 128, 128), F32),
            vm((4, 8, 128, 128), F32),
            vm((4, 8, 128, 128), F32),
            vm((2, 4, 4, 128, 128), BF),
            vm((2, 5, 4, 128, 128), BF),
            vm((512, 128), F32),
            vm((512, 128), BF),
            vm((512, 128), BF),
            vm((512, 128), BF),
            vm((512, 128), BF),
            vm((8, 2, 512, 128), BF),
            vm((512, 2048), F32),
            vm((2, 4, 3, 32, 1024), BF),
            vm((2, 4, 2, 16, 1024), BF),
            vm((2, 4, 2, 32, 1024), BF),
            vm((2, 4, 32, 1024), F32),
            vm((2, 3, 32, 1024), BF),
            vm((2, 3, 32, 1024), BF),
            vm((16, 2, 16, 512), BF),
            vm((16, 16, 512), BF),
            vm((16, 16, 512), BF),
            vm((16, 16, 512), BF),
            vm((8, 16, 512), BF),
            dma((8,)),
            dma((3,)),
        ]
        + [dma((16,))] * 2
        + [dma((2, 5, 4))] * 2
        + [dma((4, 8))] * 2
        + [dma((2, 5, 4))] * 2
        + [dma((16,))] * 2
        + [dma((2, 4, NS))] * 2
        + [dma((8,))] * 2
        + [dma((2, 5, 4))] * 2
        + [dma((2,))] * 2
        + [dma((16,))] * 2
        + [dma((8,))] * 2
        + [dma((16,))] * 2,
        compiler_params=pltpu.CompilerParams(
            collective_id=0, has_side_effects=True, vmem_limit_bytes=58 << 20
        ),
        name="layer",
    )(cols, counts, src, dst, ew, xt, cot, weight)


def finish_kernel(act_ref, fg_ref, wg_ref, act_out, fg_out, wg_out, act_in, fg_in, wg_in, sems):
    pairs = ((wg_ref, wg_in), (act_ref, act_in), (fg_ref, fg_in))
    copies = [pltpu.make_async_copy(src, dst, sems.at[i]) for i, (src, dst) in enumerate(pairs)]
    copies += [
        pltpu.make_async_copy(act_in, act_out, sems.at[3]),
        pltpu.make_async_copy(fg_in, fg_out, sems.at[4]),
    ]
    for copy in copies[:3]:
        copy.start()
    for i in (1, 2):
        copies[i].wait()
        copies[i + 2].start()
    copies[0].wait()
    wg_out[...] = wg_in[...].astype(F32)
    copies[3].wait()
    copies[4].wait()


def finish(act, fg, wg):
    anywhere = pl.BlockSpec(memory_space=pl.ANY)
    return pl.pallas_call(
        finish_kernel,
        out_shape=(
            jax.ShapeDtypeStruct((32, 2048), BF),
            jax.ShapeDtypeStruct((32, 2048), BF),
            jax.ShapeDtypeStruct((512, 512), F32),
        ),
        in_specs=[anywhere] * 3,
        out_specs=(anywhere, anywhere, pl.BlockSpec(memory_space=pltpu.VMEM)),
        scratch_shapes=[
            pltpu.VMEM((32, 2048), BF),
            pltpu.VMEM((32, 2048), BF),
            pltpu.VMEM((512, 512), BF),
            pltpu.SemaphoreType.DMA((5,)),
        ],
        compiler_params=pltpu.CompilerParams(vmem_limit_bytes=58 << 20),
        name="finish",
    )(act, fg, wg.reshape(512, 512))


def shards(features, weight, block_cols, block_count, edge_src, edge_dst, edge_weight, cotangent):
    outs = layer(
        block_cols[:, 0, :].T, block_count.T, edge_src[:, 0], edge_dst[:, 0], edge_weight[:, 0],
        features.T, cotangent.T, weight,
    )
    act, fg, wg = finish(*outs)
    return act.T, fg.T, wg


def solution(mesh):
    return jax.shard_map(
        shards,
        mesh=mesh,
        in_specs=(
            P("col", "row"),
            P(),
            P("row", "col", None),
            P("row", "col"),
            P("row", "col", None, None),
            P("row", "col", None, None),
            P("row", "col", None, None),
            P("row", "col"),
        ),
        out_specs=(P("row", "col"), P("col", "row"), P()),
        check_vma=False,
    )
```

```python
import jax
import jax.numpy as jnp
from jax import lax
from jax.experimental import pallas as pl
from jax.experimental.pallas import tpu as pltpu
from jax.sharding import PartitionSpec as P

MESH = pl.DeviceIdType.MESH
BF = jnp.bfloat16
F32 = jnp.float32
NT = (((1,), (1,)), ((), ()))
NS = 4
SUB = 512 // NS


def layer_kernel(
    cols_in, counts_in, src_in, dst_in, ew_in, xt_in, cot_in, w_in,
    act_out, fg_out, wg_out,
    cols_ref, counts_ref, src_ref, dst_ref, ew_ref, xt_ref, cot_ref, w_ref, act_ref, fg_ref, wg_ref,
    a, tiles, xg0, xg1, xg2, xg3, wt, cotb, pown, psend, precv, zr, zs, hid, axb, actb, slb, sll, tg, acc,
    xs1, xr1h, xr1f, s1, xs2, xr2,
    wp, w0r, w0s, w1r, wz,
    in_sem, out_sem,
    cot_ss, cot_rs, ag_ss, ag_rs, core_ss, core_rs, rz_ss, rz_rs,
    act_ss, act_rs, gz_ss, gz_rs, gc_ss, gc_rs, gd_ss, gd_rs, rx_ss, rx_rs,
    w0_ss, w0_rs, w1_ss, w1_rs, w2_ss, w2_rs, w3_ss, w3_rs,
):
    r = lax.axis_index("row")
    c = lax.axis_index("col")
    x, y = r // 4, r % 4
    z, k = c // 2, c % 2

    def at_x(o):
        return ((x + o) % 4 * 4 + y, c)

    def at_y(o):
        return (x * 4 + (y + o) % 4, c)

    def at_z(o):
        return (r, (z + o) % 8 * 2 + k)

    twin = (r, z * 2 + 1 - k)

    def rc(src, dst, ss, rs, dev):
        return pltpu.make_async_remote_copy(
            src_ref=src, dst_ref=dst, send_sem=ss, recv_sem=rs, device_id=dev, device_id_type=MESH
        )

    xg = (xg0, xg1, xg2, xg3)
    sent = []

    def send(src, dst, ss, rs, dev):
        copy = rc(src, dst, ss, rs, dev)
        copy.start()
        sent.append(copy)

    def got(ref, ss, rs, dev):
        rc(ref, ref, ss, rs, dev).wait_recv()

    pairs = (
        (xt_in, xt_ref), (w_in, w_ref), (cols_in, cols_ref), (counts_in, counts_ref),
        (src_in, src_ref), (dst_in, dst_ref), (ew_in, ew_ref), (cot_in, cot_ref),
    )
    loads = [pltpu.make_async_copy(src, dst, in_sem.at[i]) for i, (src, dst) in enumerate(pairs)]
    for load in loads:
        load.start()

    barrier = pltpu.get_barrier_semaphore()

    for i in (8, 7, 9, 6, 10, 5, 11, 4, 12, 3, 13, 2, 14, 1, 15):
        pl.semaphore_signal(barrier, inc=1, device_id=(r, (c + i) % 16), device_id_type=MESH)
        pl.semaphore_signal(barrier, inc=1, device_id=((r + i) % 16, c), device_id_type=MESH)
    loads[0].wait()
    for b in range(16):
        xg0[b, y] = xt_ref[:, b * 128 : (b + 1) * 128]

    spots = lax.broadcasted_iota(jnp.int32, (128, 512), 0).astype(F32).astype(BF)
    slots = lax.broadcasted_iota(jnp.int32, (8, 512), 0)

    def spread(row):
        piece = jnp.broadcast_to(row, (16, row.shape[1])).astype(BF)
        return jnp.concatenate([piece] * 8, axis=0)

    def make_block(g):
        src = src_ref[g].astype(F32)
        dst = dst_ref[g].astype(F32)
        wts = jnp.where(slots < counts_ref[0, g], ew_ref[g].astype(F32), 0.0)
        for s in range(8):
            left = jnp.where(spots == spread(dst[s : s + 1]), spread(wts[s : s + 1]), BF(0))
            right = jnp.where(spots == spread(src[s : s + 1]), BF(1), BF(0))
            tile = lax.dot_general(right, left, NT, preferred_element_type=F32)
            tiles[g, s * 128 : (s + 1) * 128] = tile.astype(BF)

    def place_block(g):
        names = [spread(jnp.full((1, 128), cols_ref[s, g].astype(F32), F32)) for s in range(8)]
        rows = pl.ds(pl.multiple_of(g * 128, 128), 128)
        for j in range(16):
            here = BF(j)
            t = [
                jnp.where(names[s] == here, tiles[g, s * 128 : (s + 1) * 128], BF(0))
                for s in range(8)
            ]
            total = ((t[0] + t[1]) + (t[2] + t[3])) + ((t[4] + t[5]) + (t[6] + t[7]))
            a[j * 128 : (j + 1) * 128, rows] = total

    def nth_block(i):
        n = i // 2
        step = (n + 1) // 2
        d = 4 + jnp.where(n % 2 == 1, -step, step)
        return (z + d) % 8 * 2 + i % 2

    def over(which, start, stop):
        def one(i, _):
            which(nth_block(i))
            return 0

        lax.fori_loop(start, stop, one, 0)

    def make(start, stop):
        over(make_block, start, stop)

    def place(start, stop):
        over(place_block, start, stop)

    pl.semaphore_wait(barrier, 30)

    def xg_at(h, o1, o2):
        ox, oy = ((o2, o1), (o1, o2))[h]
        return xg[ox % 4].at[8 * h : 8 * h + 8, (y + oy) % 4]

    def along_x(h, ring):
        return (h + ring) % 2 == 1

    def ag_send(h, ring, lane, j, o1, o2):
        step = (1, -1, 1, -1)[j] if ring == 1 else (1, -1, 2)[j]
        src = xg_at(h, o1, o2)
        if along_x(h, ring):
            dst = xg_at(h, o1 - step, o2) if ring == 0 else xg_at(h, o1, o2 - step)
            dev = at_x(step)
        else:
            dst = src
            dev = at_y(step)
        if ring == 1 and j >= 2:
            rows = slice(0, 16) if j == 2 else slice(16, 32)
            src, dst = src.at[:, rows], dst.at[:, rows]
        send(src, dst, ag_ss.at[h, lane, j], ag_rs.at[h, lane, j], dev)

    def ag_got(h, ring, lane, j):
        if ring == 0:
            step = (1, -1, 2)[j]
            piece = xg_at(h, -step, 0)
        else:
            step = (1, -1, 1, -1)[j]
            piece = xg_at(h, lane - 1, -step if j < 2 else 2)
            if j >= 2:
                piece = piece.at[:, slice(0, 16) if j == 2 else slice(16, 32)]
        dev = at_x(-step) if along_x(h, ring) else at_y(-step)
        got(piece, ag_ss.at[h, lane, j], ag_rs.at[h, lane, j], dev)

    def ag_ring2_own(h, o1):
        for j in (0, 1):
            ag_send(h, 1, 1 + o1, j, o1, 0)

    def ag_ring2_pass(h, o1):
        for j, o in ((0, 3), (1, 1)):
            ag_got(h, 1, 1 + o1, j)
            ag_send(h, 1, 1 + o1, 2 + j, o1, o)

    def ag_ring2_end(h, o1):
        for j in (2, 3):
            ag_got(h, 1, 1 + o1, j)

    for h in (0, 1):
        for j in (0, 1):
            ag_send(h, 0, 0, j, 0, 0)
    for h in (0, 1):
        ag_ring2_own(h, 0)
    for h in (0, 1):
        ag_send(h, 0, 0, 2, 0, 0)

    def cot_copy(i, peer, mine):
        return rc(
            cot_ref.at[:, pl.ds(pl.multiple_of(peer * 128, 128), 128)],
            cotb.at[pl.ds(pl.multiple_of(mine * 32, 32), 32), :],
            cot_ss.at[i], cot_rs.at[i], (r, peer),
        )

    def cot_send(i, _):
        cot_copy(i, (c + i) % 16, c).start()
        return 0

    loads[7].wait()
    lax.fori_loop(1, 16, cot_send, 0)
    cotb[pl.ds(pl.multiple_of(c * 32, 32), 32), :] = cot_ref[:, pl.ds(pl.multiple_of(c * 128, 128), 128)]

    loads[1].wait()
    eye = lax.broadcasted_iota(jnp.int32, (512, 512), 0) == lax.broadcasted_iota(jnp.int32, (512, 512), 1)
    wt[...] = lax.dot_general(
        jnp.where(eye, 1.0, 0.0).astype(BF), w_ref[...], NT, preferred_element_type=F32
    ).astype(BF)
    for load in loads[2:7]:
        load.wait()
    make(0, 4)
    for j, o in ((0, 3), (1, 1)):
        for h in (0, 1):
            ag_got(h, 0, 0, j)
            ag_ring2_own(h, o)
    for h in (1, 0):
        ag_ring2_pass(h, 0)
    for h in (0, 1):
        ag_got(h, 0, 0, 2)
        ag_ring2_own(h, 2)
    make(4, 8)
    for o1 in (3, 1):
        for h in (0, 1):
            ag_ring2_pass(h, o1)
    ag_ring2_end(1, 0)

    def block_product(offsets, g):
        picked = []
        for s in range(8):
            col = cols_ref[s, g]
            rows = [xg[o][col].reshape(128, 128) for o in offsets]
            picked.append(rows[0] if len(rows) == 1 else jnp.concatenate(rows, axis=0))
        left = jnp.concatenate(picked, axis=1)
        return jnp.dot(left, tiles[g], preferred_element_type=F32)

    def product(offsets, *ds):
        for d in ds:
            first = (z + d) % 8 * 2
            value = block_product(offsets, first + 1 - k)
            for i, o in enumerate(offsets):
                psend[o, d] = value[128 * i : 128 * i + 128]
                send(psend.at[o, d], precv.at[o, d], core_ss.at[o, d], core_rs.at[o, d], twin)
            value = block_product(offsets, first + k)
            for i, o in enumerate(offsets):
                pown[o, d] = value[128 * i : 128 * i + 128]

    def twin_got(o, d):
        got(precv.at[o, d], core_ss.at[o, d], core_rs.at[o, d], twin)

    HALVES = (slice(0, 64), slice(64, 128))

    def z_step(offsets, dist):
        for o in offsets:
            for d in (4,) if dist == 4 else (dist, 8 - dist):
                twin_got(o, d)
            for side in (0, 1):
                d = dist if side == 0 else 8 - dist
                sems = (rz_ss.at[side, dist, o], rz_rs.at[side, dist, o])
                before = (rz_ss.at[side, dist + 1, o], rz_rs.at[side, dist + 1, o]) if dist < 4 else None
                came, goes = at_z(-1 if side == 0 else 1), at_z(1 if side == 0 else -1)
                if dist == 4:
                    half = HALVES[side]
                    zs[side, 4, o, half] = (pown[o, d, half] + precv[o, d, half]).astype(BF)
                    send(zs.at[side, 4, o, half], zr.at[side, 3, o, half], *sems, goes)
                    continue
                value = pown[o, d] + precv[o, d]
                if dist == 3:
                    half, other = HALVES[side], HALVES[1 - side]
                    got(zr.at[side, 3, o, half], *before, came)
                    zs[side, 3, o, half] = (value[half] + zr[side, 3, o, half].astype(F32)).astype(BF)
                    zs[side, 3, o, other] = value[other].astype(BF)
                else:
                    got(zr.at[side, dist, o], *before, came)
                    zs[side, dist, o] = (value + zr[side, dist, o].astype(F32)).astype(BF)
                send(zs.at[side, dist, o], zr.at[side, dist - 1, o], *sems, goes)

    def z_last(offsets):
        for o in offsets:
            twin_got(o, 0)
            value = pown[o, 0] + precv[o, 0]
            for side in (0, 1):
                got(zr.at[side, 0, o], rz_ss.at[side, 1, o], rz_rs.at[side, 1, o], at_z(-1 if side == 0 else 1))
                value = value + zr[side, 0, o].astype(F32)
            start = pl.multiple_of((x + o) % 4 * 128, 128)
            high = value.astype(BF)
            low = (value - high.astype(F32)).astype(BF)
            axb[pl.ds(start, 128)] = high
            weights = wt[:, pl.ds(start, 128)]
            part = jnp.dot(
                jnp.concatenate([weights, weights], axis=1),
                jnp.concatenate([high, low], axis=0),
                preferred_element_type=F32,
            )
            hid[...] = part if o == 0 else hid[...] + part

    G0, G1, G2 = (0,), (1, 3), (2,)
    product(G0, 4, 3, 5)
    z_step(G0, 4)
    for h in (0, 1):
        ag_ring2_pass(h, 2)
    make(8, 13)
    for o1 in (3, 1):
        ag_ring2_end(1, o1)
    product(G1, 4)
    z_step(G0, 3)
    product(G1, 3, 5)
    z_step(G1, 4)
    make(13, 16)
    product(G0, 2, 6)
    for o1 in (0, 3, 1, 2):
        ag_ring2_end(0, o1)
    ag_ring2_end(1, 2)
    product(G2, 4)
    z_step(G0, 2)
    z_step(G2, 4)
    product(G1, 2, 6)
    z_step(G1, 3)
    product(G2, 3, 5)
    z_step(G2, 3)
    product(G0, 1, 7)
    z_step(G0, 1)
    product(G1, 1, 7)
    z_step(G1, 2)
    product(G2, 2, 6)
    z_step(G2, 2)
    product(G1, 0)
    z_step(G1, 1)
    product(G2, 1, 7)
    z_step(G2, 1)
    product(G0, 0)
    product(G2, 0)
    place(14, 16)
    z_last(G0 + G1)
    place(10, 14)
    z_last(G2)

    def cot_wait(i, _):
        cot_copy(i, c, (c + 16 - i) % 16).wait_recv()
        return 0

    lax.fori_loop(1, 16, cot_wait, 0)
    hidden = hid[...]
    sig = jax.nn.sigmoid(hidden)
    actb[...] = (hidden * sig).astype(BF)
    slope = cotb[...].astype(F32) * sig * (1.0 + hidden * (1.0 - sig))
    slb[...] = slope.astype(BF)
    sll[...] = (slope - slb[...].astype(F32)).astype(BF)
    ORDER = (2, 1, 3, 0)

    def gz_piece(side, dist, j):
        owner = (z - dist + 8) % 8 if side == 0 else (z + dist) % 8
        feats = pl.ds(pl.multiple_of((x + ORDER[j]) % 4 * 128, 128), 128)
        return tg.at[owner, k, feats]

    def gz_send(side, dist, j):
        piece = gz_piece(side, dist, j)
        send(piece, piece, gz_ss.at[side, dist, j], gz_rs.at[side, dist, j], at_z(1 if side == 0 else -1))

    def gz_got(side, dist, j):
        piece = gz_piece(side, dist, j)
        got(piece, gz_ss.at[side, dist - 1, j], gz_rs.at[side, dist - 1, j], at_z(-1 if side == 0 else 1))

    def gc_send(d):
        piece = tg.at[(z + d) % 8, k]
        send(piece, piece, gc_ss.at[d], gc_rs.at[d], twin)

    def gc_got(d):
        piece = tg.at[(z + d) % 8, 1 - k]
        got(piece, gc_ss.at[d], gc_rs.at[d], twin)

    for j in range(NS):
        feats = pl.ds(pl.multiple_of((x + ORDER[j]) % 4 * 128, 128), 128)
        tg[z, k, feats] = (
            jnp.dot(w_ref[feats], slb[...], preferred_element_type=F32)
            + jnp.dot(w_ref[feats], sll[...], preferred_element_type=F32)
        ).astype(BF)
        for side in (0, 1):
            gz_send(side, 0, j)
    gc_send(0)

    def act_copy(i, peer, mine):
        return rc(
            actb.at[pl.ds(pl.multiple_of(peer * 32, 32), 32), :],
            act_ref.at[:, pl.ds(pl.multiple_of(mine * 128, 128), 128)],
            act_ss.at[i], act_rs.at[i], (r, peer),
        )

    def act_send(i, _):
        act_copy(i, (c + i) % 16, c).start()
        return 0

    wp[...] = (
        lax.dot_general(axb[...], slb[...], NT, preferred_element_type=F32)
        .astype(BF)
        .reshape(16, 2, 16, 512)
    )
    send(wp.at[:, 1 - k], w0r, w0_ss.at[0], w0_rs.at[0], twin)

    def w1_copy(i, peer, mine):
        return rc(w0s.at[peer], w1r.at[mine], w1_ss.at[i], w1_rs.at[i], (peer, c))

    def w1_send(i, _):
        w1_copy(i, (r + i) % 16, r).start()
        return 0

    def w1_wait(i, _):
        w1_copy(i, r, (r + 16 - i) % 16).wait_recv()
        return 0

    def w2_copy(i, peer, mine):
        return rc(wz.at[mine], wz.at[mine], w2_ss.at[i], w2_rs.at[i], (r, peer * 2 + k))

    def w2_send(i, _):
        w2_copy(i, (z + i) % 8, z).start()
        return 0

    def w2_wait(i, _):
        w2_copy(i, z, (z + 8 - i) % 8).wait_recv()
        return 0

    def w3_copy(i, peer, mine):
        return rc(wg_ref.at[mine, k], wg_ref.at[mine, k], w3_ss.at[i], w3_rs.at[i], (peer, c))

    def w3_send(i, _):
        w3_copy(i, (r + i) % 16, r).start()
        return 0

    def w3_wait(i, _):
        w3_copy(i, r, (r + 16 - i) % 16).wait_recv()
        return 0

    def w_start_row():
        got(w0r, w0_ss.at[0], w0_rs.at[0], twin)
        w0s[...] = (wp[:, k].astype(F32) + w0r[...].astype(F32)).astype(BF)
        lax.fori_loop(1, 16, w1_send, 0)
        w1r[r] = w0s[r]

    def w_start_z():
        lax.fori_loop(1, 16, w1_wait, 0)
        total = w1r[0].astype(F32)
        for i in range(1, 16):
            total = total + w1r[i].astype(F32)
        wz[z] = total.astype(BF)
        lax.fori_loop(1, 8, w2_send, 0)

    def w_start_last():
        lax.fori_loop(1, 8, w2_wait, 0)
        total = wz[0].astype(F32)
        for i in range(1, 8):
            total = total + wz[i].astype(F32)
        wg_ref[r, k] = total.astype(BF)
        lax.fori_loop(1, 16, w3_send, 0)

    def w_finish():
        lax.fori_loop(1, 16, w3_wait, 0)
        send(wg_ref.at[:, k], wg_ref.at[:, k], w0_ss.at[1], w0_rs.at[1], twin)
        got(wg_ref.at[:, 1 - k], w0_ss.at[1], w0_rs.at[1], twin)

    def z_rows(side, dist, j):
        return dist < 4 or (j < NS // 2) == (side == 0)

    def far_piece(core, j):
        feats = pl.ds(pl.multiple_of((x + ORDER[j]) % 4 * 128, 128), 128)
        return tg.at[(z + 4) % 8, core, feats]

    def gather_step(dist):
        for j in range(NS):
            for side in (0, 1):
                if not z_rows(side, dist, j):
                    continue
                gz_got(side, dist, j)
                if dist < 4 and z_rows(side, dist + 1, j):
                    gz_send(side, dist, j)
                if dist == 4:
                    send(far_piece(k, j), far_piece(k, j), gd_ss.at[j], gd_rs.at[j], twin)
        if dist < 4:
            for d in (dist, 8 - dist):
                gc_send(d)

    def back_part(d):
        block = (z + d) % 8
        left = jnp.concatenate([tg[block, 0], tg[block, 1]], axis=1)
        rows = pl.ds(pl.multiple_of(block * 256, 256), 256)
        return lax.dot_general(left, a[:, rows], NT, preferred_element_type=F32)

    gc_got(0)
    acc[...] = back_part(0)
    gather_step(1)
    w_start_row()
    place(6, 10)
    gather_step(2)
    for d in (1, 7):
        gc_got(d)
        acc[...] += back_part(d)
    place(2, 6)
    gather_step(3)
    w_start_z()
    for d in (2, 6):
        gc_got(d)
        acc[...] += back_part(d)
    place(0, 2)
    for d in (3, 5):
        gc_got(d)
        acc[...] += back_part(d)
    gather_step(4)
    for j in range(NS):
        got(far_piece(1 - k, j), gd_ss.at[j], gd_rs.at[j], twin)

    early = len(sent)

    def q_rows(h, o1, o2):
        if h == 0:
            block = (x + o1) % 4 * 4 + (y + o2) % 4
        else:
            block = (x + o2) % 4 * 4 + (y + o1) % 4
        return block * 32

    def q(h, o1, o2, half):
        start = q_rows(h, o1, o2)
        if half is None:
            return acc[pl.ds(pl.multiple_of(start, 32), 32), h * 1024 : (h + 1) * 1024]
        return acc[pl.ds(pl.multiple_of(start + 16 * half, 16), 16), h * 1024 : (h + 1) * 1024]

    def rx_axis(h, ring):
        return (at_x, at_y)[(h + ring) % 2]

    def rx(src, dst, h, ring, lane, j, start):
        dev = rx_axis(h, ring)(1 if j % 2 == 0 else -1)
        if start:
            send(src, dst, rx_ss.at[h, lane, j], rx_rs.at[h, lane, j], dev)
        else:
            got(dst, rx_ss.at[h, lane, j], rx_rs.at[h, lane, j], dev)

    def s1_halves(h, o2):
        for j in (0, 1):
            xs1[h, o2, 0, 16 * j : 16 * j + 16] = q(h, 2, o2, j).astype(BF)
            rx(xs1.at[h, o2, 0, 16 * j : 16 * j + 16], xr1h.at[h, o2, j], h, 0, o2, j, True)

    def s1_pass(h, o2, j):
        o = (1, 3)[j]
        rx(None, xr1h.at[h, o2, j], h, 0, o2, j, False)
        xs1[h, o2, 1 + j, 16 * j : 16 * j + 16] = (q(h, o, o2, j) + xr1h[h, o2, j].astype(F32)).astype(BF)
        xs1[h, o2, 1 + j, 16 - 16 * j : 32 - 16 * j] = q(h, o, o2, 1 - j).astype(BF)
        rx(xs1.at[h, o2, 1 + j], xr1f.at[h, o2, j], h, 0, o2, 2 + j, True)

    def s1_final(h, o2):
        for j in (0, 1):
            rx(None, xr1f.at[h, o2, j], h, 0, o2, 2 + j, False)
        s1[h, o2] = q(h, 0, o2, None) + xr1f[h, o2, 0].astype(F32) + xr1f[h, o2, 1].astype(F32)

    def s2_send(h, o2):
        xs2[h, o2 - 1] = s1[h, o2].astype(BF)
        send(xs2.at[h, o2 - 1], xr2.at[h, o2 - 1], rx_ss.at[h, 4, o2], rx_rs.at[h, 4, o2], rx_axis(h, 1)(o2))

    def s2_final(h):
        value = s1[h, 0]
        for o2 in (2, 1, 3):
            got(xr2.at[h, o2 - 1], rx_ss.at[h, 4, o2], rx_rs.at[h, 4, o2], rx_axis(h, 1)(-o2))
            value = value + xr2[h, o2 - 1].astype(F32)
        fg_ref[:, h * 1024 : (h + 1) * 1024] = value.astype(BF)

    far = (z + 4) % 8
    left = jnp.concatenate([tg[far, 0], tg[far, 1]], axis=1)
    far_rows = pl.ds(pl.multiple_of(far * 256, 256), 256)
    for h in (0, 1):
        nodes = slice(h * 1024, (h + 1) * 1024)
        acc[:, nodes] += lax.dot_general(left, a[nodes, far_rows], NT, preferred_element_type=F32)
        for o2 in ORDER:
            s1_halves(h, o2)
    lax.fori_loop(1, 16, act_send, 0)
    act_ref[:, pl.ds(pl.multiple_of(c * 128, 128), 128)] = actb[pl.ds(pl.multiple_of(c * 32, 32), 32), :]
    for o2 in ORDER:
        for h in (0, 1):
            for j in (0, 1):
                s1_pass(h, o2, j)
        if o2 == 1:
            w_start_last()
    for copy in sent[:early]:
        copy.wait_send()
    for o2 in ORDER:
        for h in (0, 1):
            s1_final(h, o2)
            if o2 > 0:
                s2_send(h, o2)
    w_finish()
    wg_copy = pltpu.make_async_copy(wg_ref, wg_out, out_sem.at[0])
    wg_copy.start()

    def act_wait(i, _):
        act_copy(i, c, (c + 16 - i) % 16).wait_recv()
        return 0

    lax.fori_loop(1, 16, act_wait, 0)
    act_store = pltpu.make_async_copy(act_ref, act_out, out_sem.at[1])
    act_store.start()
    for h in (0, 1):
        s2_final(h)
    fg_store = pltpu.make_async_copy(fg_ref, fg_out, out_sem.at[2])
    fg_store.start()

    def last(i, _):
        act_copy(i, (c + i) % 16, c).wait_send()
        cot_copy(i, (c + i) % 16, c).wait_send()
        w1_copy(i, (r + i) % 16, r).wait_send()
        w3_copy(i, (r + i) % 16, r).wait_send()
        return 0

    lax.fori_loop(1, 16, last, 0)

    def last_z(i, _):
        w2_copy(i, (z + i) % 8, z).wait_send()
        return 0

    lax.fori_loop(1, 8, last_z, 0)
    for copy in sent[early:]:
        copy.wait_send()
    for store in (wg_copy, act_store, fg_store):
        store.wait()


def layer(cols, counts, src, dst, ew, xt, cot, weight):
    dma = pltpu.SemaphoreType.DMA
    vm = pltpu.VMEM
    anywhere = pl.BlockSpec(memory_space=pl.ANY)
    return pl.pallas_call(
        layer_kernel,
        out_shape=(
            jax.ShapeDtypeStruct((32, 2048), BF),
            jax.ShapeDtypeStruct((32, 2048), BF),
            jax.ShapeDtypeStruct((16, 2, 16, 512), BF),
        ),
        in_specs=[anywhere] * 8,
        out_specs=(anywhere,) * 3,
        scratch_shapes=[
            pltpu.SMEM((8, 16), jnp.int32),
            pltpu.SMEM((1, 16), jnp.int32),
            vm((16, 8, 512), jnp.int32),
            vm((16, 8, 512), jnp.int32),
            vm((16, 8, 512), BF),
            vm((32, 2048), BF),
            vm((32, 2048), BF),
            vm((512, 512), BF),
            vm((32, 2048), BF),
            vm((32, 2048), BF),
            vm((16, 2, 16, 512), BF),
            vm((2048, 2048), BF),
            vm((16, 1024, 128), BF),
            vm((16, 4, 32, 128), BF),
            vm((16, 4, 32, 128), BF),
            vm((16, 4, 32, 128), BF),
            vm((16, 4, 32, 128), BF),
            vm((512, 512), BF),
            vm((512, 128), BF),
            vm((4, 8, 128, 128), F32),
            vm((4, 8, 128, 128), F32),
            vm((4, 8, 128, 128), F32),
            vm((2, 4, 4, 128, 128), BF),
            vm((2, 5, 4, 128, 128), BF),
            vm((512, 128), F32),
            vm((512, 128), BF),
            vm((512, 128), BF),
            vm((512, 128), BF),
            vm((512, 128), BF),
            vm((8, 2, 512, 128), BF),
            vm((512, 2048), F32),
            vm((2, 4, 3, 32, 1024), BF),
            vm((2, 4, 2, 16, 1024), BF),
            vm((2, 4, 2, 32, 1024), BF),
            vm((2, 4, 32, 1024), F32),
            vm((2, 3, 32, 1024), BF),
            vm((2, 3, 32, 1024), BF),
            vm((16, 2, 16, 512), BF),
            vm((16, 16, 512), BF),
            vm((16, 16, 512), BF),
            vm((16, 16, 512), BF),
            vm((8, 16, 512), BF),
            dma((8,)),
            dma((3,)),
        ]
        + [dma((16,))] * 2
        + [dma((2, 5, 4))] * 2
        + [dma((4, 8))] * 2
        + [dma((2, 5, 4))] * 2
        + [dma((16,))] * 2
        + [dma((2, 4, NS))] * 2
        + [dma((8,))] * 2
        + [dma((NS,))] * 2
        + [dma((2, 5, 4))] * 2
        + [dma((2,))] * 2
        + [dma((16,))] * 2
        + [dma((8,))] * 2
        + [dma((16,))] * 2,
        compiler_params=pltpu.CompilerParams(
            collective_id=0, has_side_effects=True, vmem_limit_bytes=58 << 20
        ),
        name="layer",
    )(cols, counts, src, dst, ew, xt, cot, weight)


def finish_kernel(act_ref, fg_ref, wg_ref, act_out, fg_out, wg_out, act_in, fg_in, wg_in, wg_wide, sems):
    rows = [pl.ds(128 * i, 128) for i in range(4)]
    pairs = [(wg_ref.at[p], wg_in.at[p], wg_wide.at[p], wg_out.at[p]) for p in rows]
    pairs += [(act_ref, act_in, act_in, act_out), (fg_ref, fg_in, fg_in, fg_out)]
    loads = [pltpu.make_async_copy(p[0], p[1], sems.at[0, i]) for i, p in enumerate(pairs)]
    stores = [pltpu.make_async_copy(p[2], p[3], sems.at[1, i]) for i, p in enumerate(pairs)]
    for load in loads:
        load.start()
    for i in range(6):
        loads[i].wait()
        if i < 4:
            wg_wide[rows[i]] = wg_in[rows[i]].astype(F32)
        stores[i].start()
    for store in stores:
        store.wait()


def finish(act, fg, wg):
    anywhere = pl.BlockSpec(memory_space=pl.ANY)
    return pl.pallas_call(
        finish_kernel,
        out_shape=(
            jax.ShapeDtypeStruct((32, 2048), BF),
            jax.ShapeDtypeStruct((32, 2048), BF),
            jax.ShapeDtypeStruct((512, 512), F32),
        ),
        in_specs=[anywhere] * 3,
        out_specs=(anywhere,) * 3,
        scratch_shapes=[
            pltpu.VMEM((32, 2048), BF),
            pltpu.VMEM((32, 2048), BF),
            pltpu.VMEM((512, 512), BF),
            pltpu.VMEM((512, 512), F32),
            pltpu.SemaphoreType.DMA((2, 6)),
        ],
        compiler_params=pltpu.CompilerParams(vmem_limit_bytes=58 << 20),
        name="finish",
    )(act, fg, wg.reshape(512, 512))


def shards(features, weight, block_cols, block_count, edge_src, edge_dst, edge_weight, cotangent):
    outs = layer(
        block_cols[:, 0, :].T, block_count.T, edge_src[:, 0], edge_dst[:, 0], edge_weight[:, 0],
        features.T, cotangent.T, weight,
    )
    act, fg, wg = finish(*outs)
    return act.T, fg.T, wg


def solution(mesh):
    return jax.shard_map(
        shards,
        mesh=mesh,
        in_specs=(
            P("col", "row"),
            P(),
            P("row", "col", None),
            P("row", "col"),
            P("row", "col", None, None),
            P("row", "col", None, None),
            P("row", "col", None, None),
            P("row", "col"),
        ),
        out_specs=(P("row", "col"), P("col", "row"), P()),
        check_vma=False,
    )
```

```python
import jax
import jax.numpy as jnp
from jax import lax
from jax.experimental import pallas as pl
from jax.experimental.pallas import tpu as pltpu
from jax.sharding import PartitionSpec as P

MESH = pl.DeviceIdType.MESH
BF = jnp.bfloat16
F32 = jnp.float32
NT = (((1,), (1,)), ((), ()))
NS = 4
SUB = 512 // NS


def layer_kernel(
    cols_in, counts_in, src_in, dst_in, ew_in, xt_in, cot_in, w_in,
    act_out, fg_out, wg_out,
    cols_ref, counts_ref, src_ref, dst_ref, ew_ref, xt_ref, cot_ref, w_ref, act_ref, fg_ref, wg_ref,
    a, tiles, xg0, xg1, xg2, xg3, wt, cotb, pown, psend, precv, zr, zs, hid, axb, actb, slb, sll, tg, acc,
    xs1, xr1h, xr1f, s1, xs2, xr2,
    wp, w0r, w0s, w1r, wz,
    in_sem, out_sem,
    cot_ss, cot_rs, ag_ss, ag_rs, core_ss, core_rs, rz_ss, rz_rs,
    act_ss, act_rs, gz_ss, gz_rs, gc_ss, gc_rs, gd_ss, gd_rs, rx_ss, rx_rs,
    w0_ss, w0_rs, w1_ss, w1_rs, w2_ss, w2_rs, w3_ss, w3_rs,
):
    r = lax.axis_index("row")
    c = lax.axis_index("col")
    x, y = r // 4, r % 4
    z, k = c // 2, c % 2

    def at_x(o):
        return ((x + o) % 4 * 4 + y, c)

    def at_y(o):
        return (x * 4 + (y + o) % 4, c)

    def at_z(o):
        return (r, (z + o) % 8 * 2 + k)

    twin = (r, z * 2 + 1 - k)

    def rc(src, dst, ss, rs, dev):
        return pltpu.make_async_remote_copy(
            src_ref=src, dst_ref=dst, send_sem=ss, recv_sem=rs, device_id=dev, device_id_type=MESH
        )

    xg = (xg0, xg1, xg2, xg3)
    sent = []

    def send(src, dst, ss, rs, dev):
        copy = rc(src, dst, ss, rs, dev)
        copy.start()
        sent.append(copy)

    def got(ref, ss, rs, dev):
        rc(ref, ref, ss, rs, dev).wait_recv()

    pairs = (
        (xt_in, xt_ref), (w_in, w_ref), (cols_in, cols_ref), (counts_in, counts_ref),
        (src_in, src_ref), (dst_in, dst_ref), (ew_in, ew_ref), (cot_in, cot_ref),
    )
    loads = [pltpu.make_async_copy(src, dst, in_sem.at[i]) for i, (src, dst) in enumerate(pairs)]
    for load in loads:
        load.start()

    barrier = pltpu.get_barrier_semaphore()

    for i in (8, 7, 9, 6, 10, 5, 11, 4, 12, 3, 13, 2, 14, 1, 15):
        pl.semaphore_signal(barrier, inc=1, device_id=(r, (c + i) % 16), device_id_type=MESH)
        pl.semaphore_signal(barrier, inc=1, device_id=((r + i) % 16, c), device_id_type=MESH)
    loads[0].wait()
    for b in range(16):
        xg0[b, y] = xt_ref[:, b * 128 : (b + 1) * 128]

    spots = lax.broadcasted_iota(jnp.int32, (128, 512), 0).astype(F32).astype(BF)
    slots = lax.broadcasted_iota(jnp.int32, (8, 512), 0)

    def spread(row):
        piece = jnp.broadcast_to(row, (16, row.shape[1])).astype(BF)
        return jnp.concatenate([piece] * 8, axis=0)

    def make_block(g):
        src = src_ref[g].astype(F32)
        dst = dst_ref[g].astype(F32)
        wts = jnp.where(slots < counts_ref[0, g], ew_ref[g].astype(F32), 0.0)
        for s in range(8):
            left = jnp.where(spots == spread(dst[s : s + 1]), spread(wts[s : s + 1]), BF(0))
            right = jnp.where(spots == spread(src[s : s + 1]), BF(1), BF(0))
            tile = lax.dot_general(right, left, NT, preferred_element_type=F32)
            tiles[g, s * 128 : (s + 1) * 128] = tile.astype(BF)

    def place_block(g):
        names = [spread(jnp.full((1, 128), cols_ref[s, g].astype(F32), F32)) for s in range(8)]
        rows = pl.ds(pl.multiple_of(g * 128, 128), 128)
        for j in range(16):
            here = BF(j)
            t = [
                jnp.where(names[s] == here, tiles[g, s * 128 : (s + 1) * 128], BF(0))
                for s in range(8)
            ]
            total = ((t[0] + t[1]) + (t[2] + t[3])) + ((t[4] + t[5]) + (t[6] + t[7]))
            a[j * 128 : (j + 1) * 128, rows] = total

    def nth_block(i):
        n = i // 2
        step = (n + 1) // 2
        d = 4 + jnp.where(n % 2 == 1, -step, step)
        return (z + d) % 8 * 2 + i % 2

    def over(which, start, stop):
        def one(i, _):
            which(nth_block(i))
            return 0

        lax.fori_loop(start, stop, one, 0)

    def make(start, stop):
        over(make_block, start, stop)

    def place(start, stop):
        over(place_block, start, stop)

    pl.semaphore_wait(barrier, 30)

    def xg_at(h, o1, o2):
        ox, oy = ((o2, o1), (o1, o2))[h]
        return xg[ox % 4].at[8 * h : 8 * h + 8, (y + oy) % 4]

    def along_x(h, ring):
        return (h + ring) % 2 == 1

    def ag_send(h, ring, lane, j, o1, o2):
        step = (1, -1, 1, -1)[j] if ring == 1 else (1, -1, 2)[j]
        src = xg_at(h, o1, o2)
        if along_x(h, ring):
            dst = xg_at(h, o1 - step, o2) if ring == 0 else xg_at(h, o1, o2 - step)
            dev = at_x(step)
        else:
            dst = src
            dev = at_y(step)
        if ring == 1 and j >= 2:
            rows = slice(0, 16) if j == 2 else slice(16, 32)
            src, dst = src.at[:, rows], dst.at[:, rows]
        send(src, dst, ag_ss.at[h, lane, j], ag_rs.at[h, lane, j], dev)

    def ag_got(h, ring, lane, j):
        if ring == 0:
            step = (1, -1, 2)[j]
            piece = xg_at(h, -step, 0)
        else:
            step = (1, -1, 1, -1)[j]
            piece = xg_at(h, lane - 1, -step if j < 2 else 2)
            if j >= 2:
                piece = piece.at[:, slice(0, 16) if j == 2 else slice(16, 32)]
        dev = at_x(-step) if along_x(h, ring) else at_y(-step)
        got(piece, ag_ss.at[h, lane, j], ag_rs.at[h, lane, j], dev)

    def ag_ring2_own(h, o1):
        for j in (0, 1):
            ag_send(h, 1, 1 + o1, j, o1, 0)

    def ag_ring2_pass(h, o1):
        for j, o in ((0, 3), (1, 1)):
            ag_got(h, 1, 1 + o1, j)
            ag_send(h, 1, 1 + o1, 2 + j, o1, o)

    def ag_ring2_end(h, o1):
        for j in (2, 3):
            ag_got(h, 1, 1 + o1, j)

    for h in (0, 1):
        for j in (0, 1):
            ag_send(h, 0, 0, j, 0, 0)
    for h in (0, 1):
        ag_send(h, 0, 0, 2, 0, 0)
    for h in (0, 1):
        ag_ring2_own(h, 0)

    def cot_copy(i, peer, mine):
        return rc(
            cot_ref.at[:, pl.ds(pl.multiple_of(peer * 128, 128), 128)],
            cotb.at[pl.ds(pl.multiple_of(mine * 32, 32), 32), :],
            cot_ss.at[i], cot_rs.at[i], (r, peer),
        )

    def cot_send(i, _):
        cot_copy(i, (c + i) % 16, c).start()
        return 0

    loads[7].wait()
    lax.fori_loop(1, 16, cot_send, 0)
    cotb[pl.ds(pl.multiple_of(c * 32, 32), 32), :] = cot_ref[:, pl.ds(pl.multiple_of(c * 128, 128), 128)]

    loads[1].wait()
    eye = lax.broadcasted_iota(jnp.int32, (512, 512), 0) == lax.broadcasted_iota(jnp.int32, (512, 512), 1)
    wt[...] = lax.dot_general(
        jnp.where(eye, 1.0, 0.0).astype(BF), w_ref[...], NT, preferred_element_type=F32
    ).astype(BF)
    for load in loads[2:7]:
        load.wait()
    make(0, 4)
    for j, o in ((0, 3), (1, 1)):
        for h in (0, 1):
            ag_got(h, 0, 0, j)
            ag_ring2_own(h, o)
    for h in (0, 1):
        ag_got(h, 0, 0, 2)
        ag_ring2_own(h, 2)
    for h in (1, 0):
        ag_ring2_pass(h, 0)
    make(4, 8)
    for o1 in (3, 1):
        for h in (0, 1):
            ag_ring2_pass(h, o1)
    ag_ring2_end(1, 0)

    def block_product(offsets, g):
        picked = []
        for s in range(8):
            col = cols_ref[s, g]
            rows = [xg[o][col].reshape(128, 128) for o in offsets]
            picked.append(rows[0] if len(rows) == 1 else jnp.concatenate(rows, axis=0))
        left = jnp.concatenate(picked, axis=1)
        return jnp.dot(left, tiles[g], preferred_element_type=F32)

    def product(offsets, *ds):
        for d in ds:
            first = (z + d) % 8 * 2
            value = block_product(offsets, first + 1 - k)
            for i, o in enumerate(offsets):
                psend[o, d] = value[128 * i : 128 * i + 128]
                send(psend.at[o, d], precv.at[o, d], core_ss.at[o, d], core_rs.at[o, d], twin)
            value = block_product(offsets, first + k)
            for i, o in enumerate(offsets):
                pown[o, d] = value[128 * i : 128 * i + 128]

    def twin_got(o, d):
        got(precv.at[o, d], core_ss.at[o, d], core_rs.at[o, d], twin)

    HALVES = (slice(0, 64), slice(64, 128))

    def z_step(offsets, dist):
        for o in offsets:
            for d in (4,) if dist == 4 else (dist, 8 - dist):
                twin_got(o, d)
            for side in (0, 1):
                d = dist if side == 0 else 8 - dist
                sems = (rz_ss.at[side, dist, o], rz_rs.at[side, dist, o])
                before = (rz_ss.at[side, dist + 1, o], rz_rs.at[side, dist + 1, o]) if dist < 4 else None
                came, goes = at_z(-1 if side == 0 else 1), at_z(1 if side == 0 else -1)
                if dist == 4:
                    half = HALVES[side]
                    zs[side, 4, o, half] = (pown[o, d, half] + precv[o, d, half]).astype(BF)
                    send(zs.at[side, 4, o, half], zr.at[side, 3, o, half], *sems, goes)
                    continue
                value = pown[o, d] + precv[o, d]
                if dist == 3:
                    half, other = HALVES[side], HALVES[1 - side]
                    got(zr.at[side, 3, o, half], *before, came)
                    zs[side, 3, o, half] = (value[half] + zr[side, 3, o, half].astype(F32)).astype(BF)
                    zs[side, 3, o, other] = value[other].astype(BF)
                else:
                    got(zr.at[side, dist, o], *before, came)
                    zs[side, dist, o] = (value + zr[side, dist, o].astype(F32)).astype(BF)
                send(zs.at[side, dist, o], zr.at[side, dist - 1, o], *sems, goes)

    def z_last(offsets):
        for o in offsets:
            twin_got(o, 0)
            value = pown[o, 0] + precv[o, 0]
            for side in (0, 1):
                got(zr.at[side, 0, o], rz_ss.at[side, 1, o], rz_rs.at[side, 1, o], at_z(-1 if side == 0 else 1))
                value = value + zr[side, 0, o].astype(F32)
            start = pl.multiple_of((x + o) % 4 * 128, 128)
            high = value.astype(BF)
            low = (value - high.astype(F32)).astype(BF)
            axb[pl.ds(start, 128)] = high
            weights = wt[:, pl.ds(start, 128)]
            part = jnp.dot(
                jnp.concatenate([weights, weights], axis=1),
                jnp.concatenate([high, low], axis=0),
                preferred_element_type=F32,
            )
            hid[...] = part if o == 0 else hid[...] + part

    G0, G1, G2 = (0,), (1, 3), (2,)
    product(G0, 4, 3, 5)
    z_step(G0, 4)
    for h in (0, 1):
        ag_ring2_pass(h, 2)
    make(8, 13)
    for o1 in (3, 1):
        ag_ring2_end(1, o1)
    product(G1, 4)
    z_step(G0, 3)
    product(G1, 3, 5)
    z_step(G1, 4)
    make(13, 16)
    product(G0, 2, 6)
    for o1 in (0, 3, 1, 2):
        ag_ring2_end(0, o1)
    ag_ring2_end(1, 2)
    product(G2, 4)
    z_step(G0, 2)
    z_step(G2, 4)
    product(G1, 2, 6)
    z_step(G1, 3)
    product(G2, 3, 5)
    z_step(G2, 3)
    product(G0, 1, 7)
    z_step(G0, 1)
    product(G1, 1, 7)
    z_step(G1, 2)
    product(G2, 2, 6)
    z_step(G2, 2)
    product(G1, 0)
    z_step(G1, 1)
    product(G2, 1, 7)
    z_step(G2, 1)
    product(G0, 0)
    product(G2, 0)
    place(14, 16)
    z_last(G0 + G1)
    place(10, 14)
    z_last(G2)

    def cot_wait(i, _):
        cot_copy(i, c, (c + 16 - i) % 16).wait_recv()
        return 0

    lax.fori_loop(1, 16, cot_wait, 0)
    hidden = hid[...]
    sig = jax.nn.sigmoid(hidden)
    actb[...] = (hidden * sig).astype(BF)
    slope = cotb[...].astype(F32) * sig * (1.0 + hidden * (1.0 - sig))
    slb[...] = slope.astype(BF)
    sll[...] = (slope - slb[...].astype(F32)).astype(BF)
    ORDER = (2, 1, 3, 0)

    def gz_piece(side, dist, j):
        owner = (z - dist + 8) % 8 if side == 0 else (z + dist) % 8
        feats = pl.ds(pl.multiple_of((x + ORDER[j]) % 4 * 128, 128), 128)
        return tg.at[owner, k, feats]

    def gz_send(side, dist, j):
        piece = gz_piece(side, dist, j)
        send(piece, piece, gz_ss.at[side, dist, j], gz_rs.at[side, dist, j], at_z(1 if side == 0 else -1))

    def gz_got(side, dist, j):
        piece = gz_piece(side, dist, j)
        got(piece, gz_ss.at[side, dist - 1, j], gz_rs.at[side, dist - 1, j], at_z(-1 if side == 0 else 1))

    def gc_send(d):
        piece = tg.at[(z + d) % 8, k]
        send(piece, piece, gc_ss.at[d], gc_rs.at[d], twin)

    def gc_got(d):
        piece = tg.at[(z + d) % 8, 1 - k]
        got(piece, gc_ss.at[d], gc_rs.at[d], twin)

    for j in range(NS):
        feats = pl.ds(pl.multiple_of((x + ORDER[j]) % 4 * 128, 128), 128)
        tg[z, k, feats] = (
            jnp.dot(w_ref[feats], slb[...], preferred_element_type=F32)
            + jnp.dot(w_ref[feats], sll[...], preferred_element_type=F32)
        ).astype(BF)
        for side in (0, 1):
            gz_send(side, 0, j)
    gc_send(0)

    def act_copy(i, peer, mine):
        return rc(
            actb.at[pl.ds(pl.multiple_of(peer * 32, 32), 32), :],
            act_ref.at[:, pl.ds(pl.multiple_of(mine * 128, 128), 128)],
            act_ss.at[i], act_rs.at[i], (r, peer),
        )

    def act_send(i, _):
        act_copy(i, (c + i) % 16, c).start()
        return 0

    wp[...] = (
        lax.dot_general(axb[...], slb[...], NT, preferred_element_type=F32)
        .astype(BF)
        .reshape(16, 2, 16, 512)
    )
    send(wp.at[:, 1 - k], w0r, w0_ss.at[0], w0_rs.at[0], twin)

    def w1_copy(i, peer, mine):
        return rc(w0s.at[peer], w1r.at[mine], w1_ss.at[i], w1_rs.at[i], (peer, c))

    def w1_send(i, _):
        w1_copy(i, (r + i) % 16, r).start()
        return 0

    def w1_wait(i, _):
        w1_copy(i, r, (r + 16 - i) % 16).wait_recv()
        return 0

    def w2_copy(i, peer, mine):
        return rc(wz.at[mine], wz.at[mine], w2_ss.at[i], w2_rs.at[i], (r, peer * 2 + k))

    def w2_send(i, _):
        w2_copy(i, (z + i) % 8, z).start()
        return 0

    def w2_wait(i, _):
        w2_copy(i, z, (z + 8 - i) % 8).wait_recv()
        return 0

    def w3_copy(i, peer, mine):
        return rc(wg_ref.at[mine, k], wg_ref.at[mine, k], w3_ss.at[i], w3_rs.at[i], (peer, c))

    def w3_send(i, _):
        w3_copy(i, (r + i) % 16, r).start()
        return 0

    def w3_wait(i, _):
        w3_copy(i, r, (r + 16 - i) % 16).wait_recv()
        return 0

    def w_start_row():
        got(w0r, w0_ss.at[0], w0_rs.at[0], twin)
        w0s[...] = (wp[:, k].astype(F32) + w0r[...].astype(F32)).astype(BF)
        lax.fori_loop(1, 16, w1_send, 0)
        w1r[r] = w0s[r]

    def w_start_z():
        lax.fori_loop(1, 16, w1_wait, 0)
        total = w1r[0].astype(F32)
        for i in range(1, 16):
            total = total + w1r[i].astype(F32)
        wz[z] = total.astype(BF)
        lax.fori_loop(1, 8, w2_send, 0)

    def w_start_last():
        lax.fori_loop(1, 8, w2_wait, 0)
        total = wz[0].astype(F32)
        for i in range(1, 8):
            total = total + wz[i].astype(F32)
        wg_ref[r, k] = total.astype(BF)
        lax.fori_loop(1, 16, w3_send, 0)

    def w_finish():
        lax.fori_loop(1, 16, w3_wait, 0)
        send(wg_ref.at[:, k], wg_ref.at[:, k], w0_ss.at[1], w0_rs.at[1], twin)
        got(wg_ref.at[:, 1 - k], w0_ss.at[1], w0_rs.at[1], twin)

    def z_rows(side, dist, j):
        return dist < 4 or (j < NS // 2) == (side == 0)

    def far_piece(core, j):
        feats = pl.ds(pl.multiple_of((x + ORDER[j]) % 4 * 128, 128), 128)
        return tg.at[(z + 4) % 8, core, feats]

    def gather_step(dist):
        for j in range(NS):
            for side in (0, 1):
                if not z_rows(side, dist, j):
                    continue
                gz_got(side, dist, j)
                if dist < 4 and z_rows(side, dist + 1, j):
                    gz_send(side, dist, j)
                if dist == 4:
                    send(far_piece(k, j), far_piece(k, j), gd_ss.at[j], gd_rs.at[j], twin)
        if dist < 4:
            for d in (dist, 8 - dist):
                gc_send(d)

    def back_part(d):
        block = (z + d) % 8
        left = jnp.concatenate([tg[block, 0], tg[block, 1]], axis=1)
        rows = pl.ds(pl.multiple_of(block * 256, 256), 256)
        return lax.dot_general(left, a[:, rows], NT, preferred_element_type=F32)

    gc_got(0)
    acc[...] = back_part(0)
    gather_step(1)
    w_start_row()
    place(6, 10)
    gather_step(2)
    for d in (1, 7):
        gc_got(d)
        acc[...] += back_part(d)
    place(2, 6)
    gather_step(3)
    w_start_z()
    for d in (2, 6):
        gc_got(d)
        acc[...] += back_part(d)
    place(0, 2)
    for d in (3, 5):
        gc_got(d)
        acc[...] += back_part(d)
    gather_step(4)
    for j in range(NS):
        got(far_piece(1 - k, j), gd_ss.at[j], gd_rs.at[j], twin)

    early = len(sent)

    def q_rows(h, o1, o2):
        if h == 0:
            block = (x + o1) % 4 * 4 + (y + o2) % 4
        else:
            block = (x + o2) % 4 * 4 + (y + o1) % 4
        return block * 32

    def q(h, o1, o2, half):
        start = q_rows(h, o1, o2)
        if half is None:
            return acc[pl.ds(pl.multiple_of(start, 32), 32), h * 1024 : (h + 1) * 1024]
        return acc[pl.ds(pl.multiple_of(start + 16 * half, 16), 16), h * 1024 : (h + 1) * 1024]

    def rx_axis(h, ring):
        return (at_x, at_y)[(h + ring) % 2]

    def rx(src, dst, h, ring, lane, j, start):
        dev = rx_axis(h, ring)(1 if j % 2 == 0 else -1)
        if start:
            send(src, dst, rx_ss.at[h, lane, j], rx_rs.at[h, lane, j], dev)
        else:
            got(dst, rx_ss.at[h, lane, j], rx_rs.at[h, lane, j], dev)

    def s1_halves(h, o2):
        for j in (0, 1):
            xs1[h, o2, 0, 16 * j : 16 * j + 16] = q(h, 2, o2, j).astype(BF)
            rx(xs1.at[h, o2, 0, 16 * j : 16 * j + 16], xr1h.at[h, o2, j], h, 0, o2, j, True)

    def s1_pass(h, o2, j):
        o = (1, 3)[j]
        rx(None, xr1h.at[h, o2, j], h, 0, o2, j, False)
        xs1[h, o2, 1 + j, 16 * j : 16 * j + 16] = (q(h, o, o2, j) + xr1h[h, o2, j].astype(F32)).astype(BF)
        xs1[h, o2, 1 + j, 16 - 16 * j : 32 - 16 * j] = q(h, o, o2, 1 - j).astype(BF)
        rx(xs1.at[h, o2, 1 + j], xr1f.at[h, o2, j], h, 0, o2, 2 + j, True)

    def s1_final(h, o2):
        for j in (0, 1):
            rx(None, xr1f.at[h, o2, j], h, 0, o2, 2 + j, False)
        s1[h, o2] = q(h, 0, o2, None) + xr1f[h, o2, 0].astype(F32) + xr1f[h, o2, 1].astype(F32)

    def s2_send(h, o2):
        xs2[h, o2 - 1] = s1[h, o2].astype(BF)
        send(xs2.at[h, o2 - 1], xr2.at[h, o2 - 1], rx_ss.at[h, 4, o2], rx_rs.at[h, 4, o2], rx_axis(h, 1)(o2))

    def s2_final(h):
        value = s1[h, 0]
        for o2 in (2, 1, 3):
            got(xr2.at[h, o2 - 1], rx_ss.at[h, 4, o2], rx_rs.at[h, 4, o2], rx_axis(h, 1)(-o2))
            value = value + xr2[h, o2 - 1].astype(F32)
        fg_ref[:, h * 1024 : (h + 1) * 1024] = value.astype(BF)

    far = (z + 4) % 8
    left = jnp.concatenate([tg[far, 0], tg[far, 1]], axis=1)
    far_rows = pl.ds(pl.multiple_of(far * 256, 256), 256)
    for h in (0, 1):
        nodes = slice(h * 1024, (h + 1) * 1024)
        acc[:, nodes] += lax.dot_general(left, a[nodes, far_rows], NT, preferred_element_type=F32)
        for o2 in ORDER:
            s1_halves(h, o2)
    lax.fori_loop(1, 16, act_send, 0)
    act_ref[:, pl.ds(pl.multiple_of(c * 128, 128), 128)] = actb[pl.ds(pl.multiple_of(c * 32, 32), 32), :]
    for o2 in ORDER:
        for h in (0, 1):
            for j in (0, 1):
                s1_pass(h, o2, j)
        if o2 == 1:
            w_start_last()
    for copy in sent[:early]:
        copy.wait_send()
    for o2 in ORDER:
        for h in (0, 1):
            s1_final(h, o2)
            if o2 > 0:
                s2_send(h, o2)
    w_finish()
    wg_copy = pltpu.make_async_copy(wg_ref, wg_out, out_sem.at[0])
    wg_copy.start()

    def act_wait(i, _):
        act_copy(i, c, (c + 16 - i) % 16).wait_recv()
        return 0

    lax.fori_loop(1, 16, act_wait, 0)
    act_store = pltpu.make_async_copy(act_ref, act_out, out_sem.at[1])
    act_store.start()
    for h in (0, 1):
        s2_final(h)
    fg_store = pltpu.make_async_copy(fg_ref, fg_out, out_sem.at[2])
    fg_store.start()

    def last(i, _):
        act_copy(i, (c + i) % 16, c).wait_send()
        cot_copy(i, (c + i) % 16, c).wait_send()
        w1_copy(i, (r + i) % 16, r).wait_send()
        w3_copy(i, (r + i) % 16, r).wait_send()
        return 0

    lax.fori_loop(1, 16, last, 0)

    def last_z(i, _):
        w2_copy(i, (z + i) % 8, z).wait_send()
        return 0

    lax.fori_loop(1, 8, last_z, 0)
    for copy in sent[early:]:
        copy.wait_send()
    for store in (wg_copy, act_store, fg_store):
        store.wait()


def layer(cols, counts, src, dst, ew, xt, cot, weight):
    dma = pltpu.SemaphoreType.DMA
    vm = pltpu.VMEM
    anywhere = pl.BlockSpec(memory_space=pl.ANY)
    return pl.pallas_call(
        layer_kernel,
        out_shape=(
            jax.ShapeDtypeStruct((32, 2048), BF),
            jax.ShapeDtypeStruct((32, 2048), BF),
            jax.ShapeDtypeStruct((16, 2, 16, 512), BF),
        ),
        in_specs=[anywhere] * 8,
        out_specs=(anywhere,) * 3,
        scratch_shapes=[
            pltpu.SMEM((8, 16), jnp.int32),
            pltpu.SMEM((1, 16), jnp.int32),
            vm((16, 8, 512), jnp.int32),
            vm((16, 8, 512), jnp.int32),
            vm((16, 8, 512), BF),
            vm((32, 2048), BF),
            vm((32, 2048), BF),
            vm((512, 512), BF),
            vm((32, 2048), BF),
            vm((32, 2048), BF),
            vm((16, 2, 16, 512), BF),
            vm((2048, 2048), BF),
            vm((16, 1024, 128), BF),
            vm((16, 4, 32, 128), BF),
            vm((16, 4, 32, 128), BF),
            vm((16, 4, 32, 128), BF),
            vm((16, 4, 32, 128), BF),
            vm((512, 512), BF),
            vm((512, 128), BF),
            vm((4, 8, 128, 128), F32),
            vm((4, 8, 128, 128), F32),
            vm((4, 8, 128, 128), F32),
            vm((2, 4, 4, 128, 128), BF),
            vm((2, 5, 4, 128, 128), BF),
            vm((512, 128), F32),
            vm((512, 128), BF),
            vm((512, 128), BF),
            vm((512, 128), BF),
            vm((512, 128), BF),
            vm((8, 2, 512, 128), BF),
            vm((512, 2048), F32),
            vm((2, 4, 3, 32, 1024), BF),
            vm((2, 4, 2, 16, 1024), BF),
            vm((2, 4, 2, 32, 1024), BF),
            vm((2, 4, 32, 1024), F32),
            vm((2, 3, 32, 1024), BF),
            vm((2, 3, 32, 1024), BF),
            vm((16, 2, 16, 512), BF),
            vm((16, 16, 512), BF),
            vm((16, 16, 512), BF),
            vm((16, 16, 512), BF),
            vm((8, 16, 512), BF),
            dma((8,)),
            dma((3,)),
        ]
        + [dma((16,))] * 2
        + [dma((2, 5, 4))] * 2
        + [dma((4, 8))] * 2
        + [dma((2, 5, 4))] * 2
        + [dma((16,))] * 2
        + [dma((2, 4, NS))] * 2
        + [dma((8,))] * 2
        + [dma((NS,))] * 2
        + [dma((2, 5, 4))] * 2
        + [dma((2,))] * 2
        + [dma((16,))] * 2
        + [dma((8,))] * 2
        + [dma((16,))] * 2,
        compiler_params=pltpu.CompilerParams(
            collective_id=0, has_side_effects=True, vmem_limit_bytes=58 << 20
        ),
        name="layer",
    )(cols, counts, src, dst, ew, xt, cot, weight)


def finish_kernel(act_ref, fg_ref, wg_ref, act_out, fg_out, wg_out, act_in, fg_in, wg_in, wg_wide, sems):
    rows = [pl.ds(128 * i, 128) for i in range(4)]
    pairs = [(wg_ref.at[p], wg_in.at[p], wg_wide.at[p], wg_out.at[p]) for p in rows]
    pairs += [(act_ref, act_in, act_in, act_out), (fg_ref, fg_in, fg_in, fg_out)]
    loads = [pltpu.make_async_copy(p[0], p[1], sems.at[0, i]) for i, p in enumerate(pairs)]
    stores = [pltpu.make_async_copy(p[2], p[3], sems.at[1, i]) for i, p in enumerate(pairs)]
    for load in loads:
        load.start()
    for i in range(6):
        loads[i].wait()
        if i < 4:
            wg_wide[rows[i]] = wg_in[rows[i]].astype(F32)
        stores[i].start()
    for store in stores:
        store.wait()


def finish(act, fg, wg):
    anywhere = pl.BlockSpec(memory_space=pl.ANY)
    return pl.pallas_call(
        finish_kernel,
        out_shape=(
            jax.ShapeDtypeStruct((32, 2048), BF),
            jax.ShapeDtypeStruct((32, 2048), BF),
            jax.ShapeDtypeStruct((512, 512), F32),
        ),
        in_specs=[anywhere] * 3,
        out_specs=(anywhere,) * 3,
        scratch_shapes=[
            pltpu.VMEM((32, 2048), BF),
            pltpu.VMEM((32, 2048), BF),
            pltpu.VMEM((512, 512), BF),
            pltpu.VMEM((512, 512), F32),
            pltpu.SemaphoreType.DMA((2, 6)),
        ],
        compiler_params=pltpu.CompilerParams(vmem_limit_bytes=58 << 20),
        name="finish",
    )(act, fg, wg.reshape(512, 512))


def shards(features, weight, block_cols, block_count, edge_src, edge_dst, edge_weight, cotangent):
    outs = layer(
        block_cols[:, 0, :].T, block_count.T, edge_src[:, 0], edge_dst[:, 0], edge_weight[:, 0],
        features.T, cotangent.T, weight,
    )
    act, fg, wg = finish(*outs)
    return act.T, fg.T, wg


def solution(mesh):
    return jax.shard_map(
        shards,
        mesh=mesh,
        in_specs=(
            P("col", "row"),
            P(),
            P("row", "col", None),
            P("row", "col"),
            P("row", "col", None, None),
            P("row", "col", None, None),
            P("row", "col", None, None),
            P("row", "col"),
        ),
        out_specs=(P("row", "col"), P("col", "row"), P()),
        check_vma=False,
    )
```
